32 devices in a mesh: dp: 4 (over x, core), ha: 4 (over z), wa: 2 (over y).
Axes of the slice: x: 2, y: 2, z: 4, core: 2. Of those that a mesh axis runs over, the one named last changes fastest.
Arguments:
- images: bfloat16 [2, 256, 16, 16, 512], P(None, 'dp', 'ha', 'wa'), may hold values from -6 to 6
- labels: int32 [2, 256], P(None, 'dp'), may hold values from 0 to 999
- class_counts: int32 [1000], replicated, may hold values from 1 to 8
- owner_share: int32 [4], replicated, may hold values from 2 to 6, as said below
- w_entry: float32 [3456, 512], P('dp'), may hold values from -0.25 to 0.25
- first_entry: float32 [3456, 512], P('dp'), may hold values from -0.00030517578 to 0.00030517578
- second_entry: float32 [3456, 512], P('dp'), may hold values from 2e-10 to 8e-10
- w_in: float32 [1, 1152, 1536], P(None, 'dp'), may hold values from -0.15625 to 0.15625
- first_in: float32 [1, 1152, 1536], P(None, 'dp'), may hold values from -0.00012207031 to 0.00012207031
- second_in: float32 [1, 1152, 1536], P(None, 'dp'), may hold values from 1.3e-11 to 5.3e-11
- w_mid: float32 [2, 2, 1152, 1152], P(None, None, 'dp'), may hold values from -0.1875 to 0.1875
- first_mid: float32 [2, 2, 1152, 1152], P(None, None, 'dp'), may hold values from -0.00021362305 to 0.00021362305
- second_mid: float32 [2, 2, 1152, 1152], P(None, None, 'dp'), may hold values from 8.7e-11 to 3.5e-10
- w_out: float32 [2, 2304, 768], P(None, 'dp'), may hold values from -0.21875 to 0.21875
- first_out: float32 [2, 2304, 768], P(None, 'dp'), may hold values from -0.00015258789 to 0.00015258789
- second_out: float32 [2, 2304, 768], P(None, 'dp'), may hold values from 2.1e-11 to 8.5e-11
- se_down: float32 [2, 1152, 1536], P(None, 'dp'), may hold values from -0.15625 to 0.15625
- first_down: float32 [2, 1152, 1536], P(None, 'dp'), may hold values from -1.1444092e-05 to 1.1444092e-05
- second_down: float32 [2, 1152, 1536], P(None, 'dp'), may hold values from 1.7e-13 to 6.8e-13
- se_up: float32 [2, 2304, 768], P(None, 'dp'), may hold values from -0.21875 to 0.21875
- first_up: float32 [2, 2304, 768], P(None, 'dp'), may hold values from -4.7683716e-06 to 4.7683716e-06
- second_up: float32 [2, 2304, 768], P(None, 'dp'), may hold values from 3.5e-14 to 1.4e-13
- w_final: float32 [4608, 1536], P('dp'), may hold values from -0.15625 to 0.15625
- first_final: float32 [4608, 1536], P('dp'), may hold values from -0.00015258789 to 0.00015258789
- second_final: float32 [4608, 1536], P('dp'), may hold values from 6.5e-11 to 2.6e-10
- head: float32 [4608, 1000], P('dp'), may hold values from -0.3125 to 0.3125
- first_head: float32 [4608, 1000], P('dp'), may hold values from -6.1035156e-05 to 6.1035156e-05
- second_head: float32 [4608, 1000], P('dp'), may hold values from 1e-11 to 4e-11
- small_params: float32 [1002], replicated, may hold values from -2 to 5
- first_small: float32 [1002], replicated, may hold values from -0.0066 to 0.0066
- second_small: float32 [1002], replicated, may hold values from 4e-11 to 4e-07
Outputs:
- loss_sum: float32 [], replicated
- new_first_entry: float32 [3456, 512], P('dp')
- new_second_entry: float32 [3456, 512], P('dp')
- new_w_entry: float32 [3456, 512], P('dp')
- new_first_in: float32 [1, 1152, 1536], P(None, 'dp')
- new_second_in: float32 [1, 1152, 1536], P(None, 'dp')
- new_w_in: float32 [1, 1152, 1536], P(None, 'dp')
- new_first_mid: float32 [2, 2, 1152, 1152], P(None, None, 'dp')
- new_second_mid: float32 [2, 2, 1152, 1152], P(None, None, 'dp')
- new_w_mid: float32 [2, 2, 1152, 1152], P(None, None, 'dp')
- new_first_out: float32 [2, 2304, 768], P(None, 'dp')
- new_second_out: float32 [2, 2304, 768], P(None, 'dp')
- new_w_out: float32 [2, 2304, 768], P(None, 'dp')
- new_first_down: float32 [2, 1152, 1536], P(None, 'dp')
- new_second_down: float32 [2, 1152, 1536], P(None, 'dp')
- new_se_down: float32 [2, 1152, 1536], P(None, 'dp')
- new_first_up: float32 [2, 2304, 768], P(None, 'dp')
- new_second_up: float32 [2, 2304, 768], P(None, 'dp')
- new_se_up: float32 [2, 2304, 768], P(None, 'dp')
- new_first_final: float32 [4608, 1536], P('dp')
- new_second_final: float32 [4608, 1536], P('dp')
- new_w_final: float32 [4608, 1536], P('dp')
- new_first_head: float32 [4608, 1000], P('dp')
- new_second_head: float32 [4608, 1000], P('dp')
- new_head: float32 [4608, 1000], P('dp')
- new_first_small: float32 [1002], replicated
- new_second_small: float32 [1002], replicated
- new_small_params: float32 [1002], replicated
The draws below stay inside these ranges and needn't reach their ends.
Inputs may be any that keep to these rules, and one draw needn't show every extreme that they name: `owner_share`: entries sum to 16.
All inputs are finite; a program needn't handle non-finite values.
Results may differ from the reference program's by a relative error of at most 0.04.
Values may be sent and summed in bfloat16 or wider, within the bound.
A program may use at most 640 MiB of HBM per device.

```python
import math
import jax
import jax.numpy as jnp
from jax import lax

IN_WIDTH = 512
WIDTH = 1536
NECK = 768
GROUP = 128
SQUEEZE = 768
FINAL = 3072
CLASSES = 1000
HEIGHT = 8
BREADTH = 8
LAYERS = 2
MICRO = 2
STEP_COUNT = 5
FAN_MID = 1152
BATCH = 256
IMAGES = 512
N_DP = 4


def draw_owner_share(key, part):
    order_key, step_key = jax.random.split(jax.random.fold_in(key, 11))
    order = jax.random.permutation(order_key, N_DP)
    steps = jax.random.randint(step_key, ((N_DP - 2) // 2,), -1, 2).astype(jnp.int32)
    moves = jnp.concatenate([jnp.array([2, -2], jnp.int32), jnp.stack([steps, -steps], axis=1).reshape(-1)])
    return jnp.zeros((N_DP,), jnp.int32).at[order].set(4 + moves).astype(jnp.int32)


def draw_small_params(key, part):
    gain_key, bias_key = jax.random.split(jax.random.fold_in(key, 21))
    gains = jnp.exp(jax.random.uniform(gain_key, (LAYERS,), jnp.float32, jnp.log(2.0), jnp.log(5.0)))
    bias = 0.5 * jnp.clip(jax.random.normal(bias_key, (CLASSES,), jnp.float32), -4.0, 4.0)
    return jnp.concatenate([gains, bias])


def draw_first_small(key, part):
    values = jnp.clip(jax.random.normal(jax.random.fold_in(key, 31), (LAYERS + CLASSES,), jnp.float32), -6.0, 6.0)
    scales = jnp.concatenate([jnp.full((LAYERS,), 0.0011, jnp.float32), jnp.full((CLASSES,), 2.2e-05, jnp.float32)])
    return values * scales


def draw_second_small(key, part):
    spread = jax.random.uniform(jax.random.fold_in(key, 41), (LAYERS + CLASSES,), jnp.float32, 0.0, jnp.log(4.0))
    bases = jnp.concatenate([jnp.full((LAYERS,), 1e-07, jnp.float32), jnp.full((CLASSES,), 4e-11, jnp.float32)])
    return bases * jnp.exp(spread)


def with_ends(result, rng, least, high):
    index_at = [jax.random.randint(jax.random.fold_in(rng, axis), (), 0, length) for axis, length in enumerate(result.shape)]
    main_axis = result.shape.index(max(result.shape))
    next_to = index_at[:main_axis] + [(index_at[main_axis] + 1) % result.shape[main_axis]] + index_at[main_axis + 1:]
    return result.at[tuple(index_at)].set(least).at[tuple(next_to)].set(high)


def block_levels(rng, shape, cuts, least, top_value):
    factor_of, own = 1.0, jax.random.fold_in(rng, 6)
    for axis_at, parts in cuts:
        steps = jnp.exp(jax.random.uniform(jax.random.fold_in(own, axis_at), (parts,), jnp.float32, least / len(cuts), top_value / len(cuts)))
        factor_of = factor_of * jnp.repeat(steps, shape[axis_at] // parts).reshape([-1 if axis == axis_at else 1 for axis in range(len(shape))])
    return factor_of


def scatter_about(own_key, shape, width, limit, shards=(), held_as=jnp.bfloat16):
    entries = width * jax.random.normal(own_key, shape, jnp.float32)
    if shards:
        entries = entries * block_levels(own_key, shape, shards, -0.22, 0.18)
    return jnp.clip(entries, -limit, limit).astype(held_as)


def setup_inputs(seed: int = 0) -> dict:
    seeds = jax.random.split(jax.random.key(seed), 32)
    return {
        "images": scatter_about(seeds[0], (MICRO, BATCH, 2 * HEIGHT, 2 * BREADTH, IN_WIDTH), 1.0, 6.0, ((1, 4), (2, 4), (3, 2))),
        "labels": with_ends(jax.random.randint(seeds[1], (MICRO, BATCH), 0, CLASSES), jax.random.fold_in(seeds[1], 1), 0, CLASSES - 1).astype(jnp.int32),
        "class_counts": with_ends(jax.random.randint(seeds[2], (CLASSES,), 1, 9), jax.random.fold_in(seeds[2], 1), 1, 8).astype(jnp.int32),
        "owner_share": draw_owner_share(jax.random.fold_in(seeds[31], 71), 0),
        "w_entry": scatter_about(seeds[4], (3 * (NECK + WIDTH) // 2, IN_WIDTH), IN_WIDTH ** -0.5, 0.25, ((0, 4),), jnp.float32),
        "first_entry": scatter_about(seeds[5], (3 * (NECK + WIDTH) // 2, IN_WIDTH), 0.000049, 0.00030517578, ((0, 4),), jnp.float32),
        "second_entry": jnp.clip(jnp.exp(math.log(8.000000106811456e-10) - 1.3862944 * jax.random.uniform(seeds[6], (3 * (NECK + WIDTH) // 2, IN_WIDTH), jnp.float32) ** block_levels(seeds[6], (3 * (NECK + WIDTH) // 2, IN_WIDTH), ((0, 4),), -0.2, 0.2)), 2.000000026702864e-10, 8.000000106811456e-10),
        "w_in": scatter_about(seeds[7], (LAYERS - 1, 3 * NECK // 2, WIDTH), WIDTH ** -0.5, 0.15625, ((1, 4),), jnp.float32),
        "first_in": scatter_about(seeds[8], (LAYERS - 1, 3 * NECK // 2, WIDTH), 0.000019, 0.00012207031, ((1, 4),), jnp.float32),
        "second_in": jnp.clip(jnp.exp(math.log(5.300000022190332e-11) - 1.40534253 * jax.random.uniform(seeds[9], (LAYERS - 1, 3 * NECK // 2, WIDTH), jnp.float32) ** block_levels(seeds[9], (LAYERS - 1, 3 * NECK // 2, WIDTH), ((1, 4),), -0.2, 0.2)), 1.3000000381735433e-11, 5.300000022190332e-11),
        "w_mid": scatter_about(seeds[10], (LAYERS, 2, 3 * NECK // 2, FAN_MID), FAN_MID ** -0.5, 0.1875, ((2, 4),), jnp.float32),
        "first_mid": scatter_about(seeds[11], (LAYERS, 2, 3 * NECK // 2, FAN_MID), 0.000033, 0.00021362305, ((2, 4),), jnp.float32),
        "second_mid": jnp.clip(jnp.exp(math.log(3.5000000120355423e-10) - 1.3920251 * jax.random.uniform(seeds[12], (LAYERS, 2, 3 * NECK // 2, FAN_MID), jnp.float32) ** block_levels(seeds[12], (LAYERS, 2, 3 * NECK // 2, FAN_MID), ((2, 4),), -0.2, 0.2)), 8.699999748396081e-11, 3.5000000120355423e-10),
        "w_out": scatter_about(seeds[13], (LAYERS, 3 * WIDTH // 2, NECK), NECK ** -0.5, 0.21875, ((1, 4),), jnp.float32),
        "first_out": scatter_about(seeds[14], (LAYERS, 3 * WIDTH // 2, NECK), 0.000024, 0.00015258789, ((1, 4),), jnp.float32),
        "second_out": jnp.clip(jnp.exp(math.log(8.500000009403763e-11) - 1.3981288 * jax.random.uniform(seeds[15], (LAYERS, 3 * WIDTH // 2, NECK), jnp.float32) ** block_levels(seeds[15], (LAYERS, 3 * WIDTH // 2, NECK), ((1, 4),), -0.2, 0.2)), 2.100000034976901e-11, 8.500000009403763e-11),
        "se_down": scatter_about(seeds[16], (LAYERS, 3 * SQUEEZE // 2, WIDTH), WIDTH ** -0.5, 0.15625, ((1, 4),), jnp.float32),
        "first_down": scatter_about(seeds[17], (LAYERS, 3 * SQUEEZE // 2, WIDTH), 0.0000018, 1.1444091796875e-05, ((1, 4),), jnp.float32),
        "second_down": jnp.clip(jnp.exp(math.log(6.800000016196628e-13) - 1.3862944 * jax.random.uniform(seeds[18], (LAYERS, 3 * SQUEEZE // 2, WIDTH), jnp.float32) ** block_levels(seeds[18], (LAYERS, 3 * SQUEEZE // 2, WIDTH), ((1, 4),), -0.2, 0.2)), 1.700000004049157e-13, 6.800000016196628e-13),
        "se_up": scatter_about(seeds[19], (LAYERS, 3 * WIDTH // 2, SQUEEZE), SQUEEZE ** -0.5, 0.21875, ((1, 4),), jnp.float32),
        "first_up": scatter_about(seeds[20], (LAYERS, 3 * WIDTH // 2, SQUEEZE), 0.0000008, 4.76837158203125e-06, ((1, 4),), jnp.float32),
        "second_up": jnp.clip(jnp.exp(math.log(1.4000000431949738e-13) - 1.3862944 * jax.random.uniform(seeds[21], (LAYERS, 3 * WIDTH // 2, SQUEEZE), jnp.float32) ** block_levels(seeds[21], (LAYERS, 3 * WIDTH // 2, SQUEEZE), ((1, 4),), -0.2, 0.2)), 3.5000001079874346e-14, 1.4000000431949738e-13),
        "w_final": scatter_about(seeds[22], (3 * FINAL // 2, WIDTH), WIDTH ** -0.5, 0.15625, ((0, 4),), jnp.float32),
        "first_final": scatter_about(seeds[23], (3 * FINAL // 2, WIDTH), 0.000028, 0.00015258789, ((0, 4),), jnp.float32),
        "second_final": jnp.clip(jnp.exp(math.log(2.5999999375692084e-10) - 1.3862944 * jax.random.uniform(seeds[24], (3 * FINAL // 2, WIDTH), jnp.float32) ** block_levels(seeds[24], (3 * FINAL // 2, WIDTH), ((0, 4),), -0.2, 0.2)), 6.499999843923021e-11, 2.5999999375692084e-10),
        "head": scatter_about(seeds[25], (3 * FINAL // 2, CLASSES), (FINAL // 9) ** -0.5, 0.3125, ((0, 4),), jnp.float32),
        "first_head": scatter_about(seeds[26], (3 * FINAL // 2, CLASSES), 0.000011, 6.103515625e-05, ((0, 4),), jnp.float32),
        "second_head": jnp.clip(jnp.exp(math.log(3.999999984016789e-11) - 1.3862944 * jax.random.uniform(seeds[27], (3 * FINAL // 2, CLASSES), jnp.float32) ** block_levels(seeds[27], (3 * FINAL // 2, CLASSES), ((0, 4),), -0.2, 0.2)), 9.999999960041972e-12, 3.999999984016789e-11),
        "small_params": draw_small_params(jax.random.fold_in(seeds[31], 71), 0),
        "first_small": draw_first_small(jax.random.fold_in(seeds[31], 71), 0),
        "second_small": draw_second_small(jax.random.fold_in(seeds[31], 71), 0),
    }


GAMMA = 1.7015043497085571
ALPHA = 0.2
CLIP = 0.01
RATE = 0.05
SMALL_RATE = 0.5
DECAY_ONE = 0.9
DECAY_TWO = 0.999
ADAM_EPS = 1e-08
WEIGHT_DECAY = 5e-05
STD_EPS = 0.0001
HIGH = lax.Precision.HIGHEST
ROW_DIMS = (0, 1, 2, 1, 1, 1, 0, 0)

@jax.custom_vjp
def low(v):
    return lax.optimization_barrier(v.astype(jnp.bfloat16)).astype(jnp.float32)

@jax.custom_vjp
def low_back(v):
    return v

def low_keep(v):
    return (low(v), None)

def low_pass(kept, grad):
    return (grad,)

def back_keep(v):
    return (v, None)

def back_low(kept, grad):
    return (low(grad),)
low.defvjp(low_keep, low_pass)
low_back.defvjp(back_keep, back_low)

def gelu_act(values):
    return jax.nn.gelu(values, approximate=True)

def standardize(weight):
    fan_in = weight.shape[-1]
    centre = weight - lax.optimization_barrier(jnp.mean(weight, axis=-1, keepdims=True))
    spread = lax.optimization_barrier(jnp.mean(centre * centre, axis=-1, keepdims=True))
    return centre * lax.rsqrt(spread * fan_in + STD_EPS)

def owner_rows(shares, rows):
    part = rows // (4 * N_DP)
    ends = jnp.cumsum(shares).astype(jnp.int32)
    starts = (ends - shares).astype(jnp.int32)
    part_ids = jnp.arange(4 * N_DP, dtype=jnp.int32)
    owner = lax.optimization_barrier(jnp.sum((part_ids[:, None] >= ends[None, :]).astype(jnp.int32), axis=1)).astype(jnp.int32)
    chosen = owner[:, None] == jnp.arange(N_DP, dtype=jnp.int32)[None, :]
    first_part = lax.optimization_barrier(jnp.sum(jnp.where(chosen, starts[None, :], 0), axis=1)).astype(jnp.int32)
    slot = (owner * 6 + part_ids - first_part).astype(jnp.int32)
    row_ids = jnp.arange(rows, dtype=jnp.int32)
    return (jnp.take(slot, row_ids // part) * part + row_ids % part).astype(jnp.int32)

def unpack(padded, shares, axis):
    rows = padded.shape[axis] * 2 // 3
    return jnp.take(padded, owner_rows(shares, rows), axis=axis)

def linear(inputs, weight):
    return jnp.einsum('...c,oc->...o', inputs, weight, precision=HIGH)

def conv_group(inputs, weight, stride):
    amount, size_h, size_w, channels = inputs.shape
    groups = channels // GROUP
    if stride == 1:
        padded = jnp.pad(inputs, ((0, 0), (1, 1), (1, 1), (0, 0)))
    else:
        padded = jnp.pad(inputs, ((0, 0), (0, 1), (0, 1), (0, 0)))
    out_h = size_h // stride
    out_w = size_w // stride
    kernel = weight.reshape(groups, GROUP, 9, GROUP)
    summed = jnp.zeros((amount, out_h, out_w, groups, GROUP), jnp.float32)
    for offset in range(9):
        shift_y = offset // 3
        shift_x = offset % 3
        window = padded[:, shift_y:shift_y + stride * (out_h - 1) + 1:stride, shift_x:shift_x + stride * (out_w - 1) + 1:stride]
        window = window.reshape(amount, out_h, out_w, groups, GROUP)
        summed = summed + jnp.einsum('nhwgc,goc->nhwgo', window, kernel[:, :, offset, :], precision=HIGH)
    return summed.reshape(amount, out_h, out_w, channels)

def bottleneck(hidden, layer_i, in_low, skip_low, mid_low, out_low, down_low, up_low, gain):
    pre_scale = (1.0 + layer_i * ALPHA * ALPHA) ** (-0.5)
    stride = 2 if layer_i == 0 else 1
    act_zero = low(gelu_act(hidden) * (GAMMA * pre_scale))
    pre_one = low_back(linear(act_zero, in_low))
    act_one = low(gelu_act(pre_one) * GAMMA)
    pre_two = low_back(conv_group(act_one, mid_low[0], stride))
    act_two = low(gelu_act(pre_two) * GAMMA)
    pre_three = low_back(conv_group(act_two, mid_low[1], 1))
    act_three = low(gelu_act(pre_three) * GAMMA)
    pre_four = low_back(linear(act_three, out_low))
    squeezed = low(lax.optimization_barrier(jnp.mean(pre_four, axis=(1, 2))))
    pre_down = low_back(linear(squeezed, down_low))
    act_down = low(gelu_act(pre_down))
    pre_up = low_back(linear(act_down, up_low))
    gate_value = 2.0 * jax.nn.sigmoid(pre_up)
    branch = ALPHA * gain * pre_four * gate_value[:, None, None, :]
    if layer_i == 0:
        amount, size_h, size_w, channels = act_zero.shape
        pooled = low(lax.optimization_barrier(jnp.mean(act_zero.reshape(amount, size_h // 2, 2, size_w // 2, 2, channels), axis=(2, 4))))
        return low_back(linear(pooled, skip_low)) + branch
    return hidden + branch

def micro_loss_fn(params_low, small, hidden, labels_mb, class_weight):
    entry_low, in_low, mid_low, out_low, down_low, up_low, final_low, head_low = params_low
    for layer_i in range(LAYERS):
        if layer_i == 0:
            in_now = entry_low[:NECK]
            skip_now = entry_low[NECK:]
        else:
            in_now = in_low[layer_i - 1]
            skip_now = None
        hidden = bottleneck(hidden, layer_i, in_now, skip_now, mid_low[layer_i], out_low[layer_i], down_low[layer_i], up_low[layer_i], small[layer_i])
    pre_final = low_back(linear(low(hidden), final_low))
    pooled = low(lax.optimization_barrier(jnp.mean(gelu_act(pre_final) * GAMMA, axis=(1, 2))))
    logits = low_back(jnp.einsum('nc,co->no', pooled, head_low, precision=HIGH)) + small[LAYERS:]
    log_probs = jax.nn.log_softmax(logits, axis=-1)
    picked = jnp.take_along_axis(log_probs, labels_mb[:, None], axis=1)[:, 0]
    image_weight = jnp.take(class_weight, labels_mb)
    return -jnp.sum(image_weight * picked)

def objective(params, images_float, labels, class_weight, shares):
    full = [unpack(params[member], shares, ROW_DIMS[member]) for member in range(8)]
    standard = (True, True, True, True, False, False, True, False)
    params_low = tuple((low(standardize(full[member]) if standard[member] else full[member]) for member in range(8)))
    checked = jax.checkpoint(micro_loss_fn)
    loss_sum = jnp.zeros((), jnp.float32)
    for micro_i in range(MICRO):
        loss_sum = loss_sum + checked(params_low, params[8], images_float[micro_i], labels[micro_i], class_weight)
    return (loss_sum / IMAGES, loss_sum)

def clip_unit(gradient, weight):
    weight_norm = jnp.sqrt(lax.optimization_barrier(jnp.sum(weight * weight, axis=-1, keepdims=True)))
    grad_norm = jnp.sqrt(lax.optimization_barrier(jnp.sum(gradient * gradient, axis=-1, keepdims=True)))
    ceiling = CLIP * weight_norm
    return gradient * (ceiling / jnp.maximum(grad_norm, ceiling))

def adam_step(weight, gradient, moment_one, moment_two, rate):
    first_new = DECAY_ONE * moment_one + (1.0 - DECAY_ONE) * gradient
    second_new = DECAY_TWO * moment_two + (1.0 - DECAY_TWO) * gradient * gradient
    first_hat = first_new / (1.0 - DECAY_ONE ** STEP_COUNT)
    second_hat = second_new / (1.0 - DECAY_TWO ** STEP_COUNT)
    weight_new = weight - rate * (first_hat / (jnp.sqrt(second_hat) + ADAM_EPS) + WEIGHT_DECAY * weight)
    return (first_new, second_new, weight_new)

def reference(images, labels, class_counts, owner_share, w_entry, first_entry, second_entry, w_in, first_in, second_in, w_mid, first_mid, second_mid, w_out, first_out, second_out, se_down, first_down, second_down, se_up, first_up, second_up, w_final, first_final, second_final, head, first_head, second_head, small_params, first_small, second_small):
    params = (w_entry, w_in, w_mid, w_out, se_down, se_up, w_final, head, small_params)
    firsts = (first_entry, first_in, first_mid, first_out, first_down, first_up, first_final, first_head, first_small)
    seconds = (second_entry, second_in, second_mid, second_out, second_down, second_up, second_final, second_head, second_small)
    class_weight = 1.0 / class_counts.astype(jnp.float32)
    images_float = images.astype(jnp.float32)

    def wrapped(params_now):
        return objective(params_now, images_float, labels, class_weight, owner_share)
    mean_loss, pull_back, loss_sum = jax.vjp(wrapped, params, has_aux=True)
    gradients = pull_back(jnp.ones((), jnp.float32))[0]
    results = [loss_sum]
    for member in range(9):
        gradient = gradients[member]
        if member < 7:
            gradient = clip_unit(gradient, params[member])
        rate = SMALL_RATE if member == 8 else RATE
        results.extend(adam_step(params[member], gradient, firsts[member], seconds[member], rate))
    return (results[0], results[1], results[2], results[3], results[4], results[5], results[6], results[7], results[8], results[9], results[10], results[11], results[12], results[13], results[14], results[15], results[16], results[17], results[18], results[19], results[20], results[21], results[22], results[23], results[24], results[25], results[26], results[27])
```

```python
import functools

import jax
import jax.numpy as jnp
from jax import lax
from jax.experimental import pallas as pl
from jax.experimental.pallas import tpu as pltpu
from jax.sharding import PartitionSpec as P

NECK = 768
GROUP = 128
HEIGHT = 8
BREADTH = 8
CELLS = HEIGHT * BREADTH
LAYERS = 2
STEP_COUNT = 5

GAMMA = 1.7015043497085571
ALPHA = 0.2
CLIP = 0.01
RATE = 0.05
SMALL_RATE = 0.5
DECAY_ONE = 0.9
DECAY_TWO = 0.999
ADAM_EPS = 1e-08
WEIGHT_DECAY = 5e-05
STD_EPS = 0.0001
GELU_SCALE = 0.7978845608028654
GELU_CUBE = 0.044715
EVERY = ("dp", "ha", "wa")
MIB = 1 << 20

TAPS_ONE = tuple((0, t // 3 - 1, t % 3 - 1) for t in range(9))
TAPS_TWO = tuple(((t // 3 % 2) * 2 + t % 3 % 2, t // 3 // 2, t % 3 // 2) for t in range(9))

f32 = jnp.float32
bf16 = jnp.bfloat16


def gelu_act(v):
    return 0.5 * v * (1.0 + jnp.tanh(GELU_SCALE * (v + GELU_CUBE * v * v * v)))


def gelu_prime(v):
    th = jnp.tanh(GELU_SCALE * (v + GELU_CUBE * v * v * v))
    return 0.5 * (1.0 + th) + (0.5 * GELU_SCALE) * v * (1.0 - th * th) * (
        1.0 + 3.0 * GELU_CUBE * v * v
    )


def standardize(weight):
    fan_in = weight.shape[-1]
    centre = weight - jnp.mean(weight, axis=-1, keepdims=True)
    spread = jnp.mean(centre * centre, axis=-1, keepdims=True)
    return centre * lax.rsqrt(spread * fan_in + STD_EPS)


def owner_tables(shares):
    devices = shares.shape[0]
    ids = jnp.arange(devices, dtype=jnp.int32)
    starts = jnp.sum(jnp.where(ids[None, :] < ids[:, None], shares[None, :], 0), axis=1)
    part_ids = jnp.arange(4 * devices, dtype=jnp.int32)
    owner = jnp.sum((part_ids[:, None] >= (starts + shares)[None, :]).astype(jnp.int32), axis=1)
    first = jnp.sum(jnp.where(owner[:, None] == ids[None, :], starts[None, :], 0), axis=1)
    local = (part_ids - first).astype(jnp.int32)
    held = jnp.minimum(jnp.arange(6, dtype=jnp.int32)[None, :], shares[:, None] - 1)
    return owner, local, starts, (starts[:, None] + held).reshape(-1).astype(jnp.int32)


def known_mesh():
    return tuple(lax.axis_size(a) for a in EVERY) == (4, 4, 2)


def unit_slots(owner, local, part):
    return ((owner * 6 + local)[:, None] * part + jnp.arange(part)[None, :]).reshape(-1)


def gather_plain(entries, owner, local):
    full = []
    for array, lead, standard in entries:
        block = standardize(array[lead]) if standard else array[lead]
        every = lax.all_gather(block.astype(bf16), "dp", axis=0, tiled=True)
        full.append(jnp.take(every, unit_slots(owner, local, block.shape[0] // 6), axis=0))
    return full


def sum_plain(gradient, slot_part):
    part = gradient.shape[0] // (4 * lax.axis_size("dp"))
    units = (slot_part[:, None] * part + jnp.arange(part)[None, :]).reshape(-1)
    slots = jnp.take(gradient, units, axis=0)
    owned = lax.psum_scatter(slots, "dp", scatter_dimension=0, tiled=True)
    return lax.psum(owned, ("ha", "wa"))


def leads(shape):
    tuples = [()]
    for size in shape[:-2]:
        tuples = [t + (i,) for t in tuples for i in range(size)]
    return tuples


def packed_rows(part, width):
    return part * (-(-width // 128))


def pack_into(ref, at, block):
    part, width = block.shape
    for column in range(0, width, 128):
        lanes = min(128, width - column)
        piece = block[:, column : column + lanes]
        if lanes < 128:
            piece = jnp.concatenate([piece, jnp.zeros((part, 128 - lanes), piece.dtype)], axis=1)
        ref[at : at + part, :] = piece
        at += part
    return at


def read_packed(ref, at, part, width):
    pieces = []
    for column in range(0, width, 128):
        pieces.append(ref[at : at + part, : min(128, width - column)])
        at += part
    return (pieces[0] if len(pieces) == 1 else jnp.concatenate(pieces, axis=1)), at


def pack_weights_kernel(standard, *refs):
    out_ref = refs[-1]
    at = 0
    for ref, flag in zip(refs[:-1], standard):
        block = ref[...]
        at = pack_into(out_ref, at, (standardize(block) if flag else block).astype(bf16))


def pack_weights(entries):
    specs, rows = [], 0
    for array, lead, _ in entries:
        part, width = array.shape[-2] // 6, array.shape[-1]
        specs.append(
            pl.BlockSpec((None,) * len(lead) + (part, width), lambda j, lead=lead: lead + (j, 0))
        )
        rows += packed_rows(part, width)
    return pl.pallas_call(
        functools.partial(pack_weights_kernel, tuple(e[2] for e in entries)),
        grid=(6,),
        out_shape=jax.ShapeDtypeStruct((6, rows, 128), bf16),
        in_specs=specs,
        out_specs=pl.BlockSpec((None, rows, 128), lambda j: (j, 0, 0)),
        compiler_params=pltpu.CompilerParams(vmem_limit_bytes=40 * MIB),
        cost_estimate=pl.CostEstimate(
            flops=6 * rows * 128 * 8, bytes_accessed=6 * rows * 128 * 6, transcendentals=0
        ),
        name="pack_weights",
    )(*[e[0] for e in entries])


def unpack_kernel(counts, shapes, which_ref, *refs):
    sources = refs[counts : counts + counts]
    outs = refs[2 * counts :]
    for s, source in enumerate(sources):

        @pl.when(which_ref[pl.program_id(0)] == s)
        def _(source=source):
            at = 0
            for out, (part, width) in zip(outs, shapes):
                block, at = read_packed(source, at, part, width)
                out[...] = block


def unpack_weights(sources, which, places, shapes):
    count, parts = len(sources), which.shape[0]
    rows = sources[0].shape[1]
    grid_spec = pltpu.PrefetchScalarGridSpec(
        num_scalar_prefetch=1 + count,
        grid=(parts,),
        in_specs=[
            pl.BlockSpec((None, rows, 128), lambda i, *tables, s=s: (tables[1 + s][i], 0, 0))
            for s in range(count)
        ],
        out_specs=[pl.BlockSpec((p, w), lambda i, *tables: (i, 0)) for p, w in shapes],
    )
    return pl.pallas_call(
        functools.partial(unpack_kernel, count, shapes),
        grid_spec=grid_spec,
        out_shape=[jax.ShapeDtypeStruct((parts * p, w), bf16) for p, w in shapes],
        compiler_params=pltpu.CompilerParams(vmem_limit_bytes=40 * MIB),
        cost_estimate=pl.CostEstimate(
            flops=0, bytes_accessed=parts * rows * 128 * 4, transcendentals=0
        ),
        name="unpack_weights",
    )(which, *places, *sources)


def gather_packed(packed, halves, owner, local):
    me = lax.axis_index("dp")
    chip = [(i, i ^ 2) for i in range(4)]
    core = [(i, i ^ 1) for i in range(4)]
    buffers = [packed]
    if halves:
        side = lax.axis_index("wa")
        mine = lax.dynamic_slice_in_dim(packed, side * 3, 3, 0)
        near = lax.ppermute(mine, "dp", chip)
        far = lax.ppermute(near, "wa", [(0, 1), (1, 0)])
        buffers += [near, far]
    else:
        buffers += [lax.ppermute(packed, "dp", chip)]
    buffers += [lax.ppermute(b, "dp", core) for b in buffers]
    half = len(buffers) // 2
    apart = (owner // 2 != me // 2).astype(jnp.int32)
    if halves:
        which = jnp.where(apart == 1, jnp.where(local // 3 == side, 1, 2), 0)
        at = jnp.where(apart == 1, local % 3, local)
    else:
        which, at = apart, local
    which = (which + half * (owner % 2 != me % 2)).astype(jnp.int32)
    places = []
    parts = jnp.arange(owner.shape[0])
    for s in range(len(buffers)):
        found = jnp.where((which[None, :] == s) & (parts[None, :] <= parts[:, None]), at[None, :], 0)
        places.append(jnp.max(found, axis=1).astype(jnp.int32))
    return buffers, which, places


def pack_gradients_kernel(pad, part_ref, *refs):
    out_ref = refs[-1]
    at = 0
    for ref in refs[:-1]:
        at = pack_into(out_ref, at, ref[...].astype(bf16))
    if pad:
        out_ref[at : at + pad, :] = jnp.zeros((pad, 128), bf16)


def pack_gradients(gradients, slot_part, devices, unit):
    specs, rows = [], 0
    for gradient in gradients:
        part, width = gradient.shape[0] // (4 * devices), gradient.shape[1]
        specs.append(pl.BlockSpec((part, width), lambda s, parts: (parts[s], 0)))
        rows += packed_rows(part, width)
    pad = -rows % unit
    rows += pad
    slots = 6 * devices
    return pl.pallas_call(
        functools.partial(pack_gradients_kernel, pad),
        grid_spec=pltpu.PrefetchScalarGridSpec(
            num_scalar_prefetch=1,
            grid=(slots,),
            in_specs=specs,
            out_specs=pl.BlockSpec((None, rows, 128), lambda s, parts: (s, 0, 0)),
        ),
        out_shape=jax.ShapeDtypeStruct((slots, rows, 128), bf16),
        compiler_params=pltpu.CompilerParams(vmem_limit_bytes=40 * MIB),
        cost_estimate=pl.CostEstimate(
            flops=0, bytes_accessed=slots * rows * 128 * 4, transcendentals=0
        ),
        name="pack_gradients",
    )(slot_part, *gradients)


SPAN = 1280
AXES = ("x", "y", "near", "far")


def sum_kernel(orders, spans, packed, owned, own, core, one, two, three, four, sends, recvs, local_sems):
    dp, z, y = lax.axis_index("dp"), lax.axis_index("ha"), lax.axis_index("wa")
    bit = {"x": dp // 2, "core": dp % 2, "y": y, "near": z % 2, "far": z // 2}
    peer = {
        "x": {"dp": (dp + 2) % 4},
        "core": {"dp": dp + 1 - 2 * (dp % 2)},
        "y": {"wa": 1 - y},
        "near": {"ha": z + 1 - 2 * (z % 2)},
        "far": {"ha": (z + 2) % 4},
    }
    barrier = pltpu.get_barrier_semaphore()
    for other in peer.values():
        pl.semaphore_signal(barrier, inc=1, device_id=other, device_id_type=pl.DeviceIdType.MESH)
    pl.semaphore_wait(barrier, len(peer))

    buffers = [core, one, two, three, four]
    kinds = len(orders)

    def index(ref, chunk, names, fixed):
        return ref.at[(chunk,) + tuple(fixed[n] if n in fixed else slice(None) for n in names)]

    def remote(src, dst, stage, chunk, to):
        return pltpu.make_async_remote_copy(
            src_ref=src,
            dst_ref=dst,
            send_sem=sends.at[stage, chunk],
            recv_sem=recvs.at[stage, chunk],
            device_id=peer[to],
            device_id_type=pl.DeviceIdType.MESH,
        )

    def copy_of(stage, kind, chunk):
        order = orders[kind]
        if stage == 0:
            return remote(packed.at[:, 1 - bit["core"], chunk], core.at[chunk], 0, chunk, "core")
        if stage <= 4:
            before = [n for n in AXES if n not in order[: stage - 1]]
            axis = order[stage - 1]
            src = index(buffers[stage - 1], chunk, before, {axis: 1 - bit[axis]})
            return remote(src, buffers[stage].at[chunk], stage, chunk, axis)
        spread = [n for n in reversed(order) if n != "x"]
        axis = spread[stage - 5]
        fixed = {n: bit[n] for n in spread[stage - 5 :]}
        place = index(owned, chunk, AXES[1:], fixed)
        return remote(four.at[chunk] if stage == 5 else place, place, stage, chunk, axis)

    def load(chunk):
        slot = chunk % 2
        return pltpu.make_async_copy(
            packed.at[:, bit["core"], chunk], own.at[slot], local_sems.at[slot]
        )

    def store(chunk):
        place = owned.at[chunk, bit["y"], bit["near"], bit["far"]]
        return pltpu.make_async_copy(four.at[chunk], place, local_sems.at[2 + chunk])

    def add(target, names, other, prefix=()):
        for at in names:
            there = target[at].astype(f32) + other(at).astype(f32)
            target[at] = there.astype(bf16)

    def grid(count):
        return leads((2,) * count + (1, 1))

    def arrive(stage, kind, chunk):
        copy_of(stage, kind, chunk).wait_recv()
        order = orders[kind]
        if stage == 0:
            load(chunk).wait()
            add(core, [(chunk,) + t for t in grid(4)], lambda at: own[(chunk % 2,) + at[1:]])
        elif stage <= 4:
            before = [n for n in AXES if n not in order[: stage - 1]]
            axis = order[stage - 1]
            where = before.index(axis)

            def mine(at):
                rest = at[1:]
                return buffers[stage - 1][(chunk,) + rest[:where] + (bit[axis],) + rest[where:]]

            add(buffers[stage], [(chunk,) + t for t in grid(4 - stage)], mine)
            if stage == 4:
                store(chunk).start()
        if stage == 5:
            store(chunk).wait()

    ahead, last = 3, 7
    for chunk in range(ahead):
        copy_of(0, chunk % kinds, chunk).start()
    load(0).start()

    def step(s, q, first=False):
        @pl.when(s + ahead < spans)
        def _():
            copy_of(0, (q + ahead) % kinds, s + ahead).start()

        @pl.when(s + 1 < spans)
        def _():
            load(s + 1).start()

        for stage in range(last + 1):
            chunk = s - stage
            kind = (q - stage) % kinds

            @pl.when((chunk >= 0) & (chunk < spans))
            def _(stage=stage, chunk=chunk, kind=kind):
                arrive(stage, kind, chunk)
                if stage < last:
                    copy_of(stage + 1, kind, chunk).start()

    def steps(i, carry):
        for q in range(kinds):
            step(i * kinds + q, q)
        return carry

    lax.fori_loop(0, -(-(spans + last) // kinds), steps, 0)

    def sent(i, carry):
        for q in range(kinds):
            for stage in range(last + 1):
                copy_of(stage, q, i * kinds + q).wait_send()
        return carry

    lax.fori_loop(0, spans // kinds, sent, 0)


def sum_at_owners(packed):
    slots, rows, lanes = packed.shape
    spans = 6 * rows // SPAN
    r = SPAN // 8
    orders = (AXES,)
    owned = pl.pallas_call(
        functools.partial(sum_kernel, orders, spans),
        out_shape=jax.ShapeDtypeStruct((spans, 2, 2, 2, r, 128), bf16),
        in_specs=[pl.BlockSpec(memory_space=pl.ANY)],
        out_specs=pl.BlockSpec(memory_space=pl.ANY),
        scratch_shapes=[
            pltpu.VMEM((2, 2, 2, 2, 2, r, 128), bf16),
            pltpu.VMEM((spans, 2, 2, 2, 2, r, 128), bf16),
            pltpu.VMEM((spans, 2, 2, 2, r, 128), bf16),
            pltpu.VMEM((spans, 2, 2, r, 128), bf16),
            pltpu.VMEM((spans, 2, r, 128), bf16),
            pltpu.VMEM((spans, r, 128), bf16),
            pltpu.SemaphoreType.DMA((8, spans)),
            pltpu.SemaphoreType.DMA((8, spans)),
            pltpu.SemaphoreType.DMA((2 + spans,)),
        ],
        compiler_params=pltpu.CompilerParams(
            collective_id=1, has_side_effects=True, vmem_limit_bytes=56 * MIB
        ),
        cost_estimate=pl.CostEstimate(
            flops=slots * rows * 128, bytes_accessed=slots * rows * 128 * 4, transcendentals=0
        ),
        name="sum_at_owners",
    )(packed.reshape(2, 2, spans, 2, 2, 2, r, 128))
    return owned.reshape(6, rows, lanes)


def moved(image, down, right):
    if right:
        column = lax.broadcasted_iota(jnp.int32, image.shape, 1) + right
        image = pltpu.roll(image, (-right) % BREADTH, 1)
        image = jnp.where((column >= 0) & (column < BREADTH), image, 0.0)
    if down:
        edge = jnp.zeros((abs(down),) + image.shape[1:], image.dtype)
        if down > 0:
            image = jnp.concatenate([image[down:], edge], axis=0)
        else:
            image = jnp.concatenate([edge, image[:down]], axis=0)
    return image


def fill_taps(taps, sign, read, write):
    for phase in sorted({t[0] for t in taps}):
        image = read(phase).astype(f32).reshape(HEIGHT, BREADTH, GROUP)
        for right in sorted({t[2] for t in taps if t[0] == phase}):
            shifted = moved(image, 0, sign * right)
            for tap, (own, down, own_right) in enumerate(taps):
                if own == phase and own_right == right:
                    window = moved(shifted, sign * down, 0)
                    write(tap, window.reshape(CELLS, GROUP).astype(bf16))


def conv_kernel(taps, chunk, act_ref, w_ref, pre_ref, out_ref, cols):
    rows = chunk * CELLS

    def step(i, carry):
        base = pl.multiple_of(i * rows, rows)
        for n in range(chunk):

            def read(phase, n=n):
                return act_ref[phase, pl.ds(base + n * CELLS, CELLS), :]

            def write(tap, window, n=n):
                cols[n * CELLS : (n + 1) * CELLS, tap * GROUP : (tap + 1) * GROUP] = window

            fill_taps(taps, 1, read, write)
        pre = lax.dot_general(
            cols[...], w_ref[...], (((1,), (1,)), ((), ())), preferred_element_type=f32
        )
        pre_ref[pl.ds(base, rows), :] = pre
        out_ref[pl.ds(base, rows), :] = (gelu_act(pre) * GAMMA).astype(bf16)
        return carry

    lax.fori_loop(0, pre_ref.shape[0] // rows, step, 0)


def conv_forward(act, weight, taps):
    phases, cells, channels = act.shape
    chunk = 4
    return pl.pallas_call(
        functools.partial(conv_kernel, taps, chunk),
        grid=(channels // GROUP,),
        out_shape=[
            jax.ShapeDtypeStruct((cells, channels), f32),
            jax.ShapeDtypeStruct((cells, channels), bf16),
        ],
        in_specs=[
            pl.BlockSpec((phases, cells, GROUP), lambda g: (0, 0, g)),
            pl.BlockSpec((GROUP, 9 * GROUP), lambda g: (g, 0)),
        ],
        out_specs=[
            pl.BlockSpec((cells, GROUP), lambda g: (0, g)),
            pl.BlockSpec((cells, GROUP), lambda g: (0, g)),
        ],
        scratch_shapes=[pltpu.VMEM((chunk * CELLS, 9 * GROUP), bf16)],
        compiler_params=pltpu.CompilerParams(vmem_limit_bytes=32 * MIB),
        cost_estimate=pl.CostEstimate(
            flops=2 * cells * channels * 9 * GROUP,
            bytes_accessed=cells * channels * (6 + 2 * phases),
            transcendentals=cells * channels,
        ),
        name="conv_forward",
    )(act, weight)


def conv_back_kernel(taps, chunk, up_ref, act_ref, pre_ref, w_ref, down_ref, grad_ref, w_cols, up_cols, act_cols):
    rows = chunk * CELLS
    phases = act_ref.shape[0]
    order = [t for q in range(phases) for t in range(9) if taps[t][0] == q]
    place = {t: i for i, t in enumerate(order)}
    for t in range(9):
        w_cols[place[t] * GROUP : (place[t] + 1) * GROUP, :] = w_ref[:, t * GROUP : (t + 1) * GROUP]

    def step(i, carry):
        base = pl.multiple_of(i * rows, rows)
        for n in range(chunk):

            def read_act(phase, n=n):
                return act_ref[phase, pl.ds(base + n * CELLS, CELLS), :]

            def write_act(tap, window, n=n):
                act_cols[pl.ds(base + n * CELLS, CELLS), tap * GROUP : (tap + 1) * GROUP] = window

            fill_taps(taps, 1, read_act, write_act)
            flat = tuple((0, t[1], t[2]) for t in taps)

            def read_up(phase, n=n):
                return up_ref[pl.ds(base + n * CELLS, CELLS), :]

            def write_up(tap, window, n=n):
                at = place[tap] * GROUP
                up_cols[n * CELLS : (n + 1) * CELLS, at : at + GROUP] = window

            fill_taps(flat, -1, read_up, write_up)
        at = 0
        for phase in range(phases):
            size = sum(t[0] == phase for t in taps) * GROUP
            back = jnp.dot(
                up_cols[:, at : at + size], w_cols[at : at + size, :], preferred_element_type=f32
            )
            at += size
            pre = pre_ref[phase, pl.ds(base, rows), :]
            down_ref[phase, pl.ds(base, rows), :] = (gelu_prime(pre) * GAMMA * back).astype(bf16)
        return carry

    lax.fori_loop(0, up_ref.shape[0] // rows, step, 0)
    grad_ref[...] = lax.dot_general(
        up_ref[...], act_cols[...], (((0,), (0,)), ((), ())), preferred_element_type=f32
    ).astype(grad_ref.dtype)


def conv_backward(up, act, pre, weight, taps):
    phases, cells, channels = act.shape
    chunk = 4
    return pl.pallas_call(
        functools.partial(conv_back_kernel, taps, chunk),
        grid=(channels // GROUP,),
        out_shape=[
            jax.ShapeDtypeStruct((phases, cells, channels), bf16),
            jax.ShapeDtypeStruct((channels, 9 * GROUP), bf16),
        ],
        in_specs=[
            pl.BlockSpec((cells, GROUP), lambda g: (0, g)),
            pl.BlockSpec((phases, cells, GROUP), lambda g: (0, 0, g)),
            pl.BlockSpec((phases, cells, GROUP), lambda g: (0, 0, g)),
            pl.BlockSpec((GROUP, 9 * GROUP), lambda g: (g, 0)),
        ],
        out_specs=[
            pl.BlockSpec((phases, cells, GROUP), lambda g: (0, 0, g)),
            pl.BlockSpec((GROUP, 9 * GROUP), lambda g: (g, 0)),
        ],
        scratch_shapes=[
            pltpu.VMEM((9 * GROUP, GROUP), bf16),
            pltpu.VMEM((chunk * CELLS, 9 * GROUP), bf16),
            pltpu.VMEM((cells, 9 * GROUP), bf16),
        ],
        compiler_params=pltpu.CompilerParams(vmem_limit_bytes=48 * MIB),
        cost_estimate=pl.CostEstimate(
            flops=4 * cells * channels * 9 * GROUP,
            bytes_accessed=cells * channels * (2 + 8 * phases),
            transcendentals=cells * channels * phases,
        ),
        name="conv_backward",
    )(up, act, pre, weight)


def new_values(w, g, m, v, standard, clip):
    fan_in = w.shape[1]
    if standard:
        centre = w - jnp.mean(w, axis=-1, keepdims=True)
        spread = jnp.mean(centre * centre, axis=-1, keepdims=True)
        scale = lax.rsqrt(spread * fan_in + STD_EPS)
        along = jnp.sum(g * centre, axis=-1, keepdims=True)
        mean_g = jnp.mean(g, axis=-1, keepdims=True)
        g = scale * (g - mean_g) - (scale * scale * scale * along) * centre
    if clip:
        ceiling = CLIP * jnp.sqrt(jnp.sum(w * w, axis=-1, keepdims=True))
        norm = jnp.sqrt(jnp.sum(g * g, axis=-1, keepdims=True))
        g = g * (ceiling / jnp.maximum(norm, ceiling))
    m = DECAY_ONE * m + (1.0 - DECAY_ONE) * g
    v = DECAY_TWO * v + (1.0 - DECAY_TWO) * g * g
    m_hat = m * (1.0 / (1.0 - DECAY_ONE**STEP_COUNT))
    v_hat = v * (1.0 / (1.0 - DECAY_TWO**STEP_COUNT))
    return m, v, w - RATE * (m_hat / (jnp.sqrt(v_hat) + ADAM_EPS) + WEIGHT_DECAY * w)


def update_packed_kernel(shapes, share_ref, packed_ref, *refs):
    count = len(shapes)
    valid = pl.program_id(0) < share_ref[0]
    at = 0
    for k, shape in enumerate(shapes):
        part, width = shape[-2] // 6, shape[-1]
        for lead in leads(shape):
            g, at = read_packed(packed_ref, at, part, width)
            g = jnp.where(valid, g.astype(f32), 0.0)
            w, m, v = (refs[3 * k + i][lead] for i in range(3))
            for i, value in enumerate(new_values(w, g, m, v, True, True)):
                refs[3 * (count + k) + i][lead] = value


def update_packed(packed, members, share):
    specs, operands, shapes = [], [], []
    for weight, first, second in members:
        shape = weight.shape
        block = shape[:-2] + (shape[-2] // 6, shape[-1])
        zeros = (0,) * (len(shape) - 2)
        specs += [pl.BlockSpec(block, lambda j, zeros=zeros: zeros + (j, 0))] * 3
        operands += [weight, first, second]
        shapes.append(shape)
    total = sum(o.size for o in operands)
    outs = pl.pallas_call(
        functools.partial(update_packed_kernel, tuple(shapes)),
        grid=(6,),
        out_shape=[jax.ShapeDtypeStruct(o.shape, f32) for o in operands],
        in_specs=[
            pl.BlockSpec(memory_space=pltpu.SMEM),
            pl.BlockSpec((None,) + packed.shape[1:], lambda j: (j, 0, 0)),
        ]
        + specs,
        out_specs=specs,
        compiler_params=pltpu.CompilerParams(vmem_limit_bytes=58 * MIB),
        cost_estimate=pl.CostEstimate(
            flops=10 * total, bytes_accessed=9 * total, transcendentals=total // 3
        ),
        name="update_packed",
    )(share, packed, *operands)
    return [tuple(outs[3 * k : 3 * k + 3]) for k in range(len(members))]


def update_kernel(unit, standard, clip, block, share_ref, w_ref, g_ref, m_ref, v_ref, m_out, v_out, w_out):
    row = pl.program_id(0) * block + lax.broadcasted_iota(jnp.int32, (block, 1), 0)
    g = jnp.where(row % (6 * unit) < share_ref[0] * unit, g_ref[...].astype(f32), 0.0)
    m_out[...], v_out[...], w_out[...] = new_values(
        w_ref[...], g, m_ref[...], v_ref[...], standard, clip
    )


def update(weight, gradient, first, second, share, standard, clip):
    shape = weight.shape
    width = shape[-1]
    flat = [a.reshape(-1, width) for a in (weight, gradient, first, second)]
    rows = flat[0].shape[0]
    block = rows
    for size in range(192, 0, -16):
        if rows % size == 0:
            block = size
            break
    spec = pl.BlockSpec((block, width), lambda i: (i, 0))
    outs = pl.pallas_call(
        functools.partial(update_kernel, shape[-2] // 6, standard, clip, block),
        grid=(rows // block,),
        out_shape=[jax.ShapeDtypeStruct((rows, width), f32)] * 3,
        in_specs=[pl.BlockSpec(memory_space=pltpu.SMEM)] + [spec] * 4,
        out_specs=[spec] * 3,
        compiler_params=pltpu.CompilerParams(vmem_limit_bytes=48 * MIB),
        cost_estimate=pl.CostEstimate(
            flops=30 * rows * width, bytes_accessed=28 * rows * width, transcendentals=rows * width
        ),
        name="update",
    )(share, *flat)
    return tuple(o.reshape(shape) for o in outs)


def dot_t(left, right):
    return lax.dot_general(
        left, right, (((left.ndim - 1,), (1,)), ((), ())), preferred_element_type=f32
    )


def dot_n(left, right):
    return lax.dot_general(
        left, right, (((left.ndim - 1,), (0,)), ((), ())), preferred_element_type=f32
    )


def dot_sum(upstream, inputs):
    up = upstream.reshape(-1, upstream.shape[-1])
    low = inputs.reshape(-1, inputs.shape[-1])
    return lax.dot_general(up, low, (((0,), (0,)), ((), ())), preferred_element_type=f32)


def tail_forward(act_three, out_w, down_w, up_w):
    images = act_three.shape[0] // CELLS
    pre_four = dot_t(act_three, out_w).reshape(images, CELLS, -1)
    squeezed = (jnp.sum(pre_four, axis=1) / CELLS).astype(bf16)
    pre_down = dot_t(squeezed, down_w)
    act_down = gelu_act(pre_down).astype(bf16)
    gate_sig = jax.nn.sigmoid(dot_t(act_down, up_w))
    return pre_four, squeezed, pre_down, act_down, gate_sig


def tail_backward(grad_hidden, stored, down_w, up_w, gain):
    pre_four, squeezed, pre_down, act_down, gate_sig = stored
    gate = 2.0 * gate_sig
    raw_gate = jnp.sum(grad_hidden * pre_four, axis=1)
    gain_part = ALPHA * jnp.sum(raw_gate * gate)
    grad_gate = raw_gate * (ALPHA * gain)
    grad_up = (grad_gate * 2.0 * gate_sig * (1.0 - gate_sig)).astype(bf16)
    grad_down = (gelu_prime(pre_down) * dot_n(grad_up, up_w)).astype(bf16)
    grad_squeezed = dot_n(grad_down, down_w)
    grad_four = (
        grad_hidden * (ALPHA * gain * gate)[:, None, :] + (grad_squeezed / CELLS)[:, None, :]
    ).astype(bf16)
    factors = jnp.concatenate([grad_up, act_down, grad_down, squeezed], axis=1)
    return grad_four.reshape(-1, grad_four.shape[-1]), factors, gain_part


def body(
    images,
    labels,
    class_counts,
    owner_share,
    w_entry,
    first_entry,
    second_entry,
    w_in,
    first_in,
    second_in,
    w_mid,
    first_mid,
    second_mid,
    w_out,
    first_out,
    second_out,
    se_down,
    first_down,
    second_down,
    se_up,
    first_up,
    second_up,
    w_final,
    first_final,
    second_final,
    head,
    first_head,
    second_head,
    small_params,
    first_small,
    second_small,
):
    owner, local, starts, slot_part = owner_tables(owner_share)
    me = lax.axis_index("dp")
    devices = lax.axis_size("dp")
    my_share = lax.dynamic_slice_in_dim(owner_share, me, 1, 0)
    my_start = lax.dynamic_index_in_dim(starts, me, 0, keepdims=False)

    rows_n, cols_n = lax.axis_size("ha"), lax.axis_size("wa")
    spread = rows_n * cols_n
    micro, per_dp, tile_h, tile_w, in_width = images.shape
    count = micro * per_dp // spread
    tiles = images.reshape(spread, count, tile_h, tile_w, in_width)
    tiles = lax.all_to_all(tiles, ("ha", "wa"), 0, 0, tiled=True)
    tiles = tiles.reshape(
        rows_n, cols_n, count, tile_h // 2, 2, tile_w // 2, 2, in_width
    ).transpose(4, 6, 2, 0, 3, 1, 5, 7)
    cells = count * CELLS
    pixels = tiles.reshape(4, cells, in_width)
    spot = lax.axis_index("ha") * cols_n + lax.axis_index("wa")
    my_labels = lax.dynamic_slice_in_dim(labels.reshape(-1), spot * count, count, 0)

    def gather(entries, halves):
        if not known_mesh():
            return gather_plain(entries, owner, local)
        shapes = tuple((e[0].shape[-2] // 6, e[0].shape[-1]) for e in entries)
        buffers, which, places = gather_packed(pack_weights(entries), halves, owner, local)
        return unpack_weights(buffers, which, places, shapes)

    def block_entries(layer):
        first = (w_entry, (), True) if layer == 0 else (w_in, (layer - 1,), True)
        return [
            first,
            (w_mid, (layer, 0), True),
            (w_mid, (layer, 1), True),
            (w_out, (layer,), True),
            (se_down, (layer,), False),
            (se_up, (layer,), False),
        ]

    in_low, mid_low, out_low, down_low, up_low = ([None] * LAYERS for _ in range(5))
    for layer in range(LAYERS):
        in_low[layer], mid_a, mid_b, out_low[layer], down_low[layer], up_low[layer] = gather(
            block_entries(layer), layer > 0
        )
        mid_low[layer] = (mid_a, mid_b)
    final_low, head_low = gather([(w_final, (), True), (head, (), False)], True)
    entry_low = in_low[0]
    in_low[0] = entry_low[:NECK]
    skip_low = entry_low[NECK:]

    gains = small_params[:LAYERS]
    head_bias = small_params[LAYERS:]
    images_all = micro * per_dp * lax.axis_size("dp")
    class_weight = 1.0 / class_counts.astype(f32)

    kept = []
    hidden = None
    for layer in range(LAYERS):
        scale = GAMMA * (1.0 + layer * ALPHA * ALPHA) ** (-0.5)
        source = pixels.astype(f32) if layer == 0 else hidden
        act_zero = (gelu_act(source) * scale).astype(bf16)
        if layer:
            act_zero = act_zero.reshape(1, cells, -1)
        taps = TAPS_TWO if layer == 0 else TAPS_ONE
        pre_one = dot_t(act_zero, in_low[layer])
        act_one = (gelu_act(pre_one) * GAMMA).astype(bf16)
        pre_two, act_two = conv_forward(act_one, mid_low[layer][0], taps)
        pre_three, act_three = conv_forward(act_two[None], mid_low[layer][1], TAPS_ONE)
        tail = tail_forward(act_three, out_low[layer], down_low[layer], up_low[layer])
        branch = (ALPHA * gains[layer]) * tail[0] * (2.0 * tail[4])[:, None, :]
        pooled = None
        if layer == 0:
            pooled = (jnp.sum(act_zero.astype(f32), axis=0) * 0.25).astype(bf16)
            shortcut = dot_t(pooled, skip_low).reshape(branch.shape)
        else:
            shortcut = hidden.reshape(branch.shape)
        before = hidden
        hidden = (shortcut + branch).reshape(cells, -1)
        kept.append((before, act_zero, pre_one, act_one, pre_two, act_two, pre_three, act_three, tail, pooled))

    hidden_low = hidden.astype(bf16)
    pre_final = dot_t(hidden_low, final_low).reshape(count, CELLS, -1)
    pooled_final = (jnp.sum(gelu_act(pre_final) * GAMMA, axis=1) / CELLS).astype(bf16)
    logits = dot_n(pooled_final, head_low) + head_bias
    largest = jnp.max(logits, axis=1, keepdims=True)
    log_total = largest[:, 0] + jnp.log(jnp.sum(jnp.exp(logits - largest), axis=1))
    one_hot = (my_labels[:, None] == jnp.arange(logits.shape[1])[None, :]).astype(f32)
    picked = jnp.sum(one_hot * logits, axis=1)
    image_weight = jnp.sum(one_hot * class_weight[None, :], axis=1)
    loss_part = jnp.sum(image_weight * (log_total - picked))
    softmax_p = jnp.exp(logits - log_total[:, None])
    grad_logits = image_weight[:, None] * (softmax_p - one_hot) / images_all
    bias_part = jnp.sum(grad_logits, axis=0)
    grad_low = grad_logits.astype(bf16)
    head_factors = lax.all_gather(
        jnp.concatenate([pooled_final, grad_low], axis=1), EVERY, axis=0, tiled=True
    )
    grad_pooled = dot_t(grad_low, head_low) * (GAMMA / CELLS)
    grad_final = (gelu_prime(pre_final) * grad_pooled[:, None, :]).astype(bf16).reshape(cells, -1)
    final_grad = dot_sum(grad_final, hidden_low).astype(bf16)
    grad_hidden = dot_n(grad_final, final_low)

    in_grads = [None] * LAYERS
    mid_grads = [None] * LAYERS
    out_grads = [None] * LAYERS
    block_factors = [None] * LAYERS
    gain_parts = [None] * LAYERS
    for layer in reversed(range(LAYERS)):
        before, act_zero, pre_one, act_one, pre_two, act_two, pre_three, act_three, tail, pooled = kept[layer]
        taps = TAPS_TWO if layer == 0 else TAPS_ONE
        grad_four, factors, gain_parts[layer] = tail_backward(
            grad_hidden.reshape(count, CELLS, -1), tail, down_low[layer], up_low[layer], gains[layer]
        )
        block_factors[layer] = lax.all_gather(factors, EVERY, axis=0, tiled=True)
        out_grads[layer] = dot_sum(grad_four, act_three).astype(bf16)
        grad_three = (gelu_prime(pre_three) * GAMMA * dot_n(grad_four, out_low[layer])).astype(bf16)
        grad_two, mid_b = conv_backward(grad_three, act_two[None], pre_two[None], mid_low[layer][1], TAPS_ONE)
        grad_one, mid_a = conv_backward(grad_two[0], act_one, pre_one, mid_low[layer][0], taps)
        mid_grads[layer] = (mid_a, mid_b)
        in_grad = dot_sum(grad_one, act_zero).astype(bf16)
        if layer == 0:
            skip_grad = dot_sum(grad_hidden.astype(bf16), pooled).astype(bf16)
            in_grads[layer] = jnp.concatenate([in_grad, skip_grad], axis=0)
        else:
            in_grads[layer] = in_grad
            scale = GAMMA * (1.0 + layer * ALPHA * ALPHA) ** (-0.5)
            grad_zero = dot_n(grad_one[0], in_low[layer])
            grad_hidden = grad_hidden + gelu_prime(before) * scale * grad_zero

    def own_units(units, inputs):
        width = units.shape[1]
        part = width // starts.shape[0] // 4
        padded = jnp.pad(units, ((0, 0), (0, 4 * part)))
        mine = lax.dynamic_slice_in_dim(padded, my_start * part, 6 * part, 1)
        return dot_sum(mine, inputs)

    final_width = pooled_final.shape[1]
    head_own = own_units(head_factors[:, :final_width], head_factors[:, final_width:])
    wide, narrow = tail[0].shape[-1], tail[3].shape[-1]
    up_own, down_own = [], []
    for layer in range(LAYERS):
        every = block_factors[layer]
        ends = [wide, wide + narrow, wide + 2 * narrow, 2 * wide + 2 * narrow]
        up_own.append(own_units(every[:, : ends[0]], every[:, ends[0] : ends[1]]))
        down_own.append(own_units(every[:, ends[1] : ends[2]], every[:, ends[2] : ends[3]]))

    small = jnp.concatenate([loss_part[None], jnp.stack(gain_parts), bias_part])
    small = jnp.sum(lax.all_gather(small, EVERY, axis=0, tiled=False), axis=0)
    loss_sum = small[0]
    small_grad = small[1:]

    flat_mids = [g for pair in mid_grads for g in pair]
    local_grads = [final_grad, in_grads[0]] + in_grads[1:] + out_grads + flat_mids
    members = (
        (w_final, first_final, second_final),
        (w_entry, first_entry, second_entry),
        (w_in, first_in, second_in),
        (w_out, first_out, second_out),
        (w_mid, first_mid, second_mid),
    )
    if known_mesh():
        packed = pack_gradients(local_grads, slot_part, devices, SPAN)
        new = update_packed(sum_at_owners(packed), members, my_share)
    else:
        sums = [sum_plain(g, slot_part) for g in local_grads]
        new = []
        for weight, first, second in members:
            count = len(leads(weight.shape))
            total, sums = jnp.stack(sums[:count]), sums[count:]
            new.append(update(weight, total, first, second, my_share, True, True))
    final_new, entry_new, in_new, out_new, mid_new = new
    down_new = update(se_down, jnp.stack(down_own), first_down, second_down, my_share, False, True)
    up_new = update(se_up, jnp.stack(up_own), first_up, second_up, my_share, False, True)
    head_new = update(head, head_own, first_head, second_head, my_share, False, False)
    results = [loss_sum]
    for new in (entry_new, in_new, mid_new, out_new, down_new, up_new, final_new, head_new):
        results.extend(new)
    m = DECAY_ONE * first_small + (1.0 - DECAY_ONE) * small_grad
    v = DECAY_TWO * second_small + (1.0 - DECAY_TWO) * small_grad * small_grad
    m_hat = m / (1.0 - DECAY_ONE**STEP_COUNT)
    v_hat = v / (1.0 - DECAY_TWO**STEP_COUNT)
    results.extend(
        [
            m,
            v,
            small_params
            - SMALL_RATE * (m_hat / (jnp.sqrt(v_hat) + ADAM_EPS) + WEIGHT_DECAY * small_params),
        ]
    )
    return tuple(results)


def solution(mesh):
    owned = (
        [P("dp", None)] * 3
        + [P(None, "dp", None)] * 3
        + [P(None, None, "dp", None)] * 3
        + [P(None, "dp", None)] * 9
        + [P("dp", None)] * 6
        + [P()] * 3
    )
    return jax.shard_map(
        body,
        mesh=mesh,
        in_specs=tuple([P(None, "dp", "ha", "wa", None), P(None, "dp"), P(), P()] + owned),
        out_specs=tuple([P()] + owned),
        check_vma=False,
    )
```

```python
import functools

import jax
import jax.numpy as jnp
from jax import lax
from jax.experimental import pallas as pl
from jax.experimental.pallas import tpu as pltpu
from jax.sharding import PartitionSpec as P

NECK = 768
GROUP = 128
HEIGHT = 8
BREADTH = 8
CELLS = HEIGHT * BREADTH
LAYERS = 2
STEP_COUNT = 5

GAMMA = 1.7015043497085571
ALPHA = 0.2
CLIP = 0.01
RATE = 0.05
SMALL_RATE = 0.5
DECAY_ONE = 0.9
DECAY_TWO = 0.999
ADAM_EPS = 1e-08
WEIGHT_DECAY = 5e-05
STD_EPS = 0.0001
GELU_SCALE = 0.7978845608028654
GELU_CUBE = 0.044715
EVERY = ("dp", "ha", "wa")
MIB = 1 << 20

TAPS_ONE = tuple((0, t // 3 - 1, t % 3 - 1) for t in range(9))
TAPS_TWO = tuple(((t // 3 % 2) * 2 + t % 3 % 2, t // 3 // 2, t % 3 // 2) for t in range(9))

CHUNK = 16

f32 = jnp.float32
bf16 = jnp.bfloat16


def gelu_act(v):
    return 0.5 * v * (1.0 + jnp.tanh(GELU_SCALE * (v + GELU_CUBE * v * v * v)))


def gelu_prime(v):
    th = jnp.tanh(GELU_SCALE * (v + GELU_CUBE * v * v * v))
    return 0.5 * (1.0 + th) + (0.5 * GELU_SCALE) * v * (1.0 - th * th) * (
        1.0 + 3.0 * GELU_CUBE * v * v
    )


def standardize(weight):
    fan_in = weight.shape[-1]
    centre = weight - jnp.mean(weight, axis=-1, keepdims=True)
    spread = jnp.mean(centre * centre, axis=-1, keepdims=True)
    return centre * lax.rsqrt(spread * fan_in + STD_EPS)


def owner_tables(shares):
    devices = shares.shape[0]
    ids = jnp.arange(devices, dtype=jnp.int32)
    starts = jnp.sum(jnp.where(ids[None, :] < ids[:, None], shares[None, :], 0), axis=1)
    part_ids = jnp.arange(4 * devices, dtype=jnp.int32)
    owner = jnp.sum((part_ids[:, None] >= (starts + shares)[None, :]).astype(jnp.int32), axis=1)
    first = jnp.sum(jnp.where(owner[:, None] == ids[None, :], starts[None, :], 0), axis=1)
    local = (part_ids - first).astype(jnp.int32)
    held = jnp.minimum(jnp.arange(6, dtype=jnp.int32)[None, :], shares[:, None] - 1)
    return owner, local, starts, (starts[:, None] + held).reshape(-1).astype(jnp.int32)


def known_mesh():
    return tuple(lax.axis_size(a) for a in EVERY) == (4, 4, 2)


def unit_slots(owner, local, part):
    return ((owner * 6 + local)[:, None] * part + jnp.arange(part)[None, :]).reshape(-1)


def gather_plain(entries, owner, local):
    full = []
    for array, lead, standard in entries:
        block = standardize(array[lead]) if standard else array[lead]
        every = lax.all_gather(block.astype(bf16), "dp", axis=0, tiled=True)
        full.append(jnp.take(every, unit_slots(owner, local, block.shape[0] // 6), axis=0))
    return full


def sum_plain(gradient, slot_part):
    part = gradient.shape[0] // (4 * lax.axis_size("dp"))
    units = (slot_part[:, None] * part + jnp.arange(part)[None, :]).reshape(-1)
    slots = jnp.take(gradient, units, axis=0)
    owned = lax.psum_scatter(slots, "dp", scatter_dimension=0, tiled=True)
    return lax.psum(owned, ("ha", "wa"))


def leads(shape):
    tuples = [()]
    for size in shape[:-2]:
        tuples = [t + (i,) for t in tuples for i in range(size)]
    return tuples


def packed_rows(part, width):
    return part * (-(-width // 128))


def pack_into(ref, at, block):
    part, width = block.shape
    for column in range(0, width, 128):
        lanes = min(128, width - column)
        piece = block[:, column : column + lanes]
        if lanes < 128:
            piece = jnp.concatenate([piece, jnp.zeros((part, 128 - lanes), piece.dtype)], axis=1)
        ref[at : at + part, :] = piece
        at += part
    return at


def read_packed(ref, at, part, width):
    pieces = []
    for column in range(0, width, 128):
        pieces.append(ref[at : at + part, : min(128, width - column)])
        at += part
    return (pieces[0] if len(pieces) == 1 else jnp.concatenate(pieces, axis=1)), at


def pack_weights_kernel(standard, *refs):
    out_ref = refs[-1]
    at = 0
    for ref, flag in zip(refs[:-1], standard):
        block = ref[...]
        at = pack_into(out_ref, at, (standardize(block) if flag else block).astype(bf16))


def pack_weights(entries):
    specs, rows = [], 0
    for array, lead, _ in entries:
        part, width = array.shape[-2] // 6, array.shape[-1]
        specs.append(
            pl.BlockSpec((None,) * len(lead) + (part, width), lambda j, lead=lead: lead + (j, 0))
        )
        rows += packed_rows(part, width)
    return pl.pallas_call(
        functools.partial(pack_weights_kernel, tuple(e[2] for e in entries)),
        grid=(6,),
        out_shape=jax.ShapeDtypeStruct((6, rows, 128), bf16),
        in_specs=specs,
        out_specs=pl.BlockSpec((None, rows, 128), lambda j: (j, 0, 0)),
        compiler_params=pltpu.CompilerParams(vmem_limit_bytes=40 * MIB),
        cost_estimate=pl.CostEstimate(
            flops=6 * rows * 128 * 8, bytes_accessed=6 * rows * 128 * 6, transcendentals=0
        ),
        name="pack_weights",
    )(*[e[0] for e in entries])


def unpack_kernel(count, shapes, which_ref, place_ref, *refs):
    sources = refs[:count]
    outs = refs[count : count + len(shapes)]
    held, *rest = refs[count + len(shapes) :]
    stages, (arrived, left) = rest[: len(shapes)], rest[len(shapes) :]
    parts = which_ref.shape[0]

    def fetch(i, carry):
        for s, source in enumerate(sources):

            @pl.when(which_ref[i] == s)
            def _(source=source):
                pltpu.make_async_copy(source.at[place_ref[i]], held.at[i], arrived.at[i]).start()

        return carry

    def spread(i, carry):
        pltpu.make_async_copy(held.at[i], held.at[i], arrived.at[i]).wait()
        at = 0
        for k, (part, width) in enumerate(shapes):
            rows = pl.ds(pl.multiple_of(i * part, part), part)
            block, at = read_packed(held.at[i], at, part, width)
            stages[k][rows, :] = block
            pltpu.make_async_copy(stages[k].at[rows, :], outs[k].at[rows, :], left.at[k]).start()
        return carry

    lax.fori_loop(0, parts, fetch, 0)
    lax.fori_loop(0, parts, spread, 0)
    for k in range(len(shapes)):
        pltpu.make_async_copy(stages[k], outs[k], left.at[k]).wait()


def unpack_weights(sources, which, place, shapes):
    count, parts = len(sources), which.shape[0]
    rows = sources[0].shape[1]
    full = [(parts * p, w) for p, w in shapes]
    return pl.pallas_call(
        functools.partial(unpack_kernel, count, shapes),
        out_shape=[jax.ShapeDtypeStruct(f, bf16) for f in full],
        in_specs=[pl.BlockSpec(memory_space=pltpu.SMEM)] * 2
        + [pl.BlockSpec(memory_space=pl.ANY)] * count,
        out_specs=[pl.BlockSpec(memory_space=pl.ANY)] * len(shapes),
        scratch_shapes=[pltpu.VMEM((parts, rows, 128), bf16)]
        + [pltpu.VMEM(f, bf16) for f in full]
        + [pltpu.SemaphoreType.DMA((parts,)), pltpu.SemaphoreType.DMA((len(shapes),))],
        compiler_params=pltpu.CompilerParams(vmem_limit_bytes=40 * MIB),
        cost_estimate=pl.CostEstimate(
            flops=0, bytes_accessed=parts * rows * 128 * 4, transcendentals=0
        ),
        name="unpack_weights",
    )(which, place, *sources)


def after(value, *others):
    return lax.optimization_barrier((value,) + others)[0]


CHIP = [(i, i ^ 2) for i in range(4)]
CORE = [(i, i ^ 1) for i in range(4)]


class Gather:
    def __init__(self, entries, whole=False):
        self.shapes = tuple((e[0].shape[-2] // 6, e[0].shape[-1]) for e in entries)
        self.own = pack_weights(entries)
        self.whole = whole

    def along_x(self, *others):
        mine = self.own
        if not self.whole:
            mine = lax.dynamic_slice_in_dim(mine, lax.axis_index("wa") * 3, 3, 0)
        self.near = lax.ppermute(after(mine, *others), "dp", CHIP)

    def along_y(self):
        self.far = lax.ppermute(self.near, "wa", [(0, 1), (1, 0)])

    def cores(self):
        buffers = [self.own, self.near] + ([] if self.whole else [self.far])
        self.buffers = buffers + [lax.ppermute(b, "dp", CORE) for b in buffers]

    def unpacked(self, tables):
        return unpack_weights(self.buffers, *tables[self.whole], self.shapes)


def source_tables(owner, local, whole):
    me = lax.axis_index("dp")
    side = lax.axis_index("wa")
    away = owner // 2 != me // 2
    if whole:
        which, at, count = away.astype(jnp.int32), local, 2
    else:
        which = jnp.where(away, jnp.where(local // 3 == side, 1, 2), 0)
        at, count = jnp.where(away, local % 3, local), 3
    which = (which + count * (owner % 2 != me % 2)).astype(jnp.int32)
    return which, at.astype(jnp.int32)


def pack_gradients_kernel(pad, part_ref, *refs):
    out_ref = refs[-1]
    at = 0
    for ref in refs[:-1]:
        at = pack_into(out_ref, at, ref[...].astype(bf16))
    if pad:
        out_ref[at : at + pad, :] = jnp.zeros((pad, 128), bf16)


def pack_gradients(gradients, slot_part, devices, unit):
    specs, rows = [], 0
    for gradient in gradients:
        part, width = gradient.shape[0] // (4 * devices), gradient.shape[1]
        specs.append(pl.BlockSpec((part, width), lambda s, parts: (parts[s], 0)))
        rows += packed_rows(part, width)
    pad = -rows % unit
    rows += pad
    slots = 6 * devices
    return pl.pallas_call(
        functools.partial(pack_gradients_kernel, pad),
        grid_spec=pltpu.PrefetchScalarGridSpec(
            num_scalar_prefetch=1,
            grid=(slots,),
            in_specs=specs,
            out_specs=pl.BlockSpec((None, rows, 128), lambda s, parts: (s, 0, 0)),
        ),
        out_shape=jax.ShapeDtypeStruct((slots, rows, 128), bf16),
        compiler_params=pltpu.CompilerParams(vmem_limit_bytes=40 * MIB),
        cost_estimate=pl.CostEstimate(
            flops=0, bytes_accessed=slots * rows * 128 * 4, transcendentals=0
        ),
        name="pack_gradients",
    )(slot_part, *gradients)


SPAN = 1024
AXES = ("x", "y", "near", "far")
ORDERS = (AXES,)
LAGS = (0, 1, 2, 3, 4, 5, 6, 7)


def sum_kernel(orders, spans, packed, owned, own, core, one, two, three, four, sends, recvs, local_sems):
    dp, z, y = lax.axis_index("dp"), lax.axis_index("ha"), lax.axis_index("wa")
    bit = {"x": dp // 2, "core": dp % 2, "y": y, "near": z % 2, "far": z // 2}
    peer = {
        "x": {"dp": (dp + 2) % 4},
        "core": {"dp": dp + 1 - 2 * (dp % 2)},
        "y": {"wa": 1 - y},
        "near": {"ha": z + 1 - 2 * (z % 2)},
        "far": {"ha": (z + 2) % 4},
    }
    barrier = pltpu.get_barrier_semaphore()
    for other in peer.values():
        pl.semaphore_signal(barrier, inc=1, device_id=other, device_id_type=pl.DeviceIdType.MESH)
    pl.semaphore_wait(barrier, len(peer))

    buffers = [core, one, two, three, four]
    kinds = len(orders)

    def index(ref, chunk, names, fixed):
        return ref.at[(chunk,) + tuple(fixed[n] if n in fixed else slice(None) for n in names)]

    def remote(src, dst, stage, chunk, to):
        return pltpu.make_async_remote_copy(
            src_ref=src,
            dst_ref=dst,
            send_sem=sends.at[stage, chunk],
            recv_sem=recvs.at[stage, chunk],
            device_id=peer[to],
            device_id_type=pl.DeviceIdType.MESH,
        )

    def copy_of(stage, kind, chunk):
        order = orders[kind]
        if stage == 0:
            return remote(packed.at[:, 1 - bit["core"], chunk], core.at[chunk], 0, chunk, "core")
        if stage <= 4:
            before = [n for n in AXES if n not in order[: stage - 1]]
            axis = order[stage - 1]
            src = index(buffers[stage - 1], chunk, before, {axis: 1 - bit[axis]})
            return remote(src, buffers[stage].at[chunk], stage, chunk, axis)
        spread = [n for n in reversed(order) if n != "x"]
        axis = spread[stage - 5]
        fixed = {n: bit[n] for n in spread[stage - 5 :]}
        place = index(owned, chunk, AXES[1:], fixed)
        return remote(four.at[chunk] if stage == 5 else place, place, stage, chunk, axis)

    def load(chunk):
        slot = chunk % 2
        return pltpu.make_async_copy(
            packed.at[:, bit["core"], chunk], own.at[slot], local_sems.at[slot]
        )

    def store(chunk):
        place = owned.at[chunk, bit["y"], bit["near"], bit["far"]]
        return pltpu.make_async_copy(four.at[chunk], place, local_sems.at[2 + chunk])

    def add(target, names, other, prefix=()):
        for at in names:
            there = target[at].astype(f32) + other(at).astype(f32)
            target[at] = there.astype(bf16)

    def grid(count):
        return leads((2,) * count + (1, 1))

    def arrive(stage, kind, chunk):
        copy_of(stage, kind, chunk).wait_recv()
        order = orders[kind]
        if stage == 0:
            load(chunk).wait()
            add(core, [(chunk,) + t for t in grid(4)], lambda at: own[(chunk % 2,) + at[1:]])
        elif stage <= 4:
            before = [n for n in AXES if n not in order[: stage - 1]]
            axis = order[stage - 1]
            where = before.index(axis)

            def mine(at):
                rest = at[1:]
                return buffers[stage - 1][(chunk,) + rest[:where] + (bit[axis],) + rest[where:]]

            add(buffers[stage], [(chunk,) + t for t in grid(4 - stage)], mine)
            if stage == 4:
                store(chunk).start()
        if stage == 5:
            store(chunk).wait()

    ahead, last = 3, 7
    for chunk in range(ahead):
        copy_of(0, chunk % kinds, chunk).start()
    load(0).start()

    def step(s, q):
        @pl.when(s + ahead < spans)
        def _():
            copy_of(0, (q + ahead) % kinds, s + ahead).start()

        @pl.when(s + 1 < spans)
        def _():
            load(s + 1).start()

        for stage in range(last + 1):
            chunk = s - LAGS[stage]
            kind = (q - LAGS[stage]) % kinds

            @pl.when((chunk >= 0) & (chunk < spans))
            def _(stage=stage, chunk=chunk, kind=kind):
                arrive(stage, kind, chunk)
                if stage < last:
                    copy_of(stage + 1, kind, chunk).start()

    def steps(i, carry):
        for q in range(kinds):
            step(i * kinds + q, q)
        return carry

    lax.fori_loop(0, -(-(spans + LAGS[-1]) // kinds), steps, 0)

    def sent(i, carry):
        for q in range(kinds):
            for stage in range(last + 1):
                copy_of(stage, q, i * kinds + q).wait_send()
        return carry

    lax.fori_loop(0, spans // kinds, sent, 0)


def sum_at_owners(packed):
    slots, rows, lanes = packed.shape
    spans = 6 * rows // SPAN
    r = SPAN // 8
    orders = ORDERS
    owned = pl.pallas_call(
        functools.partial(sum_kernel, orders, spans),
        out_shape=jax.ShapeDtypeStruct((spans, 2, 2, 2, r, 128), bf16),
        in_specs=[pl.BlockSpec(memory_space=pl.ANY)],
        out_specs=pl.BlockSpec(memory_space=pl.ANY),
        scratch_shapes=[
            pltpu.VMEM((2, 2, 2, 2, 2, r, 128), bf16),
            pltpu.VMEM((spans, 2, 2, 2, 2, r, 128), bf16),
            pltpu.VMEM((spans, 2, 2, 2, r, 128), bf16),
            pltpu.VMEM((spans, 2, 2, r, 128), bf16),
            pltpu.VMEM((spans, 2, r, 128), bf16),
            pltpu.VMEM((spans, r, 128), bf16),
            pltpu.SemaphoreType.DMA((8, spans)),
            pltpu.SemaphoreType.DMA((8, spans)),
            pltpu.SemaphoreType.DMA((2 + spans,)),
        ],
        compiler_params=pltpu.CompilerParams(
            collective_id=1, has_side_effects=True, vmem_limit_bytes=56 * MIB
        ),
        cost_estimate=pl.CostEstimate(
            flops=slots * rows * 128, bytes_accessed=slots * rows * 128 * 4, transcendentals=0
        ),
        name="sum_at_owners",
    )(packed.reshape(2, 2, spans, 2, 2, 2, r, 128))
    return owned.reshape(6, rows, lanes)


def prepare_kernel(tiles_ref, place_ref, act_ref, pooled_ref):
    sources, tile_h, tile_w, width = tiles_ref.shape
    pixels = tiles_ref[...].astype(f32).reshape(sources * tile_h * tile_w, width).astype(bf16)
    image = jnp.dot(place_ref[...], pixels, preferred_element_type=f32)
    act = (gelu_act(image) * GAMMA).astype(bf16).reshape(4, CELLS, width)
    act_ref[...] = act
    total = act[0].astype(f32) + act[1].astype(f32) + act[2].astype(f32) + act[3].astype(f32)
    pooled_ref[...] = (total * 0.25).astype(bf16)


def prepare(tiles, rows_n, cols_n):
    sources, count, tile_h, tile_w, width = tiles.shape
    pixels = 4 * CELLS
    down = jnp.arange(sources)[:, None, None] // cols_n * tile_h + jnp.arange(tile_h)[None, :, None]
    along = jnp.arange(sources)[:, None, None] % cols_n * tile_w + jnp.arange(tile_w)[None, None, :]
    target = ((down % 2 * 2 + along % 2) * HEIGHT + down // 2) * BREADTH + along // 2
    place = (jnp.arange(pixels)[:, None] == target.reshape(1, pixels)).astype(bf16)
    return pl.pallas_call(
        prepare_kernel,
        grid=(count,),
        out_shape=[
            jax.ShapeDtypeStruct((4, count * CELLS, width), bf16),
            jax.ShapeDtypeStruct((count * CELLS, width), bf16),
        ],
        in_specs=[
            pl.BlockSpec((sources, None, tile_h, tile_w, width), lambda n: (0, n, 0, 0, 0)),
            pl.BlockSpec((pixels, pixels), lambda n: (0, 0)),
        ],
        out_specs=[
            pl.BlockSpec((4, CELLS, width), lambda n: (0, n, 0)),
            pl.BlockSpec((CELLS, width), lambda n: (n, 0)),
        ],
        compiler_params=pltpu.CompilerParams(vmem_limit_bytes=32 * MIB),
        cost_estimate=pl.CostEstimate(
            flops=2 * count * pixels * pixels * width,
            bytes_accessed=5 * count * pixels * width,
            transcendentals=count * pixels * width,
        ),
        name="prepare",
    )(tiles, place)


def moved(image, down, right):
    if right:
        column = lax.broadcasted_iota(jnp.int32, image.shape, 1) + right
        image = pltpu.roll(image, (-right) % BREADTH, 1)
        image = jnp.where((column >= 0) & (column < BREADTH), image, 0.0)
    if down:
        edge = jnp.zeros((abs(down),) + image.shape[1:], image.dtype)
        if down > 0:
            image = jnp.concatenate([image[down:], edge], axis=0)
        else:
            image = jnp.concatenate([edge, image[:down]], axis=0)
    return image


def fill_taps(taps, sign, read, write):
    for phase in sorted({t[0] for t in taps}):
        image = read(phase).astype(f32).reshape(HEIGHT, BREADTH, GROUP)
        for right in sorted({t[2] for t in taps if t[0] == phase}):
            shifted = moved(image, 0, sign * right)
            for tap, (own, down, own_right) in enumerate(taps):
                if own == phase and own_right == right:
                    window = moved(shifted, sign * down, 0)
                    write(tap, window.reshape(CELLS, GROUP).astype(bf16))


def conv_kernel(taps, chunk, act_ref, w_ref, pre_ref, out_ref, cols):
    rows = chunk * CELLS

    def step(i, carry):
        base = pl.multiple_of(i * rows, rows)
        for n in range(chunk):

            def read(phase, n=n):
                return act_ref[phase, pl.ds(base + n * CELLS, CELLS), :]

            def write(tap, window, n=n):
                cols[n * CELLS : (n + 1) * CELLS, tap * GROUP : (tap + 1) * GROUP] = window

            fill_taps(taps, 1, read, write)
        pre = lax.dot_general(
            cols[...], w_ref[...], (((1,), (1,)), ((), ())), preferred_element_type=f32
        )
        pre_ref[pl.ds(base, rows), :] = pre
        out_ref[pl.ds(base, rows), :] = (gelu_act(pre) * GAMMA).astype(bf16)
        return carry

    lax.fori_loop(0, pre_ref.shape[0] // rows, step, 0)


def conv_forward(act, weight, taps):
    phases, cells, channels = act.shape
    chunk = min(CHUNK, cells // CELLS)
    return pl.pallas_call(
        functools.partial(conv_kernel, taps, chunk),
        grid=(channels // GROUP,),
        out_shape=[
            jax.ShapeDtypeStruct((cells, channels), f32),
            jax.ShapeDtypeStruct((cells, channels), bf16),
        ],
        in_specs=[
            pl.BlockSpec((phases, cells, GROUP), lambda g: (0, 0, g)),
            pl.BlockSpec((GROUP, 9 * GROUP), lambda g: (g, 0)),
        ],
        out_specs=[
            pl.BlockSpec((cells, GROUP), lambda g: (0, g)),
            pl.BlockSpec((cells, GROUP), lambda g: (0, g)),
        ],
        scratch_shapes=[pltpu.VMEM((chunk * CELLS, 9 * GROUP), bf16)],
        compiler_params=pltpu.CompilerParams(vmem_limit_bytes=32 * MIB),
        cost_estimate=pl.CostEstimate(
            flops=2 * cells * channels * 9 * GROUP,
            bytes_accessed=cells * channels * (6 + 2 * phases),
            transcendentals=cells * channels,
        ),
        name="conv_forward",
    )(act, weight)


def conv_back_kernel(taps, chunk, up_ref, act_ref, pre_ref, w_ref, down_ref, grad_ref, w_cols, up_cols, act_cols):
    rows = chunk * CELLS
    phases = act_ref.shape[0]
    order = [t for q in range(phases) for t in range(9) if taps[t][0] == q]
    place = {t: i for i, t in enumerate(order)}
    for t in range(9):
        w_cols[place[t] * GROUP : (place[t] + 1) * GROUP, :] = w_ref[:, t * GROUP : (t + 1) * GROUP]

    def step(i, carry):
        base = pl.multiple_of(i * rows, rows)
        for n in range(chunk):

            def read_act(phase, n=n):
                return act_ref[phase, pl.ds(base + n * CELLS, CELLS), :]

            def write_act(tap, window, n=n):
                act_cols[pl.ds(base + n * CELLS, CELLS), tap * GROUP : (tap + 1) * GROUP] = window

            fill_taps(taps, 1, read_act, write_act)
            flat = tuple((0, t[1], t[2]) for t in taps)

            def read_up(phase, n=n):
                return up_ref[pl.ds(base + n * CELLS, CELLS), :]

            def write_up(tap, window, n=n):
                at = place[tap] * GROUP
                up_cols[n * CELLS : (n + 1) * CELLS, at : at + GROUP] = window

            fill_taps(flat, -1, read_up, write_up)
        at = 0
        for phase in range(phases):
            size = sum(t[0] == phase for t in taps) * GROUP
            back = jnp.dot(
                up_cols[:, at : at + size], w_cols[at : at + size, :], preferred_element_type=f32
            )
            at += size
            pre = pre_ref[phase, pl.ds(base, rows), :]
            down_ref[phase, pl.ds(base, rows), :] = (gelu_prime(pre) * GAMMA * back).astype(bf16)
        return carry

    lax.fori_loop(0, up_ref.shape[0] // rows, step, 0)
    grad_ref[...] = lax.dot_general(
        up_ref[...], act_cols[...], (((0,), (0,)), ((), ())), preferred_element_type=f32
    ).astype(grad_ref.dtype)


def conv_backward(up, act, pre, weight, taps):
    phases, cells, channels = act.shape
    chunk = min(CHUNK, cells // CELLS)
    return pl.pallas_call(
        functools.partial(conv_back_kernel, taps, chunk),
        grid=(channels // GROUP,),
        out_shape=[
            jax.ShapeDtypeStruct((phases, cells, channels), bf16),
            jax.ShapeDtypeStruct((channels, 9 * GROUP), bf16),
        ],
        in_specs=[
            pl.BlockSpec((cells, GROUP), lambda g: (0, g)),
            pl.BlockSpec((phases, cells, GROUP), lambda g: (0, 0, g)),
            pl.BlockSpec((phases, cells, GROUP), lambda g: (0, 0, g)),
            pl.BlockSpec((GROUP, 9 * GROUP), lambda g: (g, 0)),
        ],
        out_specs=[
            pl.BlockSpec((phases, cells, GROUP), lambda g: (0, 0, g)),
            pl.BlockSpec((GROUP, 9 * GROUP), lambda g: (g, 0)),
        ],
        scratch_shapes=[
            pltpu.VMEM((9 * GROUP, GROUP), bf16),
            pltpu.VMEM((chunk * CELLS, 9 * GROUP), bf16),
            pltpu.VMEM((cells, 9 * GROUP), bf16),
        ],
        compiler_params=pltpu.CompilerParams(vmem_limit_bytes=48 * MIB),
        cost_estimate=pl.CostEstimate(
            flops=4 * cells * channels * 9 * GROUP,
            bytes_accessed=cells * channels * (2 + 8 * phases),
            transcendentals=cells * channels * phases,
        ),
        name="conv_backward",
    )(up, act, pre, weight)


def new_values(w, g, m, v, standard, clip):
    fan_in = w.shape[1]
    if standard:
        centre = w - jnp.mean(w, axis=-1, keepdims=True)
        spread = jnp.mean(centre * centre, axis=-1, keepdims=True)
        scale = lax.rsqrt(spread * fan_in + STD_EPS)
        along = jnp.sum(g * centre, axis=-1, keepdims=True)
        mean_g = jnp.mean(g, axis=-1, keepdims=True)
        g = scale * (g - mean_g) - (scale * scale * scale * along) * centre
    if clip:
        ceiling = CLIP * jnp.sqrt(jnp.sum(w * w, axis=-1, keepdims=True))
        norm = jnp.sqrt(jnp.sum(g * g, axis=-1, keepdims=True))
        g = g * (ceiling / jnp.maximum(norm, ceiling))
    m = DECAY_ONE * m + (1.0 - DECAY_ONE) * g
    v = DECAY_TWO * v + (1.0 - DECAY_TWO) * g * g
    root = v * lax.rsqrt(v) * (1.0 - DECAY_TWO**STEP_COUNT) ** -0.5 + ADAM_EPS
    step = (RATE / (1.0 - DECAY_ONE**STEP_COUNT)) * m * pl.reciprocal(root)
    return m, v, (1.0 - RATE * WEIGHT_DECAY) * w - step


def update_packed_kernel(shapes, share_ref, packed_ref, *refs):
    count = len(shapes)
    valid = pl.program_id(0) < share_ref[0]
    at = 0
    for k, shape in enumerate(shapes):
        part, width = shape[-2] // 6, shape[-1]
        for lead in leads(shape):
            g, at = read_packed(packed_ref, at, part, width)
            g = jnp.where(valid, g.astype(f32), 0.0)
            w, m, v = (refs[3 * k + i][lead] for i in range(3))
            for i, value in enumerate(new_values(w, g, m, v, True, True)):
                refs[3 * (count + k) + i][lead] = value


def update_packed(packed, members, share):
    specs, operands, shapes = [], [], []
    for weight, first, second in members:
        shape = weight.shape
        block = shape[:-2] + (shape[-2] // 6, shape[-1])
        zeros = (0,) * (len(shape) - 2)
        specs += [pl.BlockSpec(block, lambda j, zeros=zeros: zeros + (j, 0))] * 3
        operands += [weight, first, second]
        shapes.append(shape)
    total = sum(o.size for o in operands)
    outs = pl.pallas_call(
        functools.partial(update_packed_kernel, tuple(shapes)),
        grid=(6,),
        out_shape=[jax.ShapeDtypeStruct(o.shape, f32) for o in operands],
        in_specs=[
            pl.BlockSpec(memory_space=pltpu.SMEM),
            pl.BlockSpec((None,) + packed.shape[1:], lambda j: (j, 0, 0)),
        ]
        + specs,
        out_specs=specs,
        compiler_params=pltpu.CompilerParams(vmem_limit_bytes=58 * MIB),
        cost_estimate=pl.CostEstimate(
            flops=10 * total, bytes_accessed=9 * total, transcendentals=total // 3
        ),
        name="update_packed",
    )(share, packed, *operands)
    return [tuple(outs[3 * k : 3 * k + 3]) for k in range(len(members))]


def update_factors_kernel(unit, turned, block, share_ref, units_ref, inputs_ref, w_ref, m_ref, v_ref, m_out, v_out, w_out, g_all):
    step = pl.program_id(1)

    @pl.when(step == 0)
    def _():
        left, right = (inputs_ref, units_ref) if turned else (units_ref, inputs_ref)
        g_all[...] = lax.dot_general(
            left[...], right[...], (((0,), (0,)), ((), ())), preferred_element_type=f32
        )

    rows = pl.ds(pl.multiple_of(step * block, 8), block)
    shape = w_ref.shape
    index = lax.broadcasted_iota(jnp.int32, shape if turned else (block, 1), 1 if turned else 0)
    index += 0 if turned else step * block
    g = jnp.where(index < share_ref[0] * unit, g_all[rows, :], 0.0)
    m_out[...], v_out[...], w_out[...] = new_values(
        w_ref[...], g, m_ref[...], v_ref[...], False, not turned
    )


def update_factors(weight, units, gathered, columns, first, second, share, turned=False):
    count, rows, width = weight.shape
    images = units.shape[1]
    start, across, stride = columns
    block = 504 if turned else rows
    steps = -(-rows // block)
    spec = pl.BlockSpec((None, block, width), lambda k, i: (k, i, 0))
    owned = (width if turned else rows) // 6
    made = (across, width) if turned else (rows, across)
    return pl.pallas_call(
        functools.partial(update_factors_kernel, owned, turned, block),
        grid=(count, steps),
        out_shape=[jax.ShapeDtypeStruct(weight.shape, f32)] * 3,
        in_specs=[
            pl.BlockSpec(memory_space=pltpu.SMEM),
            pl.BlockSpec((None, images, units.shape[2]), lambda k, i: (k, 0, 0)),
            pl.BlockSpec((images, across), lambda k, i: (0, start + stride * k)),
        ]
        + [spec] * 3,
        out_specs=[spec] * 3,
        scratch_shapes=[pltpu.VMEM(made, f32)],
        compiler_params=pltpu.CompilerParams(vmem_limit_bytes=56 * MIB),
        cost_estimate=pl.CostEstimate(
            flops=count * rows * width * (2 * images + 15),
            bytes_accessed=24 * count * rows * width,
            transcendentals=count * rows * width,
        ),
        name="update_factors",
    )(share, units, gathered, weight, first, second)


def update_kernel(unit, standard, clip, block, share_ref, w_ref, g_ref, m_ref, v_ref, m_out, v_out, w_out):
    row = pl.program_id(0) * block + lax.broadcasted_iota(jnp.int32, (block, 1), 0)
    g = jnp.where(row % (6 * unit) < share_ref[0] * unit, g_ref[...].astype(f32), 0.0)
    m_out[...], v_out[...], w_out[...] = new_values(
        w_ref[...], g, m_ref[...], v_ref[...], standard, clip
    )


def update(weight, gradient, first, second, share, standard, clip):
    shape = weight.shape
    width = shape[-1]
    flat = [a.reshape(-1, width) for a in (weight, gradient, first, second)]
    rows = flat[0].shape[0]
    block = rows
    for size in range(192, 0, -16):
        if rows % size == 0:
            block = size
            break
    spec = pl.BlockSpec((block, width), lambda i: (i, 0))
    outs = pl.pallas_call(
        functools.partial(update_kernel, shape[-2] // 6, standard, clip, block),
        grid=(rows // block,),
        out_shape=[jax.ShapeDtypeStruct((rows, width), f32)] * 3,
        in_specs=[pl.BlockSpec(memory_space=pltpu.SMEM)] + [spec] * 4,
        out_specs=[spec] * 3,
        compiler_params=pltpu.CompilerParams(vmem_limit_bytes=48 * MIB),
        cost_estimate=pl.CostEstimate(
            flops=30 * rows * width, bytes_accessed=28 * rows * width, transcendentals=rows * width
        ),
        name="update",
    )(share, *flat)
    return tuple(o.reshape(shape) for o in outs)


def split_small(values, rows):
    values = jnp.pad(values, (0, -values.shape[0] % (128 * rows))).reshape(rows, -1)
    terms = []
    for _ in range(3):
        term = lax.reduce_precision(values, 8, 7)
        terms.append(term.astype(bf16))
        values = values - term
    return terms


def join_small(terms, rows):
    width = terms.shape[1] // 3
    total = jnp.sum(terms.astype(f32).reshape(-1, rows, 3 * width), axis=0)
    return (total[:, :width] + total[:, width : 2 * width] + total[:, 2 * width :]).reshape(-1)


def dot_t(left, right):
    return lax.dot_general(
        left, right, (((left.ndim - 1,), (1,)), ((), ())), preferred_element_type=f32
    )


def dot_n(left, right):
    return lax.dot_general(
        left, right, (((left.ndim - 1,), (0,)), ((), ())), preferred_element_type=f32
    )


def dot_sum(upstream, inputs):
    up = upstream.reshape(-1, upstream.shape[-1])
    low = inputs.reshape(-1, inputs.shape[-1])
    return lax.dot_general(up, low, (((0,), (0,)), ((), ())), preferred_element_type=f32)


def tail_forward(act_three, out_w, down_w, up_w):
    images = act_three.shape[0] // CELLS
    pre_four = dot_t(act_three, out_w).reshape(images, CELLS, -1)
    squeezed = (jnp.sum(pre_four, axis=1) / CELLS).astype(bf16)
    pre_down = dot_t(squeezed, down_w)
    act_down = gelu_act(pre_down).astype(bf16)
    gate_sig = jax.nn.sigmoid(dot_t(act_down, up_w))
    return pre_four, squeezed, pre_down, act_down, gate_sig


def tail_backward(grad_hidden, stored, down_w, up_w, gain):
    pre_four, squeezed, pre_down, act_down, gate_sig = stored
    gate = 2.0 * gate_sig
    raw_gate = jnp.sum(grad_hidden * pre_four, axis=1)
    gain_part = ALPHA * jnp.sum(raw_gate * gate)
    grad_gate = raw_gate * (ALPHA * gain)
    grad_up = (grad_gate * 2.0 * gate_sig * (1.0 - gate_sig)).astype(bf16)
    grad_down = (gelu_prime(pre_down) * dot_n(grad_up, up_w)).astype(bf16)
    grad_squeezed = dot_n(grad_down, down_w)
    grad_four = (
        grad_hidden * (ALPHA * gain * gate)[:, None, :] + (grad_squeezed / CELLS)[:, None, :]
    ).astype(bf16)
    factors = [grad_up, act_down, grad_down, squeezed]
    return grad_four.reshape(-1, grad_four.shape[-1]), factors, gain_part


def body(
    images,
    labels,
    class_counts,
    owner_share,
    w_entry,
    first_entry,
    second_entry,
    w_in,
    first_in,
    second_in,
    w_mid,
    first_mid,
    second_mid,
    w_out,
    first_out,
    second_out,
    se_down,
    first_down,
    second_down,
    se_up,
    first_up,
    second_up,
    w_final,
    first_final,
    second_final,
    head,
    first_head,
    second_head,
    small_params,
    first_small,
    second_small,
):
    owner, local, starts, slot_part = owner_tables(owner_share)
    me = lax.axis_index("dp")
    devices = lax.axis_size("dp")
    my_share = lax.dynamic_slice_in_dim(owner_share, me, 1, 0)
    my_start = lax.dynamic_index_in_dim(starts, me, 0, keepdims=False)

    rows_n, cols_n = lax.axis_size("ha"), lax.axis_size("wa")
    spread = rows_n * cols_n
    micro, per_dp, tile_h, tile_w, in_width = images.shape
    count = micro * per_dp // spread
    tiles = images.reshape(spread, count, tile_h, tile_w, in_width)
    tiles = lax.all_to_all(tiles, ("ha", "wa"), 0, 0, tiled=True)
    spot = lax.axis_index("ha") * cols_n + lax.axis_index("wa")
    my_labels = lax.dynamic_slice_in_dim(labels.reshape(-1), spot * count, count, 0)

    def block_entries(layer):
        return [
            (w_mid, (layer, 0), True),
            (w_mid, (layer, 1), True),
            (w_out, (layer,), True),
            (se_down, (layer,), False),
            (se_up, (layer,), False),
        ]

    groups = [
        [(w_entry, (), True)],
        block_entries(0),
        [(w_in, (0,), True)] + block_entries(1),
        [(w_final, (), True)],
        [(head, (), False)],
    ]
    staged = known_mesh()
    if staged:
        tables = {flag: source_tables(owner, local, flag) for flag in (True, False)}
        moves = [Gather(groups[0], True), Gather(groups[1])]
        moves[0].along_x()
        moves[1].along_x(moves[0].near)
        moves[0].cores()
        for entries in groups[2:]:
            entries[0] = (after(entries[0][0], moves[0].near),) + entries[0][1:]
            moves.append(Gather(entries))
        moves[1].near = after(moves[1].near, *[m.own for m in moves[2:]])
        moves[1].along_y()
        moves[2].along_x(moves[1].near)
    cells = count * CELLS
    if staged:
        act_zero, pooled = prepare(tiles, rows_n, cols_n)
    else:
        pixels = tiles.reshape(
            rows_n, cols_n, count, tile_h // 2, 2, tile_w // 2, 2, in_width
        ).transpose(4, 6, 2, 0, 3, 1, 5, 7).reshape(4, cells, in_width)
        act_zero = (gelu_act(pixels.astype(f32)) * GAMMA).astype(bf16)
        pooled = (jnp.sum(act_zero.astype(f32), axis=0) * 0.25).astype(bf16)

    def hold(value, *arrivals):
        if not staged:
            return value
        kept = [getattr(moves[k], name) for k, name in arrivals]
        value, *kept = lax.optimization_barrier((value, *kept))
        for (k, name), buffer in zip(arrivals, kept):
            setattr(moves[k], name, buffer)
        return value

    def weights_of(group):
        if staged:
            return moves[group].unpacked(tables)
        return gather_plain(groups[group], owner, local)

    gains = small_params[:LAYERS]
    head_bias = small_params[LAYERS:]
    images_all = micro * per_dp * lax.axis_size("dp")
    class_weight = 1.0 / class_counts.astype(f32)

    kept = []
    weights = []
    hidden = None
    for layer in range(LAYERS):
        if layer:
            scale = GAMMA * (1.0 + layer * ALPHA * ALPHA) ** (-0.5)
            act_zero = (gelu_act(hidden) * scale).astype(bf16).reshape(1, cells, -1)
        taps = TAPS_TWO if layer == 0 else TAPS_ONE
        if layer == 0:
            (entry_low,) = weights_of(0)
            in_low, skip_low = entry_low[:NECK], entry_low[NECK:]
        else:
            in_low, *others = weights_of(1 + layer)
        pre_one = dot_t(act_zero, in_low)
        act_one = (gelu_act(pre_one) * GAMMA).astype(bf16)
        if layer == 0:
            act_one = hold(act_one, (1, "far"), (2, "near"))
            if staged:
                moves[1].cores()
                moves[2].along_y()
                moves[3].along_x(moves[2].near)
            others = weights_of(1)
        mid_a, mid_b, out_low, down_low, up_low = others
        weights.append((in_low, mid_a, mid_b, out_low, down_low, up_low))
        pre_two, act_two = conv_forward(act_one, mid_a, taps)
        if layer == 1:
            act_two = hold(act_two, (4, "near"))
            if staged:
                moves[4].along_y()
        pre_three, act_three = conv_forward(act_two[None], mid_b, TAPS_ONE)
        if layer == 1:
            act_three = hold(act_three, (3, "far"))
            if staged:
                moves[3].cores()
        tail = tail_forward(act_three, out_low, down_low, up_low)
        branch = (ALPHA * gains[layer]) * tail[0] * (2.0 * tail[4])[:, None, :]
        if layer == 0:
            shortcut = dot_t(pooled, skip_low).reshape(branch.shape)
        else:
            shortcut = hidden.reshape(branch.shape)
        before = hidden
        hidden = (shortcut + branch).reshape(cells, -1)
        if layer == 0:
            hidden = hold(hidden, (2, "far"), (3, "near"))
            if staged:
                moves[2].cores()
                moves[3].along_y()
                moves[4].along_x(moves[3].near)
        kept.append((before, act_zero, pre_one, act_one, pre_two, act_two, pre_three, act_three, tail, pooled))
    (final_low,) = weights_of(3)
    hidden_low = hold(hidden.astype(bf16), (4, "far"))
    if staged:
        moves[4].cores()
    pre_final = dot_t(hidden_low, final_low).reshape(count, CELLS, -1)
    pooled_final = (jnp.sum(gelu_act(pre_final) * GAMMA, axis=1) / CELLS).astype(bf16)
    (head_low,) = weights_of(4)
    logits = dot_n(pooled_final, head_low) + head_bias
    largest = jnp.max(logits, axis=1, keepdims=True)
    log_total = largest[:, 0] + jnp.log(jnp.sum(jnp.exp(logits - largest), axis=1))
    one_hot = (my_labels[:, None] == jnp.arange(logits.shape[1])[None, :]).astype(f32)
    picked = jnp.sum(one_hot * logits, axis=1)
    image_weight = jnp.sum(one_hot * class_weight[None, :], axis=1)
    loss_part = jnp.sum(image_weight * (log_total - picked))
    softmax_p = jnp.exp(logits - log_total[:, None])
    grad_logits = image_weight[:, None] * (softmax_p - one_hot) / images_all
    bias_part = jnp.sum(grad_logits, axis=0)
    grad_low = grad_logits.astype(bf16)
    grad_pooled = dot_t(grad_low, head_low) * (GAMMA / CELLS)
    grad_final = (gelu_prime(pre_final) * grad_pooled[:, None, :]).astype(bf16).reshape(cells, -1)
    final_grad = dot_sum(grad_final, hidden_low).astype(bf16)
    grad_hidden = dot_n(grad_final, final_low)
    if staged:
        packed = pack_gradients([final_grad], slot_part, devices, 16)
        packed, grad_hidden = lax.optimization_barrier((packed, grad_hidden))
        final_part = lax.psum_scatter(
            packed.reshape(devices, -1, 128), "dp", scatter_dimension=0, tiled=False
        )
        final_sum = lax.psum(final_part, ("ha", "wa")).reshape(6, -1, 128)

    in_grads = [None] * LAYERS
    mid_grads = [None] * LAYERS
    out_grads = [None] * LAYERS
    all_factors = [pooled_final, grad_low]
    gain_parts = [None] * LAYERS
    for layer in reversed(range(LAYERS)):
        before, act_zero, pre_one, act_one, pre_two, act_two, pre_three, act_three, tail, pooled = kept[layer]
        in_low, mid_a, mid_b, out_low, down_low, up_low = weights[layer]
        taps = TAPS_TWO if layer == 0 else TAPS_ONE
        grad_four, factors, gain_parts[layer] = tail_backward(
            grad_hidden.reshape(count, CELLS, -1), tail, down_low, up_low, gains[layer]
        )
        all_factors = factors + all_factors
        if layer == 0:
            small = jnp.concatenate([loss_part[None], jnp.stack(gain_parts), bias_part])
            all_factors = jnp.concatenate(all_factors + split_small(small, count), axis=1)
            all_factors, grad_four = lax.optimization_barrier((all_factors, grad_four))
            gathered = lax.all_gather(all_factors, EVERY, axis=0, tiled=True)
        out_grads[layer] = dot_sum(grad_four, act_three).astype(bf16)
        grad_three = (gelu_prime(pre_three) * GAMMA * dot_n(grad_four, out_low)).astype(bf16)
        grad_two, mid_grad_b = conv_backward(grad_three, act_two[None], pre_two[None], mid_b, TAPS_ONE)
        grad_one, mid_grad_a = conv_backward(grad_two[0], act_one, pre_one, mid_a, taps)
        mid_grads[layer] = (mid_grad_a, mid_grad_b)
        in_grad = dot_sum(grad_one, act_zero).astype(bf16)
        if layer == 0:
            skip_grad = dot_sum(grad_hidden.astype(bf16), pooled).astype(bf16)
            in_grads[layer] = jnp.concatenate([in_grad, skip_grad], axis=0)
        else:
            in_grads[layer] = in_grad
            scale = GAMMA * (1.0 + layer * ALPHA * ALPHA) ** (-0.5)
            grad_zero = dot_n(grad_one[0], in_low)
            grad_hidden = grad_hidden + gelu_prime(before) * scale * grad_zero

    def own_units(span):
        part = span[1] // starts.shape[0] // 4
        return lax.dynamic_slice_in_dim(gathered, span[0] + my_start * part, 6 * part, 1)

    wide, narrow, final_width = tail[0].shape[-1], tail[3].shape[-1], pooled_final.shape[1]
    spans = []
    at = 0
    for width in [wide, narrow, narrow, wide] * LAYERS + [final_width, logits.shape[1]]:
        spans.append((at, width))
        at += width

    small = join_small(gathered[:, at:], count)
    loss_sum = small[0]
    small_grad = small[1 : 1 + small_params.shape[0]]

    flat_mids = [g for pair in mid_grads for g in pair]
    local_grads = in_grads + out_grads + flat_mids
    members = (
        (w_entry, first_entry, second_entry),
        (w_in, first_in, second_in),
        (w_out, first_out, second_out),
        (w_mid, first_mid, second_mid),
        (w_final, first_final, second_final),
    )
    if staged:
        packed = pack_gradients(local_grads, slot_part, devices, SPAN)
        packed = after(packed, final_part)
        new = update_packed(sum_at_owners(packed), members[:-1], my_share)
        new += update_packed(final_sum, members[-1:], my_share)
    else:
        sums = [sum_plain(g, slot_part) for g in local_grads + [final_grad]]
        new = []
        for weight, first, second in members:
            count = len(leads(weight.shape))
            total, sums = jnp.stack(sums[:count]), sums[count:]
            new.append(update(weight, total, first, second, my_share, True, True))
    entry_new, in_new, out_new, mid_new, final_new = new
    def owned(first_span):
        return jnp.stack([own_units(spans[4 * k + first_span]) for k in range(LAYERS)])

    def blocks(first_span):
        (at, across), (then, _) = spans[first_span], spans[4 + first_span]
        return at // across, across, (then - at) // across

    up_new = update_factors(
        se_up, owned(0), gathered, blocks(1), first_up, second_up, my_share
    )
    down_new = update_factors(
        se_down, owned(2), gathered, blocks(3), first_down, second_down, my_share
    )
    head_new = update_factors(
        head.T[None],
        own_units(spans[-2])[None],
        gathered,
        (spans[-1][0] // 1024, 1024, 0),
        first_head.T[None],
        second_head.T[None],
        my_share,
        turned=True,
    )
    head_new = [a[0].T for a in head_new]
    results = [loss_sum]
    for new in (entry_new, in_new, mid_new, out_new, down_new, up_new, final_new, head_new):
        results.extend(new)
    m = DECAY_ONE * first_small + (1.0 - DECAY_ONE) * small_grad
    v = DECAY_TWO * second_small + (1.0 - DECAY_TWO) * small_grad * small_grad
    m_hat = m / (1.0 - DECAY_ONE**STEP_COUNT)
    v_hat = v / (1.0 - DECAY_TWO**STEP_COUNT)
    results.extend(
        [
            m,
            v,
            small_params
            - SMALL_RATE * (m_hat / (jnp.sqrt(v_hat) + ADAM_EPS) + WEIGHT_DECAY * small_params),
        ]
    )
    return tuple(results)


def solution(mesh):
    owned = (
        [P("dp", None)] * 3
        + [P(None, "dp", None)] * 3
        + [P(None, None, "dp", None)] * 3
        + [P(None, "dp", None)] * 9
        + [P("dp", None)] * 6
        + [P()] * 3
    )
    return jax.shard_map(
        body,
        mesh=mesh,
        in_specs=tuple([P(None, "dp", "ha", "wa", None), P(None, "dp"), P(), P()] + owned),
        out_specs=tuple([P()] + owned),
        check_vma=False,
    )
```

```python
import functools

import jax
import jax.numpy as jnp
from jax import lax
from jax.experimental import pallas as pl
from jax.experimental.pallas import tpu as pltpu
from jax.sharding import PartitionSpec as P

NECK = 768
GROUP = 128
HEIGHT = 8
BREADTH = 8
CELLS = HEIGHT * BREADTH
LAYERS = 2
STEP_COUNT = 5

GAMMA = 1.7015043497085571
ALPHA = 0.2
CLIP = 0.01
RATE = 0.05
SMALL_RATE = 0.5
DECAY_ONE = 0.9
DECAY_TWO = 0.999
ADAM_EPS = 1e-08
WEIGHT_DECAY = 5e-05
STD_EPS = 0.0001
GELU_SCALE = 0.7978845608028654
GELU_CUBE = 0.044715
EVERY = ("dp", "ha", "wa")
MIB = 1 << 20

TAPS_ONE = tuple((0, t // 3 - 1, t % 3 - 1) for t in range(9))
TAPS_TWO = tuple(((t // 3 % 2) * 2 + t % 3 % 2, t // 3 // 2, t % 3 // 2) for t in range(9))

CHUNK = 16

f32 = jnp.float32
bf16 = jnp.bfloat16


def gelu_act(v):
    half = 0.5 * v
    return half + half * jnp.tanh(v * (GELU_SCALE + (GELU_SCALE * GELU_CUBE) * (v * v)))


def gelu_prime(v):
    cube = (GELU_SCALE * GELU_CUBE) * (v * v)
    th = jnp.tanh(v * (GELU_SCALE + cube))
    return 0.5 + 0.5 * (th + v * (1.0 - th * th) * (GELU_SCALE + 3.0 * cube))


def standardize(weight):
    fan_in = weight.shape[-1]
    centre = weight - jnp.mean(weight, axis=-1, keepdims=True)
    spread = jnp.mean(centre * centre, axis=-1, keepdims=True)
    return centre * lax.rsqrt(spread * fan_in + STD_EPS)


def owner_tables(shares):
    devices = shares.shape[0]
    ids = jnp.arange(devices, dtype=jnp.int32)
    starts = jnp.sum(jnp.where(ids[None, :] < ids[:, None], shares[None, :], 0), axis=1)
    part_ids = jnp.arange(4 * devices, dtype=jnp.int32)
    owner = jnp.sum((part_ids[:, None] >= (starts + shares)[None, :]).astype(jnp.int32), axis=1)
    first = jnp.sum(jnp.where(owner[:, None] == ids[None, :], starts[None, :], 0), axis=1)
    local = (part_ids - first).astype(jnp.int32)
    held = jnp.minimum(jnp.arange(6, dtype=jnp.int32)[None, :], shares[:, None] - 1)
    slot_part = (starts[:, None] + held).reshape(-1).astype(jnp.int32)
    return owner, local, starts, (slot_part, (ids[:, None] * 6 + held).reshape(-1))


def known_mesh():
    return tuple(lax.axis_size(a) for a in EVERY) == (4, 4, 2)


def unit_slots(owner, local, part):
    return ((owner * 6 + local)[:, None] * part + jnp.arange(part)[None, :]).reshape(-1)


def gather_plain(entries, owner, local):
    full = []
    for array, lead, standard in entries:
        block = standardize(array[lead]) if standard else array[lead]
        every = lax.all_gather(block.astype(bf16), "dp", axis=0, tiled=True)
        full.append(jnp.take(every, unit_slots(owner, local, block.shape[0] // 6), axis=0))
    return full


def sum_plain(gradient, slot_part):
    part = gradient.shape[0] // (4 * lax.axis_size("dp"))
    units = (slot_part[:, None] * part + jnp.arange(part)[None, :]).reshape(-1)
    slots = jnp.take(gradient, units, axis=0)
    owned = lax.psum_scatter(slots, "dp", scatter_dimension=0, tiled=True)
    return lax.psum(owned, ("ha", "wa"))


def leads(shape):
    tuples = [()]
    for size in shape[:-2]:
        tuples = [t + (i,) for t in tuples for i in range(size)]
    return tuples


def packed_rows(part, width):
    return part * (-(-width // 128))


def pack_into(ref, at, block):
    part, width = block.shape
    for column in range(0, width, 128):
        lanes = min(128, width - column)
        piece = block[:, column : column + lanes]
        if lanes < 128:
            piece = jnp.concatenate([piece, jnp.zeros((part, 128 - lanes), piece.dtype)], axis=1)
        ref[at : at + part, :] = piece
        at += part
    return at


def read_packed(ref, at, part, width):
    pieces = []
    for column in range(0, width, 128):
        pieces.append(ref[at : at + part, : min(128, width - column)])
        at += part
    return (pieces[0] if len(pieces) == 1 else jnp.concatenate(pieces, axis=1)), at


def pack_weights_kernel(standard, *refs):
    out_ref = refs[-1]
    at = 0
    for ref, flag in zip(refs[:-1], standard):
        block = ref[...]
        at = pack_into(out_ref, at, (standardize(block) if flag else block).astype(bf16))


def pack_weights(entries):
    specs, rows = [], 0
    for array, lead, _ in entries:
        part, width = array.shape[-2] // 6, array.shape[-1]
        specs.append(
            pl.BlockSpec((None,) * len(lead) + (part, width), lambda j, lead=lead: lead + (j, 0))
        )
        rows += packed_rows(part, width)
    return pl.pallas_call(
        functools.partial(pack_weights_kernel, tuple(e[2] for e in entries)),
        grid=(6,),
        out_shape=jax.ShapeDtypeStruct((6, rows, 128), bf16),
        in_specs=specs,
        out_specs=pl.BlockSpec((None, rows, 128), lambda j: (j, 0, 0)),
        compiler_params=pltpu.CompilerParams(vmem_limit_bytes=40 * MIB),
        cost_estimate=pl.CostEstimate(
            flops=6 * rows * 128 * 8, bytes_accessed=6 * rows * 128 * 6, transcendentals=0
        ),
        name="pack_weights",
    )(*[e[0] for e in entries])


def unpack_kernel(count, shapes, which_ref, place_ref, *refs):
    sources = refs[:count]
    outs = refs[count : count + len(shapes)]
    held, *rest = refs[count + len(shapes) :]
    stages, (arrived, left) = rest[: len(shapes)], rest[len(shapes) :]
    parts = which_ref.shape[0]

    def fetch(i, carry):
        for s, source in enumerate(sources):

            @pl.when(which_ref[i] == s)
            def _(source=source):
                pltpu.make_async_copy(source.at[place_ref[i]], held.at[i], arrived.at[i]).start()

        return carry

    def spread(group, carry):
        for j in range(4):
            i = group * 4 + j
            pltpu.make_async_copy(held.at[i], held.at[i], arrived.at[i]).wait()
            at = 0
            for k, (part, width) in enumerate(shapes):
                block, at = read_packed(held.at[i], at, part, width)
                stages[k][pl.ds(pl.multiple_of(i * part, part), part), :] = block
        for k, (part, width) in enumerate(shapes):
            rows = pl.ds(pl.multiple_of(group * 4 * part, part), 4 * part)
            pltpu.make_async_copy(stages[k].at[rows, :], outs[k].at[rows, :], left.at[k]).start()
        return carry

    lax.fori_loop(0, parts, fetch, 0)
    lax.fori_loop(0, parts // 4, spread, 0)
    for k in range(len(shapes)):
        pltpu.make_async_copy(stages[k], outs[k], left.at[k]).wait()


def unpack_weights(sources, which, place, shapes):
    count, parts = len(sources), which.shape[0]
    rows = sources[0].shape[1]
    full = [(parts * p, w) for p, w in shapes]
    return pl.pallas_call(
        functools.partial(unpack_kernel, count, shapes),
        out_shape=[jax.ShapeDtypeStruct(f, bf16) for f in full],
        in_specs=[pl.BlockSpec(memory_space=pltpu.SMEM)] * 2
        + [pl.BlockSpec(memory_space=pl.ANY)] * count,
        out_specs=[pl.BlockSpec(memory_space=pl.ANY)] * len(shapes),
        scratch_shapes=[pltpu.VMEM((parts, rows, 128), bf16)]
        + [pltpu.VMEM(f, bf16) for f in full]
        + [pltpu.SemaphoreType.DMA((parts,)), pltpu.SemaphoreType.DMA((len(shapes),))],
        compiler_params=pltpu.CompilerParams(vmem_limit_bytes=40 * MIB),
        cost_estimate=pl.CostEstimate(
            flops=0, bytes_accessed=parts * rows * 128 * 4, transcendentals=0
        ),
        name="unpack_weights",
    )(which, place, *sources)


def after(value, *others):
    return lax.optimization_barrier((value,) + others)[0]


CHIP = [(i, i ^ 2) for i in range(4)]
CORE = [(i, i ^ 1) for i in range(4)]


class Gather:
    def __init__(self, entries, whole=False):
        self.shapes = tuple((e[0].shape[-2] // 6, e[0].shape[-1]) for e in entries)
        self.own = pack_weights(entries)
        self.whole = whole

    def along_x(self, *others):
        mine = self.own
        if not self.whole:
            mine = lax.dynamic_slice_in_dim(mine, lax.axis_index("wa") * 3, 3, 0)
        self.near = lax.ppermute(after(mine, *others), "dp", CHIP)

    def along_y(self):
        self.far = lax.ppermute(self.near, "wa", [(0, 1), (1, 0)])

    def cores(self):
        buffers = [self.own, self.near] + ([] if self.whole else [self.far])
        self.buffers = buffers + [lax.ppermute(b, "dp", CORE) for b in buffers]

    def unpacked(self, tables):
        return unpack_weights(self.buffers, *tables[self.whole], self.shapes)


def source_tables(owner, local, whole):
    me = lax.axis_index("dp")
    side = lax.axis_index("wa")
    away = owner // 2 != me // 2
    if whole:
        which, at, count = away.astype(jnp.int32), local, 2
    else:
        which = jnp.where(away, jnp.where(local // 3 == side, 1, 2), 0)
        at, count = jnp.where(away, local % 3, local), 3
    which = (which + count * (owner % 2 != me % 2)).astype(jnp.int32)
    return which, at.astype(jnp.int32)


def pack_gradients_kernel(pad, part_ref, slot_ref, *refs):
    out_ref = refs[-1]
    at = 0
    for ref in refs[:-1]:
        at = pack_into(out_ref, at, ref[...].astype(bf16))
    if pad:
        out_ref[at : at + pad, :] = jnp.zeros((pad, 128), bf16)


def pack_gradients(gradients, slot_part, devices, unit):
    specs, rows = [], 0
    for gradient in gradients:
        part, width = gradient.shape[0] // (4 * devices), gradient.shape[1]
        specs.append(pl.BlockSpec((part, width), lambda s, parts, held: (parts[s], 0)))
        rows += packed_rows(part, width)
    pad = -rows % unit
    rows += pad
    slots = 6 * devices
    return pl.pallas_call(
        functools.partial(pack_gradients_kernel, pad),
        grid_spec=pltpu.PrefetchScalarGridSpec(
            num_scalar_prefetch=2,
            grid=(slots,),
            in_specs=specs,
            out_specs=pl.BlockSpec((None, rows, 128), lambda s, parts, held: (held[s], 0, 0)),
        ),
        out_shape=jax.ShapeDtypeStruct((slots, rows, 128), bf16),
        compiler_params=pltpu.CompilerParams(vmem_limit_bytes=40 * MIB),
        cost_estimate=pl.CostEstimate(
            flops=0, bytes_accessed=slots * rows * 128 * 4, transcendentals=0
        ),
        name="pack_gradients",
    )(*slot_part, *gradients)


SPAN = 1024
AXES = ("x", "y", "near", "far")
ORDERS = (AXES,)
LAGS = (0, 1, 2, 3, 4, 5, 6, 7)


def sum_kernel(orders, spans, packed, owned, own, core, one, two, three, four, sends, recvs, local_sems):
    dp, z, y = lax.axis_index("dp"), lax.axis_index("ha"), lax.axis_index("wa")
    bit = {"x": dp // 2, "core": dp % 2, "y": y, "near": z % 2, "far": z // 2}
    peer = {
        "x": {"dp": (dp + 2) % 4},
        "core": {"dp": dp + 1 - 2 * (dp % 2)},
        "y": {"wa": 1 - y},
        "near": {"ha": z + 1 - 2 * (z % 2)},
        "far": {"ha": (z + 2) % 4},
    }
    barrier = pltpu.get_barrier_semaphore()
    for other in peer.values():
        pl.semaphore_signal(barrier, inc=1, device_id=other, device_id_type=pl.DeviceIdType.MESH)
    pl.semaphore_wait(barrier, len(peer))

    buffers = [core, one, two, three, four]
    kinds = len(orders)

    def index(ref, chunk, names, fixed):
        return ref.at[(chunk,) + tuple(fixed[n] if n in fixed else slice(None) for n in names)]

    def remote(src, dst, stage, chunk, to):
        return pltpu.make_async_remote_copy(
            src_ref=src,
            dst_ref=dst,
            send_sem=sends.at[stage, chunk],
            recv_sem=recvs.at[stage, chunk],
            device_id=peer[to],
            device_id_type=pl.DeviceIdType.MESH,
        )

    def copy_of(stage, kind, chunk):
        order = orders[kind]
        if stage == 0:
            return remote(packed.at[:, 1 - bit["core"], chunk], core.at[chunk], 0, chunk, "core")
        if stage <= 4:
            before = [n for n in AXES if n not in order[: stage - 1]]
            axis = order[stage - 1]
            src = index(buffers[stage - 1], chunk, before, {axis: 1 - bit[axis]})
            return remote(src, buffers[stage].at[chunk], stage, chunk, axis)
        spread = [n for n in reversed(order) if n != "x"]
        axis = spread[stage - 5]
        fixed = {n: bit[n] for n in spread[stage - 5 :]}
        place = index(owned, chunk, AXES[1:], fixed)
        return remote(four.at[chunk] if stage == 5 else place, place, stage, chunk, axis)

    def load(chunk):
        slot = chunk % 2
        return pltpu.make_async_copy(
            packed.at[:, bit["core"], chunk], own.at[slot], local_sems.at[slot]
        )

    def store(chunk):
        place = owned.at[chunk, bit["y"], bit["near"], bit["far"]]
        return pltpu.make_async_copy(four.at[chunk], place, local_sems.at[2 + chunk])

    def add(target, names, other, prefix=()):
        for at in names:
            there = target[at].astype(f32) + other(at).astype(f32)
            target[at] = there.astype(bf16)

    def grid(count):
        return leads((2,) * count + (1, 1))

    def arrive(stage, kind, chunk):
        copy_of(stage, kind, chunk).wait_recv()
        order = orders[kind]
        if stage == 0:
            load(chunk).wait()
            add(core, [(chunk,) + t for t in grid(4)], lambda at: own[(chunk % 2,) + at[1:]])
        elif stage <= 4:
            before = [n for n in AXES if n not in order[: stage - 1]]
            axis = order[stage - 1]
            where = before.index(axis)

            def mine(at):
                rest = at[1:]
                return buffers[stage - 1][(chunk,) + rest[:where] + (bit[axis],) + rest[where:]]

            add(buffers[stage], [(chunk,) + t for t in grid(4 - stage)], mine)
            if stage == 4:
                store(chunk).start()
        if stage == 5:
            store(chunk).wait()

    ahead, last = 3, 7
    for chunk in range(ahead):
        copy_of(0, chunk % kinds, chunk).start()
    load(0).start()

    def step(s, q):
        @pl.when(s + ahead < spans)
        def _():
            copy_of(0, (q + ahead) % kinds, s + ahead).start()

        @pl.when(s + 1 < spans)
        def _():
            load(s + 1).start()

        for stage in range(last + 1):
            chunk = s - LAGS[stage]
            kind = (q - LAGS[stage]) % kinds

            @pl.when((chunk >= 0) & (chunk < spans))
            def _(stage=stage, chunk=chunk, kind=kind):
                arrive(stage, kind, chunk)
                if stage < last:
                    copy_of(stage + 1, kind, chunk).start()

    def steps(i, carry):
        for q in range(kinds):
            step(i * kinds + q, q)
        return carry

    lax.fori_loop(0, -(-(spans + LAGS[-1]) // kinds), steps, 0)

    def sent(i, carry):
        for q in range(kinds):
            for stage in range(last + 1):
                copy_of(stage, q, i * kinds + q).wait_send()
        return carry

    lax.fori_loop(0, spans // kinds, sent, 0)


def sum_at_owners(packed):
    slots, rows, lanes = packed.shape
    spans = 6 * rows // SPAN
    r = SPAN // 8
    orders = ORDERS
    owned = pl.pallas_call(
        functools.partial(sum_kernel, orders, spans),
        out_shape=jax.ShapeDtypeStruct((spans, 2, 2, 2, r, 128), bf16),
        in_specs=[pl.BlockSpec(memory_space=pl.ANY)],
        out_specs=pl.BlockSpec(memory_space=pl.ANY),
        scratch_shapes=[
            pltpu.VMEM((2, 2, 2, 2, 2, r, 128), bf16),
            pltpu.VMEM((spans, 2, 2, 2, 2, r, 128), bf16),
            pltpu.VMEM((spans, 2, 2, 2, r, 128), bf16),
            pltpu.VMEM((spans, 2, 2, r, 128), bf16),
            pltpu.VMEM((spans, 2, r, 128), bf16),
            pltpu.VMEM((spans, r, 128), bf16),
            pltpu.SemaphoreType.DMA((8, spans)),
            pltpu.SemaphoreType.DMA((8, spans)),
            pltpu.SemaphoreType.DMA((2 + spans,)),
        ],
        compiler_params=pltpu.CompilerParams(
            collective_id=1, has_side_effects=True, vmem_limit_bytes=56 * MIB
        ),
        cost_estimate=pl.CostEstimate(
            flops=slots * rows * 128, bytes_accessed=slots * rows * 128 * 4, transcendentals=0
        ),
        name="sum_at_owners",
    )(packed.reshape(2, 2, spans, 2, 2, 2, r, 128))
    return owned.reshape(6, rows, lanes)


def prepare_kernel(tiles_ref, place_ref, act_ref, pooled_ref):
    sources, tile_h, tile_w, width = tiles_ref.shape
    pixels = tiles_ref[...].astype(f32).reshape(sources * tile_h * tile_w, width).astype(bf16)
    image = jnp.dot(place_ref[...], pixels, preferred_element_type=f32)
    act = (gelu_act(image) * GAMMA).astype(bf16).reshape(4, CELLS, width)
    act_ref[...] = act
    total = act[0].astype(f32) + act[1].astype(f32) + act[2].astype(f32) + act[3].astype(f32)
    pooled_ref[...] = (total * 0.25).astype(bf16)


def prepare(tiles, rows_n, cols_n):
    sources, count, tile_h, tile_w, width = tiles.shape
    pixels = 4 * CELLS
    down = jnp.arange(sources)[:, None, None] // cols_n * tile_h + jnp.arange(tile_h)[None, :, None]
    along = jnp.arange(sources)[:, None, None] % cols_n * tile_w + jnp.arange(tile_w)[None, None, :]
    target = ((down % 2 * 2 + along % 2) * HEIGHT + down // 2) * BREADTH + along // 2
    place = (jnp.arange(pixels)[:, None] == target.reshape(1, pixels)).astype(bf16)
    return pl.pallas_call(
        prepare_kernel,
        grid=(count,),
        out_shape=[
            jax.ShapeDtypeStruct((4, count * CELLS, width), bf16),
            jax.ShapeDtypeStruct((count * CELLS, width), bf16),
        ],
        in_specs=[
            pl.BlockSpec((sources, None, tile_h, tile_w, width), lambda n: (0, n, 0, 0, 0)),
            pl.BlockSpec((pixels, pixels), lambda n: (0, 0)),
        ],
        out_specs=[
            pl.BlockSpec((4, CELLS, width), lambda n: (0, n, 0)),
            pl.BlockSpec((CELLS, width), lambda n: (n, 0)),
        ],
        compiler_params=pltpu.CompilerParams(vmem_limit_bytes=32 * MIB),
        cost_estimate=pl.CostEstimate(
            flops=2 * count * pixels * pixels * width,
            bytes_accessed=5 * count * pixels * width,
            transcendentals=count * pixels * width,
        ),
        name="prepare",
    )(tiles, place)


def moved(image, down, right):
    if right:
        column = lax.broadcasted_iota(jnp.int32, image.shape, 1) + right
        image = pltpu.roll(image, (-right) % BREADTH, 1)
        image = jnp.where((column >= 0) & (column < BREADTH), image, 0.0)
    if down:
        edge = jnp.zeros((abs(down),) + image.shape[1:], image.dtype)
        if down > 0:
            image = jnp.concatenate([image[down:], edge], axis=0)
        else:
            image = jnp.concatenate([edge, image[:down]], axis=0)
    return image


def fill_taps(taps, sign, read, write):
    for phase in sorted({t[0] for t in taps}):
        image = read(phase).astype(f32).reshape(HEIGHT, BREADTH, GROUP)
        for right in sorted({t[2] for t in taps if t[0] == phase}):
            shifted = moved(image, 0, sign * right)
            for tap, (own, down, own_right) in enumerate(taps):
                if own == phase and own_right == right:
                    window = moved(shifted, sign * down, 0)
                    write(tap, window.reshape(CELLS, GROUP).astype(bf16))


def conv_kernel(taps, chunk, act_ref, w_ref, pre_ref, out_ref, cols):
    rows = chunk * CELLS

    def step(i, carry):
        base = pl.multiple_of(i * rows, rows)
        for n in range(chunk):

            def read(phase, n=n):
                return act_ref[phase, pl.ds(base + n * CELLS, CELLS), :]

            def write(tap, window, n=n):
                cols[n * CELLS : (n + 1) * CELLS, tap * GROUP : (tap + 1) * GROUP] = window

            fill_taps(taps, 1, read, write)
        pre = lax.dot_general(
            cols[...], w_ref[...], (((1,), (1,)), ((), ())), preferred_element_type=f32
        )
        pre_ref[pl.ds(base, rows), :] = pre.astype(bf16)
        out_ref[pl.ds(base, rows), :] = (gelu_act(pre) * GAMMA).astype(bf16)
        return carry

    lax.fori_loop(0, pre_ref.shape[0] // rows, step, 0)


def conv_forward(act, weight, taps):
    phases, cells, channels = act.shape
    chunk = min(CHUNK, cells // CELLS)
    return pl.pallas_call(
        functools.partial(conv_kernel, taps, chunk),
        grid=(channels // GROUP,),
        out_shape=[
            jax.ShapeDtypeStruct((cells, channels), bf16),
            jax.ShapeDtypeStruct((cells, channels), bf16),
        ],
        in_specs=[
            pl.BlockSpec((phases, cells, GROUP), lambda g: (0, 0, g)),
            pl.BlockSpec((GROUP, 9 * GROUP), lambda g: (g, 0)),
        ],
        out_specs=[
            pl.BlockSpec((cells, GROUP), lambda g: (0, g)),
            pl.BlockSpec((cells, GROUP), lambda g: (0, g)),
        ],
        scratch_shapes=[pltpu.VMEM((chunk * CELLS, 9 * GROUP), bf16)],
        compiler_params=pltpu.CompilerParams(vmem_limit_bytes=32 * MIB),
        cost_estimate=pl.CostEstimate(
            flops=2 * cells * channels * 9 * GROUP,
            bytes_accessed=cells * channels * (6 + 2 * phases),
            transcendentals=cells * channels,
        ),
        name="conv_forward",
    )(act, weight)


def conv_back_kernel(taps, chunk, up_ref, act_ref, pre_ref, w_ref, down_ref, grad_ref, w_cols, up_cols, act_cols):
    rows = chunk * CELLS
    phases = act_ref.shape[0]
    order = [t for q in range(phases) for t in range(9) if taps[t][0] == q]
    place = {t: i for i, t in enumerate(order)}
    for t in range(9):
        w_cols[place[t] * GROUP : (place[t] + 1) * GROUP, :] = w_ref[:, t * GROUP : (t + 1) * GROUP]

    def step(i, carry):
        base = pl.multiple_of(i * rows, rows)
        for n in range(chunk):

            def read_act(phase, n=n):
                return act_ref[phase, pl.ds(base + n * CELLS, CELLS), :]

            def write_act(tap, window, n=n):
                act_cols[pl.ds(base + n * CELLS, CELLS), tap * GROUP : (tap + 1) * GROUP] = window

            fill_taps(taps, 1, read_act, write_act)
            flat = tuple((0, t[1], t[2]) for t in taps)

            def read_up(phase, n=n):
                return up_ref[pl.ds(base + n * CELLS, CELLS), :]

            def write_up(tap, window, n=n):
                at = place[tap] * GROUP
                up_cols[n * CELLS : (n + 1) * CELLS, at : at + GROUP] = window

            fill_taps(flat, -1, read_up, write_up)
        at = 0
        for phase in range(phases):
            size = sum(t[0] == phase for t in taps) * GROUP
            back = jnp.dot(
                up_cols[:, at : at + size], w_cols[at : at + size, :], preferred_element_type=f32
            )
            at += size
            pre = pre_ref[phase, pl.ds(base, rows), :].astype(f32)
            down_ref[phase, pl.ds(base, rows), :] = (gelu_prime(pre) * GAMMA * back).astype(bf16)
        return carry

    lax.fori_loop(0, up_ref.shape[0] // rows, step, 0)
    grad_ref[...] = lax.dot_general(
        up_ref[...], act_cols[...], (((0,), (0,)), ((), ())), preferred_element_type=f32
    ).astype(grad_ref.dtype)


def conv_backward(up, act, pre, weight, taps):
    phases, cells, channels = act.shape
    chunk = min(CHUNK, cells // CELLS)
    return pl.pallas_call(
        functools.partial(conv_back_kernel, taps, chunk),
        grid=(channels // GROUP,),
        out_shape=[
            jax.ShapeDtypeStruct((phases, cells, channels), bf16),
            jax.ShapeDtypeStruct((channels, 9 * GROUP), bf16),
        ],
        in_specs=[
            pl.BlockSpec((cells, GROUP), lambda g: (0, g)),
            pl.BlockSpec((phases, cells, GROUP), lambda g: (0, 0, g)),
            pl.BlockSpec((phases, cells, GROUP), lambda g: (0, 0, g)),
            pl.BlockSpec((GROUP, 9 * GROUP), lambda g: (g, 0)),
        ],
        out_specs=[
            pl.BlockSpec((phases, cells, GROUP), lambda g: (0, 0, g)),
            pl.BlockSpec((GROUP, 9 * GROUP), lambda g: (g, 0)),
        ],
        scratch_shapes=[
            pltpu.VMEM((9 * GROUP, GROUP), bf16),
            pltpu.VMEM((chunk * CELLS, 9 * GROUP), bf16),
            pltpu.VMEM((cells, 9 * GROUP), bf16),
        ],
        compiler_params=pltpu.CompilerParams(vmem_limit_bytes=48 * MIB),
        cost_estimate=pl.CostEstimate(
            flops=4 * cells * channels * 9 * GROUP,
            bytes_accessed=cells * channels * (2 + 8 * phases),
            transcendentals=cells * channels * phases,
        ),
        name="conv_backward",
    )(up, act, pre, weight)


def new_values(w, g, m, v, standard, clip):
    fan_in = w.shape[1]
    if standard:
        centre = w - jnp.mean(w, axis=-1, keepdims=True)
        spread = jnp.mean(centre * centre, axis=-1, keepdims=True)
        scale = lax.rsqrt(spread * fan_in + STD_EPS)
        along = jnp.sum(g * centre, axis=-1, keepdims=True)
        mean_g = jnp.mean(g, axis=-1, keepdims=True)
        g = scale * (g - mean_g) - (scale * scale * scale * along) * centre
    if clip:
        ceiling = CLIP * jnp.sqrt(jnp.sum(w * w, axis=-1, keepdims=True))
        norm = jnp.sqrt(jnp.sum(g * g, axis=-1, keepdims=True))
        g = g * (ceiling / jnp.maximum(norm, ceiling))
    m = DECAY_ONE * m + (1.0 - DECAY_ONE) * g
    v = DECAY_TWO * v + (1.0 - DECAY_TWO) * g * g
    root = v * lax.rsqrt(v) * (1.0 - DECAY_TWO**STEP_COUNT) ** -0.5 + ADAM_EPS
    step = (RATE / (1.0 - DECAY_ONE**STEP_COUNT)) * m * pl.reciprocal(root)
    return m, v, (1.0 - RATE * WEIGHT_DECAY) * w - step


def update_packed_kernel(shapes, share_ref, packed_ref, *refs):
    count = len(shapes)
    valid = pl.program_id(0) < share_ref[0]
    at = 0
    for k, shape in enumerate(shapes):
        part, width = shape[-2] // 6, shape[-1]
        for lead in leads(shape):
            g, at = read_packed(packed_ref, at, part, width)
            g = jnp.where(valid, g.astype(f32), 0.0)
            w, m, v = (refs[3 * k + i][lead] for i in range(3))
            for i, value in enumerate(new_values(w, g, m, v, True, True)):
                refs[3 * (count + k) + i][lead] = value


def update_packed(packed, members, share):
    specs, operands, shapes = [], [], []
    for weight, first, second in members:
        shape = weight.shape
        block = shape[:-2] + (shape[-2] // 6, shape[-1])
        zeros = (0,) * (len(shape) - 2)
        specs += [pl.BlockSpec(block, lambda j, zeros=zeros: zeros + (j, 0))] * 3
        operands += [weight, first, second]
        shapes.append(shape)
    total = sum(o.size for o in operands)
    outs = pl.pallas_call(
        functools.partial(update_packed_kernel, tuple(shapes)),
        grid=(6,),
        out_shape=[jax.ShapeDtypeStruct(o.shape, f32) for o in operands],
        in_specs=[
            pl.BlockSpec(memory_space=pltpu.SMEM),
            pl.BlockSpec((None,) + packed.shape[1:], lambda j: (j, 0, 0)),
        ]
        + specs,
        out_specs=specs,
        compiler_params=pltpu.CompilerParams(vmem_limit_bytes=58 * MIB),
        cost_estimate=pl.CostEstimate(
            flops=10 * total, bytes_accessed=9 * total, transcendentals=total // 3
        ),
        name="update_packed",
    )(share, packed, *operands)
    return [tuple(outs[3 * k : 3 * k + 3]) for k in range(len(members))]


def update_factors_kernel(unit, turned, block, share_ref, units_ref, inputs_ref, w_ref, m_ref, v_ref, m_out, v_out, w_out, g_all):
    step = pl.program_id(1)

    @pl.when(step == 0)
    def _():
        left, right = (inputs_ref, units_ref) if turned else (units_ref, inputs_ref)
        g_all[...] = lax.dot_general(
            left[...], right[...], (((0,), (0,)), ((), ())), preferred_element_type=f32
        )

    rows = pl.ds(pl.multiple_of(step * block, 8), block)
    shape = w_ref.shape
    index = lax.broadcasted_iota(jnp.int32, shape if turned else (block, 1), 1 if turned else 0)
    index += 0 if turned else step * block
    g = jnp.where(index < share_ref[0] * unit, g_all[rows, :], 0.0)
    m_out[...], v_out[...], w_out[...] = new_values(
        w_ref[...], g, m_ref[...], v_ref[...], False, not turned
    )


def update_factors(weight, units, gathered, columns, first, second, share, turned=False):
    count, rows, width = weight.shape
    images = units.shape[1]
    start, across, stride = columns
    block = 504 if turned else rows
    steps = -(-rows // block)
    spec = pl.BlockSpec((None, block, width), lambda k, i: (k, i, 0))
    owned = (width if turned else rows) // 6
    made = (across, width) if turned else (rows, across)
    return pl.pallas_call(
        functools.partial(update_factors_kernel, owned, turned, block),
        grid=(count, steps),
        out_shape=[jax.ShapeDtypeStruct(weight.shape, f32)] * 3,
        in_specs=[
            pl.BlockSpec(memory_space=pltpu.SMEM),
            pl.BlockSpec((None, images, units.shape[2]), lambda k, i: (k, 0, 0)),
            pl.BlockSpec((images, across), lambda k, i: (0, start + stride * k)),
        ]
        + [spec] * 3,
        out_specs=[spec] * 3,
        scratch_shapes=[pltpu.VMEM(made, f32)],
        compiler_params=pltpu.CompilerParams(vmem_limit_bytes=56 * MIB),
        cost_estimate=pl.CostEstimate(
            flops=count * rows * width * (2 * images + 15),
            bytes_accessed=24 * count * rows * width,
            transcendentals=count * rows * width,
        ),
        name="update_factors",
    )(share, units, gathered, weight, first, second)


def update_kernel(unit, standard, clip, block, share_ref, w_ref, g_ref, m_ref, v_ref, m_out, v_out, w_out):
    row = pl.program_id(0) * block + lax.broadcasted_iota(jnp.int32, (block, 1), 0)
    g = jnp.where(row % (6 * unit) < share_ref[0] * unit, g_ref[...].astype(f32), 0.0)
    m_out[...], v_out[...], w_out[...] = new_values(
        w_ref[...], g, m_ref[...], v_ref[...], standard, clip
    )


def update(weight, gradient, first, second, share, standard, clip):
    shape = weight.shape
    width = shape[-1]
    flat = [a.reshape(-1, width) for a in (weight, gradient, first, second)]
    rows = flat[0].shape[0]
    block = rows
    for size in range(192, 0, -16):
        if rows % size == 0:
            block = size
            break
    spec = pl.BlockSpec((block, width), lambda i: (i, 0))
    outs = pl.pallas_call(
        functools.partial(update_kernel, shape[-2] // 6, standard, clip, block),
        grid=(rows // block,),
        out_shape=[jax.ShapeDtypeStruct((rows, width), f32)] * 3,
        in_specs=[pl.BlockSpec(memory_space=pltpu.SMEM)] + [spec] * 4,
        out_specs=[spec] * 3,
        compiler_params=pltpu.CompilerParams(vmem_limit_bytes=48 * MIB),
        cost_estimate=pl.CostEstimate(
            flops=30 * rows * width, bytes_accessed=28 * rows * width, transcendentals=rows * width
        ),
        name="update",
    )(share, *flat)
    return tuple(o.reshape(shape) for o in outs)


def split_small(values, rows):
    values = jnp.pad(values, (0, -values.shape[0] % (128 * rows))).reshape(rows, -1)
    terms = []
    for _ in range(3):
        term = lax.reduce_precision(values, 8, 7)
        terms.append(term.astype(bf16))
        values = values - term
    return terms


def join_small(terms, rows):
    width = terms.shape[1] // 3
    total = jnp.sum(terms.astype(f32).reshape(-1, rows, 3 * width), axis=0)
    return (total[:, :width] + total[:, width : 2 * width] + total[:, 2 * width :]).reshape(-1)


def dot_t(left, right):
    return lax.dot_general(
        left, right, (((left.ndim - 1,), (1,)), ((), ())), preferred_element_type=f32
    )


def dot_n(left, right):
    return lax.dot_general(
        left, right, (((left.ndim - 1,), (0,)), ((), ())), preferred_element_type=f32
    )


def dot_sum(upstream, inputs):
    up = upstream.reshape(-1, upstream.shape[-1])
    low = inputs.reshape(-1, inputs.shape[-1])
    return lax.dot_general(up, low, (((0,), (0,)), ((), ())), preferred_element_type=f32)


def tail_forward(act_three, out_w, down_w, up_w):
    images = act_three.shape[0] // CELLS
    pre_four = dot_t(act_three, out_w).reshape(images, CELLS, -1)
    kept_four = pre_four.astype(bf16)
    squeezed = (jnp.sum(pre_four, axis=1) / CELLS).astype(bf16)
    pre_down = dot_t(squeezed, down_w)
    act_down = gelu_act(pre_down).astype(bf16)
    gate_sig = jax.nn.sigmoid(dot_t(act_down, up_w))
    return kept_four, squeezed, pre_down, act_down, gate_sig


def tail_backward(grad_hidden, stored, down_w, up_w, gain):
    pre_four, squeezed, pre_down, act_down, gate_sig = stored
    gate = 2.0 * gate_sig
    raw_gate = jnp.sum(grad_hidden * pre_four, axis=1)
    gain_part = ALPHA * jnp.sum(raw_gate * gate)
    grad_gate = raw_gate * (ALPHA * gain)
    grad_up = (grad_gate * 2.0 * gate_sig * (1.0 - gate_sig)).astype(bf16)
    grad_down = (gelu_prime(pre_down) * dot_n(grad_up, up_w)).astype(bf16)
    grad_squeezed = dot_n(grad_down, down_w)
    grad_four = (
        grad_hidden * (ALPHA * gain * gate)[:, None, :] + (grad_squeezed / CELLS)[:, None, :]
    ).astype(bf16)
    factors = [grad_up, act_down, grad_down, squeezed]
    return grad_four.reshape(-1, grad_four.shape[-1]), factors, gain_part


def body(
    images,
    labels,
    class_counts,
    owner_share,
    w_entry,
    first_entry,
    second_entry,
    w_in,
    first_in,
    second_in,
    w_mid,
    first_mid,
    second_mid,
    w_out,
    first_out,
    second_out,
    se_down,
    first_down,
    second_down,
    se_up,
    first_up,
    second_up,
    w_final,
    first_final,
    second_final,
    head,
    first_head,
    second_head,
    small_params,
    first_small,
    second_small,
):
    owner, local, starts, slot_part = owner_tables(owner_share)
    me = lax.axis_index("dp")
    devices = lax.axis_size("dp")
    my_share = lax.dynamic_slice_in_dim(owner_share, me, 1, 0)
    my_start = lax.dynamic_index_in_dim(starts, me, 0, keepdims=False)

    rows_n, cols_n = lax.axis_size("ha"), lax.axis_size("wa")
    spread = rows_n * cols_n
    micro, per_dp, tile_h, tile_w, in_width = images.shape
    count = micro * per_dp // spread
    tiles = images.reshape(spread, count, tile_h, tile_w, in_width)
    tiles = lax.all_to_all(tiles, ("ha", "wa"), 0, 0, tiled=True)
    spot = lax.axis_index("ha") * cols_n + lax.axis_index("wa")
    my_labels = lax.dynamic_slice_in_dim(labels.reshape(-1), spot * count, count, 0)

    def middle(layer):
        return [(w_mid, (layer, 0), True), (w_mid, (layer, 1), True)]

    def rest(layer):
        return [(w_out, (layer,), True), (se_down, (layer,), False), (se_up, (layer,), False)]

    groups = [
        [(w_entry, (), True)],
        middle(0) + rest(0),
        [(w_in, (0,), True)] + middle(1) + rest(1),
        [(w_final, (), True)],
        [(head, (), False)],
    ]
    staged = known_mesh()
    if staged:
        tables = {flag: source_tables(owner, local, flag) for flag in (True, False)}
        moves = [Gather(groups[0], True), Gather(groups[1])]
        moves[0].along_x()
        moves[1].along_x(moves[0].near)
        moves[0].cores()
        for entries in groups[2:]:
            entries[0] = (after(entries[0][0], moves[0].near),) + entries[0][1:]
            moves.append(Gather(entries))
        moves[1].near = after(moves[1].near, *[m.own for m in moves[2:]])
        moves[1].along_y()
        moves[2].along_x(moves[1].near)
    cells = count * CELLS
    if staged:
        act_zero, pooled = prepare(tiles, rows_n, cols_n)
    else:
        pixels = tiles.reshape(
            rows_n, cols_n, count, tile_h // 2, 2, tile_w // 2, 2, in_width
        ).transpose(4, 6, 2, 0, 3, 1, 5, 7).reshape(4, cells, in_width)
        act_zero = (gelu_act(pixels.astype(f32)) * GAMMA).astype(bf16)
        pooled = (jnp.sum(act_zero.astype(f32), axis=0) * 0.25).astype(bf16)

    def hold(value, arrivals, *then):
        if not staged:
            return value
        came = [getattr(moves[k], name) for k, name in arrivals]
        value, *came = lax.optimization_barrier((value, *came))
        for (k, name), buffer in zip(arrivals, came):
            setattr(moves[k], name, buffer)
        for step, k in then:
            if step == "x":
                moves[k].along_x(moves[k - 1].near)
            elif step == "y":
                moves[k].along_y()
            else:
                moves[k].cores()
        return value

    def weights_of(group):
        if staged:
            return moves[group].unpacked(tables)
        return gather_plain(groups[group], owner, local)

    gains = small_params[:LAYERS]
    head_bias = small_params[LAYERS:]
    images_all = micro * per_dp * lax.axis_size("dp")
    class_weight = 1.0 / class_counts.astype(f32)

    kept = []
    weights = []
    hidden = None
    for layer in range(LAYERS):
        if layer:
            scale = GAMMA * (1.0 + layer * ALPHA * ALPHA) ** (-0.5)
            act_zero = (gelu_act(hidden) * scale).astype(bf16).reshape(1, cells, -1)
        taps = TAPS_TWO if layer == 0 else TAPS_ONE
        if layer == 0:
            (entry_low,) = weights_of(0)
            in_low, skip_low = entry_low[:NECK], entry_low[NECK:]
        else:
            in_low, *others = weights_of(2)
        pre_one = dot_t(act_zero, in_low)
        act_one = (gelu_act(pre_one) * GAMMA).astype(bf16)
        if layer == 0:
            act_one = hold(
                act_one, [(1, "far"), (2, "near")], ("cores", 1), ("y", 2), ("x", 3)
            )
            others = weights_of(1)
        else:
            act_one = hold(act_one, [(4, "near")], ("y", 4))
        mid_a, mid_b, out_low, down_low, up_low = others
        weights.append((in_low, mid_a, mid_b, out_low, down_low, up_low))
        pre_two, act_two = conv_forward(act_one, mid_a, taps)
        pre_three, act_three = conv_forward(act_two[None], mid_b, TAPS_ONE)
        if layer == 0:
            act_three = hold(act_three, [(3, "near")], ("x", 4))
        tail = tail_forward(act_three, out_low, down_low, up_low)
        branch = (ALPHA * gains[layer]) * tail[0] * (2.0 * tail[4])[:, None, :]
        if layer == 0:
            shortcut = dot_t(pooled, skip_low).reshape(branch.shape)
        else:
            shortcut = hidden.reshape(branch.shape)
        before = None if hidden is None else hidden.astype(bf16)
        hidden = (shortcut + branch).reshape(cells, -1)
        if layer == 0:
            hidden = hold(hidden, [(2, "far")], ("cores", 2), ("y", 3))
        else:
            hidden = hold(hidden, [(3, "far")], ("cores", 3))
        kept.append((before, act_zero, pre_one.astype(bf16), act_one, pre_two, act_two, pre_three, act_three, tail, pooled))
    (final_low,) = weights_of(3)
    hidden_low = hidden.astype(bf16)
    pre_final = dot_t(hidden_low, final_low).reshape(count, CELLS, -1)
    pooled_final = (jnp.sum(gelu_act(pre_final) * GAMMA, axis=1) / CELLS).astype(bf16)
    pooled_final = hold(pooled_final, [(4, "far")], ("cores", 4))
    (head_low,) = weights_of(4)
    logits = dot_n(pooled_final, head_low) + head_bias
    largest = jnp.max(logits, axis=1, keepdims=True)
    log_total = largest[:, 0] + jnp.log(jnp.sum(jnp.exp(logits - largest), axis=1))
    one_hot = (my_labels[:, None] == jnp.arange(logits.shape[1])[None, :]).astype(f32)
    picked = jnp.sum(one_hot * logits, axis=1)
    image_weight = jnp.sum(one_hot * class_weight[None, :], axis=1)
    loss_part = jnp.sum(image_weight * (log_total - picked))
    softmax_p = jnp.exp(logits - log_total[:, None])
    grad_logits = image_weight[:, None] * (softmax_p - one_hot) / images_all
    bias_part = jnp.sum(grad_logits, axis=0)
    grad_low = grad_logits.astype(bf16)
    grad_pooled = dot_t(grad_low, head_low) * (GAMMA / CELLS)
    grad_final = (gelu_prime(pre_final.astype(bf16).astype(f32)) * grad_pooled[:, None, :]).astype(bf16).reshape(cells, -1)
    final_grad = dot_sum(grad_final, hidden_low).astype(bf16)
    grad_hidden = dot_n(grad_final, final_low)
    if staged:
        packed = pack_gradients([final_grad], slot_part, devices, 16)
        packed, grad_hidden = lax.optimization_barrier((packed, grad_hidden))
        final_part = lax.psum_scatter(
            packed.reshape(devices, -1, 128), "dp", scatter_dimension=0, tiled=False
        )
        final_sum = lax.psum(final_part, ("ha", "wa")).reshape(6, -1, 128)

    in_grads = [None] * LAYERS
    mid_grads = [None] * LAYERS
    out_grads = [None] * LAYERS
    all_factors = [pooled_final, grad_low]
    gain_parts = [None] * LAYERS
    for layer in reversed(range(LAYERS)):
        before, act_zero, pre_one, act_one, pre_two, act_two, pre_three, act_three, tail, pooled = kept[layer]
        in_low, mid_a, mid_b, out_low, down_low, up_low = weights[layer]
        taps = TAPS_TWO if layer == 0 else TAPS_ONE
        grad_four, factors, gain_parts[layer] = tail_backward(
            grad_hidden.reshape(count, CELLS, -1), tail, down_low, up_low, gains[layer]
        )
        all_factors = factors + all_factors
        if layer == 0:
            small = jnp.concatenate([loss_part[None], jnp.stack(gain_parts), bias_part])
            all_factors = jnp.concatenate(all_factors + split_small(small, count), axis=1)
            all_factors, grad_four = lax.optimization_barrier((all_factors, grad_four))
            gathered = lax.all_gather(all_factors, EVERY, axis=0, tiled=True)
        out_grads[layer] = dot_sum(grad_four, act_three).astype(bf16)
        grad_three = (gelu_prime(pre_three.astype(f32)) * GAMMA * dot_n(grad_four, out_low)).astype(bf16)
        grad_two, mid_grad_b = conv_backward(grad_three, act_two[None], pre_two[None], mid_b, TAPS_ONE)
        grad_one, mid_grad_a = conv_backward(grad_two[0], act_one, pre_one, mid_a, taps)
        mid_grads[layer] = (mid_grad_a, mid_grad_b)
        in_grad = dot_sum(grad_one, act_zero).astype(bf16)
        if layer == 0:
            skip_grad = dot_sum(grad_hidden.astype(bf16), pooled).astype(bf16)
            in_grads[layer] = jnp.concatenate([in_grad, skip_grad], axis=0)
        else:
            in_grads[layer] = in_grad
            scale = GAMMA * (1.0 + layer * ALPHA * ALPHA) ** (-0.5)
            grad_zero = dot_n(grad_one[0], in_low)
            grad_hidden = grad_hidden + gelu_prime(before.astype(f32)) * scale * grad_zero

    def own_units(span):
        part = span[1] // starts.shape[0] // 4
        return lax.dynamic_slice_in_dim(gathered, span[0] + my_start * part, 6 * part, 1)

    wide, narrow, final_width = tail[0].shape[-1], tail[3].shape[-1], pooled_final.shape[1]
    spans = []
    at = 0
    for width in [wide, narrow, narrow, wide] * LAYERS + [final_width, logits.shape[1]]:
        spans.append((at, width))
        at += width

    small = join_small(gathered[:, at:], count)
    loss_sum = small[0]
    small_grad = small[1 : 1 + small_params.shape[0]]

    flat_mids = [g for pair in mid_grads for g in pair]
    local_grads = in_grads + out_grads + flat_mids
    members = (
        (w_entry, first_entry, second_entry),
        (w_in, first_in, second_in),
        (w_out, first_out, second_out),
        (w_mid, first_mid, second_mid),
        (w_final, first_final, second_final),
    )
    if staged:
        packed = pack_gradients(local_grads, slot_part, devices, SPAN)
        packed = after(packed, final_part)
        new = update_packed(sum_at_owners(packed), members[:-1], my_share)
        new += update_packed(final_sum, members[-1:], my_share)
    else:
        sums = [sum_plain(g, slot_part[0]) for g in local_grads + [final_grad]]
        new = []
        for weight, first, second in members:
            count = len(leads(weight.shape))
            total, sums = jnp.stack(sums[:count]), sums[count:]
            new.append(update(weight, total, first, second, my_share, True, True))
    entry_new, in_new, out_new, mid_new, final_new = new
    def owned(first_span):
        return jnp.stack([own_units(spans[4 * k + first_span]) for k in range(LAYERS)])

    def blocks(first_span):
        (at, across), (then, _) = spans[first_span], spans[4 + first_span]
        return at // across, across, (then - at) // across

    up_new = update_factors(
        se_up, owned(0), gathered, blocks(1), first_up, second_up, my_share
    )
    down_new = update_factors(
        se_down, owned(2), gathered, blocks(3), first_down, second_down, my_share
    )
    head_new = update_factors(
        head.T[None],
        own_units(spans[-2])[None],
        gathered,
        (spans[-1][0] // 1024, 1024, 0),
        first_head.T[None],
        second_head.T[None],
        my_share,
        turned=True,
    )
    head_new = [a[0].T for a in head_new]
    results = [loss_sum]
    for new in (entry_new, in_new, mid_new, out_new, down_new, up_new, final_new, head_new):
        results.extend(new)
    m = DECAY_ONE * first_small + (1.0 - DECAY_ONE) * small_grad
    v = DECAY_TWO * second_small + (1.0 - DECAY_TWO) * small_grad * small_grad
    m_hat = m / (1.0 - DECAY_ONE**STEP_COUNT)
    v_hat = v / (1.0 - DECAY_TWO**STEP_COUNT)
    results.extend(
        [
            m,
            v,
            small_params
            - SMALL_RATE * (m_hat / (jnp.sqrt(v_hat) + ADAM_EPS) + WEIGHT_DECAY * small_params),
        ]
    )
    return tuple(results)


def solution(mesh):
    owned = (
        [P("dp", None)] * 3
        + [P(None, "dp", None)] * 3
        + [P(None, None, "dp", None)] * 3
        + [P(None, "dp", None)] * 9
        + [P("dp", None)] * 6
        + [P()] * 3
    )
    return jax.shard_map(
        body,
        mesh=mesh,
        in_specs=tuple([P(None, "dp", "ha", "wa", None), P(None, "dp"), P(), P()] + owned),
        out_specs=tuple([P()] + owned),
        check_vma=False,
    )
```

```python
import functools

import jax
import jax.numpy as jnp
from jax import lax
from jax.experimental import pallas as pl
from jax.experimental.pallas import tpu as pltpu
from jax.sharding import PartitionSpec as P

NECK = 768
GROUP = 128
HEIGHT = 8
BREADTH = 8
CELLS = HEIGHT * BREADTH
LAYERS = 2
STEP_COUNT = 5

GAMMA = 1.7015043497085571
ALPHA = 0.2
CLIP = 0.01
RATE = 0.05
SMALL_RATE = 0.5
DECAY_ONE = 0.9
DECAY_TWO = 0.999
ADAM_EPS = 1e-08
WEIGHT_DECAY = 5e-05
STD_EPS = 0.0001
GELU_SCALE = 0.7978845608028654
GELU_CUBE = 0.044715
EVERY = ("dp", "ha", "wa")
MIB = 1 << 20

TAPS_ONE = tuple((0, t // 3 - 1, t % 3 - 1) for t in range(9))
TAPS_TWO = tuple(((t // 3 % 2) * 2 + t % 3 % 2, t // 3 // 2, t % 3 // 2) for t in range(9))

CHUNK = 16

f32 = jnp.float32
bf16 = jnp.bfloat16


def gelu_act(v):
    half = 0.5 * v
    return half + half * jnp.tanh(v * (GELU_SCALE + (GELU_SCALE * GELU_CUBE) * (v * v)))


def gelu_prime(v):
    cube = (GELU_SCALE * GELU_CUBE) * (v * v)
    th = jnp.tanh(v * (GELU_SCALE + cube))
    return 0.5 + 0.5 * (th + v * (1.0 - th * th) * (GELU_SCALE + 3.0 * cube))


def standardize(weight):
    fan_in = weight.shape[-1]
    centre = weight - jnp.mean(weight, axis=-1, keepdims=True)
    spread = jnp.mean(centre * centre, axis=-1, keepdims=True)
    return centre * lax.rsqrt(spread * fan_in + STD_EPS)


def owner_tables(shares):
    devices = shares.shape[0]
    ids = jnp.arange(devices, dtype=jnp.int32)
    starts = jnp.sum(jnp.where(ids[None, :] < ids[:, None], shares[None, :], 0), axis=1)
    part_ids = jnp.arange(4 * devices, dtype=jnp.int32)
    owner = jnp.sum((part_ids[:, None] >= (starts + shares)[None, :]).astype(jnp.int32), axis=1)
    first = jnp.sum(jnp.where(owner[:, None] == ids[None, :], starts[None, :], 0), axis=1)
    local = (part_ids - first).astype(jnp.int32)
    held = jnp.minimum(jnp.arange(6, dtype=jnp.int32)[None, :], shares[:, None] - 1)
    slot_part = (starts[:, None] + held).reshape(-1).astype(jnp.int32)
    return owner, local, starts, (slot_part, (ids[:, None] * 6 + held).reshape(-1))


def known_mesh():
    return tuple(lax.axis_size(a) for a in EVERY) == (4, 4, 2)


def unit_slots(owner, local, part):
    return ((owner * 6 + local)[:, None] * part + jnp.arange(part)[None, :]).reshape(-1)


def gather_plain(entries, owner, local):
    full = []
    for array, lead, standard in entries:
        block = standardize(array[lead]) if standard else array[lead]
        every = lax.all_gather(block.astype(bf16), "dp", axis=0, tiled=True)
        full.append(jnp.take(every, unit_slots(owner, local, block.shape[0] // 6), axis=0))
    return full


def sum_plain(gradient, slot_part):
    part = gradient.shape[0] // (4 * lax.axis_size("dp"))
    units = (slot_part[:, None] * part + jnp.arange(part)[None, :]).reshape(-1)
    slots = jnp.take(gradient, units, axis=0)
    owned = lax.psum_scatter(slots, "dp", scatter_dimension=0, tiled=True)
    return lax.psum(owned, ("ha", "wa"))


def leads(shape):
    tuples = [()]
    for size in shape[:-2]:
        tuples = [t + (i,) for t in tuples for i in range(size)]
    return tuples


def packed_rows(part, width):
    return part * (-(-width // 128))


def pack_into(ref, at, block):
    part, width = block.shape
    for column in range(0, width, 128):
        lanes = min(128, width - column)
        piece = block[:, column : column + lanes]
        if lanes < 128:
            piece = jnp.concatenate([piece, jnp.zeros((part, 128 - lanes), piece.dtype)], axis=1)
        ref[at : at + part, :] = piece
        at += part
    return at


def read_packed(ref, at, part, width):
    pieces = []
    for column in range(0, width, 128):
        pieces.append(ref[at : at + part, : min(128, width - column)])
        at += part
    return (pieces[0] if len(pieces) == 1 else jnp.concatenate(pieces, axis=1)), at


def pack_weights_kernel(standard, *refs):
    out_ref = refs[-1]
    at = 0
    for ref, flag in zip(refs[:-1], standard):
        block = ref[...]
        at = pack_into(out_ref, at, (standardize(block) if flag else block).astype(bf16))


def pack_weights(entries):
    specs, rows = [], 0
    for array, lead, _ in entries:
        part, width = array.shape[-2] // 6, array.shape[-1]
        specs.append(
            pl.BlockSpec((None,) * len(lead) + (part, width), lambda j, lead=lead: lead + (j, 0))
        )
        rows += packed_rows(part, width)
    return pl.pallas_call(
        functools.partial(pack_weights_kernel, tuple(e[2] for e in entries)),
        grid=(6,),
        out_shape=jax.ShapeDtypeStruct((6, rows, 128), bf16),
        in_specs=specs,
        out_specs=pl.BlockSpec((None, rows, 128), lambda j: (j, 0, 0)),
        compiler_params=pltpu.CompilerParams(vmem_limit_bytes=40 * MIB),
        cost_estimate=pl.CostEstimate(
            flops=6 * rows * 128 * 8, bytes_accessed=6 * rows * 128 * 6, transcendentals=0
        ),
        name="pack_weights",
    )(*[e[0] for e in entries])


def unpack_kernel(count, shapes, which_ref, place_ref, *refs):
    sources = refs[:count]
    outs = refs[count : count + len(shapes)]
    held, *rest = refs[count + len(shapes) :]
    stages, (arrived, left) = rest[: len(shapes)], rest[len(shapes) :]
    parts = which_ref.shape[0]

    def fetch(i, carry):
        for s, source in enumerate(sources):

            @pl.when(which_ref[i] == s)
            def _(source=source):
                pltpu.make_async_copy(source.at[place_ref[i]], held.at[i], arrived.at[i]).start()

        return carry

    def spread(group, carry):
        for j in range(4):
            i = group * 4 + j
            pltpu.make_async_copy(held.at[i], held.at[i], arrived.at[i]).wait()
            at = 0
            for k, (part, width) in enumerate(shapes):
                block, at = read_packed(held.at[i], at, part, width)
                stages[k][pl.ds(pl.multiple_of(i * part, part), part), :] = block
        for k, (part, width) in enumerate(shapes):
            rows = pl.ds(pl.multiple_of(group * 4 * part, part), 4 * part)
            pltpu.make_async_copy(stages[k].at[rows, :], outs[k].at[rows, :], left.at[k]).start()
        return carry

    lax.fori_loop(0, parts, fetch, 0)
    lax.fori_loop(0, parts // 4, spread, 0)
    for k in range(len(shapes)):
        pltpu.make_async_copy(stages[k], outs[k], left.at[k]).wait()


def unpack_weights(sources, which, place, shapes):
    count, parts = len(sources), which.shape[0]
    rows = sources[0].shape[1]
    full = [(parts * p, w) for p, w in shapes]
    return pl.pallas_call(
        functools.partial(unpack_kernel, count, shapes),
        out_shape=[jax.ShapeDtypeStruct(f, bf16) for f in full],
        in_specs=[pl.BlockSpec(memory_space=pltpu.SMEM)] * 2
        + [pl.BlockSpec(memory_space=pl.ANY)] * count,
        out_specs=[pl.BlockSpec(memory_space=pl.ANY)] * len(shapes),
        scratch_shapes=[pltpu.VMEM((parts, rows, 128), bf16)]
        + [pltpu.VMEM(f, bf16) for f in full]
        + [pltpu.SemaphoreType.DMA((parts,)), pltpu.SemaphoreType.DMA((len(shapes),))],
        compiler_params=pltpu.CompilerParams(vmem_limit_bytes=40 * MIB),
        cost_estimate=pl.CostEstimate(
            flops=0, bytes_accessed=parts * rows * 128 * 4, transcendentals=0
        ),
        name="unpack_weights",
    )(which, place, *sources)


def after(value, *others):
    return lax.optimization_barrier((value,) + others)[0]


CHIP = [(i, i ^ 2) for i in range(4)]
CORE = [(i, i ^ 1) for i in range(4)]


class Gather:
    def __init__(self, entries):
        self.shapes = tuple((e[0].shape[-2] // 6, e[0].shape[-1]) for e in entries)
        self.own = pack_weights(entries)

    def along_x(self, *others):
        mine = lax.dynamic_slice_in_dim(self.own, lax.axis_index("wa") * 3, 3, 0)
        self.near = lax.ppermute(after(mine, *others), "dp", CHIP)

    def along_y(self):
        self.far = lax.ppermute(self.near, "wa", [(0, 1), (1, 0)])

    def cores(self):
        buffers = [self.own, self.near, self.far]
        self.buffers = buffers + [lax.ppermute(b, "dp", CORE) for b in buffers]

    def unpacked(self, tables):
        return unpack_weights(self.buffers, *tables, self.shapes)


def source_tables(owner, local):
    me = lax.axis_index("dp")
    side = lax.axis_index("wa")
    away = owner // 2 != me // 2
    which = jnp.where(away, jnp.where(local // 3 == side, 1, 2), 0)
    which = which + 3 * (owner % 2 != me % 2)
    return which.astype(jnp.int32), jnp.where(away, local % 3, local).astype(jnp.int32)


def pack_gradients_kernel(pad, part_ref, slot_ref, *refs):
    out_ref = refs[-1]
    at = 0
    for ref in refs[:-1]:
        at = pack_into(out_ref, at, ref[...].astype(bf16))
    if pad:
        out_ref[at : at + pad, :] = jnp.zeros((pad, 128), bf16)


def pack_gradients(gradients, slot_part, devices, unit):
    specs, rows = [], 0
    for gradient in gradients:
        part, width = gradient.shape[0] // (4 * devices), gradient.shape[1]
        specs.append(pl.BlockSpec((part, width), lambda s, parts, held: (parts[s], 0)))
        rows += packed_rows(part, width)
    pad = -rows % unit
    rows += pad
    slots = 6 * devices
    return pl.pallas_call(
        functools.partial(pack_gradients_kernel, pad),
        grid_spec=pltpu.PrefetchScalarGridSpec(
            num_scalar_prefetch=2,
            grid=(slots,),
            in_specs=specs,
            out_specs=pl.BlockSpec((None, rows, 128), lambda s, parts, held: (held[s], 0, 0)),
        ),
        out_shape=jax.ShapeDtypeStruct((slots, rows, 128), bf16),
        compiler_params=pltpu.CompilerParams(vmem_limit_bytes=40 * MIB),
        cost_estimate=pl.CostEstimate(
            flops=0, bytes_accessed=slots * rows * 128 * 4, transcendentals=0
        ),
        name="pack_gradients",
    )(*slot_part, *gradients)


SPAN = 1024
AXES = ("x", "y", "near", "far")
ORDERS = (AXES,)
LAGS = (0, 1, 2, 3, 4, 5, 6, 7)


def sum_kernel(orders, spans, packed, owned, own, core, one, two, three, four, sends, recvs, local_sems):
    dp, z, y = lax.axis_index("dp"), lax.axis_index("ha"), lax.axis_index("wa")
    bit = {"x": dp // 2, "core": dp % 2, "y": y, "near": z % 2, "far": z // 2}
    peer = {
        "x": {"dp": (dp + 2) % 4},
        "core": {"dp": dp + 1 - 2 * (dp % 2)},
        "y": {"wa": 1 - y},
        "near": {"ha": z + 1 - 2 * (z % 2)},
        "far": {"ha": (z + 2) % 4},
    }
    barrier = pltpu.get_barrier_semaphore()
    for other in peer.values():
        pl.semaphore_signal(barrier, inc=1, device_id=other, device_id_type=pl.DeviceIdType.MESH)
    pl.semaphore_wait(barrier, len(peer))

    buffers = [core, one, two, three, four]
    kinds = len(orders)

    def index(ref, chunk, names, fixed):
        return ref.at[(chunk,) + tuple(fixed[n] if n in fixed else slice(None) for n in names)]

    def remote(src, dst, stage, chunk, to):
        return pltpu.make_async_remote_copy(
            src_ref=src,
            dst_ref=dst,
            send_sem=sends.at[stage, chunk],
            recv_sem=recvs.at[stage, chunk],
            device_id=peer[to],
            device_id_type=pl.DeviceIdType.MESH,
        )

    def copy_of(stage, kind, chunk):
        order = orders[kind]
        if stage == 0:
            return remote(packed.at[:, 1 - bit["core"], chunk], core.at[chunk], 0, chunk, "core")
        if stage <= 4:
            before = [n for n in AXES if n not in order[: stage - 1]]
            axis = order[stage - 1]
            src = index(buffers[stage - 1], chunk, before, {axis: 1 - bit[axis]})
            return remote(src, buffers[stage].at[chunk], stage, chunk, axis)
        spread = [n for n in reversed(order) if n != "x"]
        axis = spread[stage - 5]
        fixed = {n: bit[n] for n in spread[stage - 5 :]}
        place = index(owned, chunk, AXES[1:], fixed)
        return remote(four.at[chunk] if stage == 5 else place, place, stage, chunk, axis)

    def load(chunk):
        slot = chunk % 2
        return pltpu.make_async_copy(
            packed.at[:, bit["core"], chunk], own.at[slot], local_sems.at[slot]
        )

    def store(chunk):
        place = owned.at[chunk, bit["y"], bit["near"], bit["far"]]
        return pltpu.make_async_copy(four.at[chunk], place, local_sems.at[2 + chunk])

    def add(target, names, other, prefix=()):
        for at in names:
            there = target[at].astype(f32) + other(at).astype(f32)
            target[at] = there.astype(bf16)

    def grid(count):
        return leads((2,) * count + (1, 1))

    def arrive(stage, kind, chunk):
        copy_of(stage, kind, chunk).wait_recv()
        order = orders[kind]
        if stage == 0:
            load(chunk).wait()
            add(core, [(chunk,) + t for t in grid(4)], lambda at: own[(chunk % 2,) + at[1:]])
        elif stage <= 4:
            before = [n for n in AXES if n not in order[: stage - 1]]
            axis = order[stage - 1]
            where = before.index(axis)

            def mine(at):
                rest = at[1:]
                return buffers[stage - 1][(chunk,) + rest[:where] + (bit[axis],) + rest[where:]]

            add(buffers[stage], [(chunk,) + t for t in grid(4 - stage)], mine)
            if stage == 4:
                store(chunk).start()
        if stage == 5:
            store(chunk).wait()

    ahead, last = 3, 7
    for chunk in range(ahead):
        copy_of(0, chunk % kinds, chunk).start()
    load(0).start()

    def step(s, q):
        @pl.when(s + ahead < spans)
        def _():
            copy_of(0, (q + ahead) % kinds, s + ahead).start()

        @pl.when(s + 1 < spans)
        def _():
            load(s + 1).start()

        for stage in range(last + 1):
            chunk = s - LAGS[stage]
            kind = (q - LAGS[stage]) % kinds

            @pl.when((chunk >= 0) & (chunk < spans))
            def _(stage=stage, chunk=chunk, kind=kind):
                arrive(stage, kind, chunk)
                if stage < last:
                    copy_of(stage + 1, kind, chunk).start()

    def steps(i, carry):
        for q in range(kinds):
            step(i * kinds + q, q)
        return carry

    lax.fori_loop(0, -(-(spans + LAGS[-1]) // kinds), steps, 0)

    def sent(i, carry):
        for q in range(kinds):
            for stage in range(last + 1):
                copy_of(stage, q, i * kinds + q).wait_send()
        return carry

    lax.fori_loop(0, spans // kinds, sent, 0)


def sum_at_owners(packed):
    slots, rows, lanes = packed.shape
    spans = 6 * rows // SPAN
    r = SPAN // 8
    orders = ORDERS
    owned = pl.pallas_call(
        functools.partial(sum_kernel, orders, spans),
        out_shape=jax.ShapeDtypeStruct((spans, 2, 2, 2, r, 128), bf16),
        in_specs=[pl.BlockSpec(memory_space=pl.ANY)],
        out_specs=pl.BlockSpec(memory_space=pl.ANY),
        scratch_shapes=[
            pltpu.VMEM((2, 2, 2, 2, 2, r, 128), bf16),
            pltpu.VMEM((spans, 2, 2, 2, 2, r, 128), bf16),
            pltpu.VMEM((spans, 2, 2, 2, r, 128), bf16),
            pltpu.VMEM((spans, 2, 2, r, 128), bf16),
            pltpu.VMEM((spans, 2, r, 128), bf16),
            pltpu.VMEM((spans, r, 128), bf16),
            pltpu.SemaphoreType.DMA((8, spans)),
            pltpu.SemaphoreType.DMA((8, spans)),
            pltpu.SemaphoreType.DMA((2 + spans,)),
        ],
        compiler_params=pltpu.CompilerParams(
            collective_id=1, has_side_effects=True, vmem_limit_bytes=56 * MIB
        ),
        cost_estimate=pl.CostEstimate(
            flops=slots * rows * 128, bytes_accessed=slots * rows * 128 * 4, transcendentals=0
        ),
        name="sum_at_owners",
    )(packed.reshape(2, 2, spans, 2, 2, 2, r, 128))
    return owned.reshape(6, rows, lanes)


def prepare_kernel(tiles_ref, place_ref, act_ref, pooled_ref):
    sources, tile_h, tile_w, width = tiles_ref.shape
    pixels = tiles_ref[...].astype(f32).reshape(sources * tile_h * tile_w, width).astype(bf16)
    image = jnp.dot(place_ref[...], pixels, preferred_element_type=f32)
    act = (gelu_act(image) * GAMMA).astype(bf16).reshape(4, CELLS, width)
    act_ref[...] = act
    total = act[0].astype(f32) + act[1].astype(f32) + act[2].astype(f32) + act[3].astype(f32)
    pooled_ref[...] = (total * 0.25).astype(bf16)


def prepare(tiles, rows_n, cols_n):
    sources, count, tile_h, tile_w, width = tiles.shape
    pixels = 4 * CELLS
    down = jnp.arange(sources)[:, None, None] // cols_n * tile_h + jnp.arange(tile_h)[None, :, None]
    along = jnp.arange(sources)[:, None, None] % cols_n * tile_w + jnp.arange(tile_w)[None, None, :]
    target = ((down % 2 * 2 + along % 2) * HEIGHT + down // 2) * BREADTH + along // 2
    place = (jnp.arange(pixels)[:, None] == target.reshape(1, pixels)).astype(bf16)
    return pl.pallas_call(
        prepare_kernel,
        grid=(count,),
        out_shape=[
            jax.ShapeDtypeStruct((4, count * CELLS, width), bf16),
            jax.ShapeDtypeStruct((count * CELLS, width), bf16),
        ],
        in_specs=[
            pl.BlockSpec((sources, None, tile_h, tile_w, width), lambda n: (0, n, 0, 0, 0)),
            pl.BlockSpec((pixels, pixels), lambda n: (0, 0)),
        ],
        out_specs=[
            pl.BlockSpec((4, CELLS, width), lambda n: (0, n, 0)),
            pl.BlockSpec((CELLS, width), lambda n: (n, 0)),
        ],
        compiler_params=pltpu.CompilerParams(vmem_limit_bytes=32 * MIB),
        cost_estimate=pl.CostEstimate(
            flops=2 * count * pixels * pixels * width,
            bytes_accessed=5 * count * pixels * width,
            transcendentals=count * pixels * width,
        ),
        name="prepare",
    )(tiles, place)


def moved(image, down, right):
    if right:
        column = lax.broadcasted_iota(jnp.int32, image.shape, 1) + right
        image = pltpu.roll(image, (-right) % BREADTH, 1)
        image = jnp.where((column >= 0) & (column < BREADTH), image, 0.0)
    if down:
        edge = jnp.zeros((abs(down),) + image.shape[1:], image.dtype)
        if down > 0:
            image = jnp.concatenate([image[down:], edge], axis=0)
        else:
            image = jnp.concatenate([edge, image[:down]], axis=0)
    return image


def fill_taps(taps, sign, read, write):
    for phase in sorted({t[0] for t in taps}):
        image = read(phase).astype(f32).reshape(HEIGHT, BREADTH, GROUP)
        for right in sorted({t[2] for t in taps if t[0] == phase}):
            shifted = moved(image, 0, sign * right)
            for tap, (own, down, own_right) in enumerate(taps):
                if own == phase and own_right == right:
                    window = moved(shifted, sign * down, 0)
                    write(tap, window.reshape(CELLS, GROUP).astype(bf16))


def conv_kernel(taps, chunk, act_ref, w_ref, pre_ref, out_ref, cols):
    rows = chunk * CELLS

    def step(i, carry):
        base = pl.multiple_of(i * rows, rows)
        for n in range(chunk):

            def read(phase, n=n):
                return act_ref[phase, pl.ds(base + n * CELLS, CELLS), :]

            def write(tap, window, n=n):
                cols[n * CELLS : (n + 1) * CELLS, tap * GROUP : (tap + 1) * GROUP] = window

            fill_taps(taps, 1, read, write)
        pre = lax.dot_general(
            cols[...], w_ref[...], (((1,), (1,)), ((), ())), preferred_element_type=f32
        )
        pre_ref[pl.ds(base, rows), :] = pre.astype(bf16)
        out_ref[pl.ds(base, rows), :] = (gelu_act(pre) * GAMMA).astype(bf16)
        return carry

    lax.fori_loop(0, pre_ref.shape[0] // rows, step, 0)


def conv_forward(act, weight, taps):
    phases, cells, channels = act.shape
    chunk = min(CHUNK, cells // CELLS)
    return pl.pallas_call(
        functools.partial(conv_kernel, taps, chunk),
        grid=(channels // GROUP,),
        out_shape=[
            jax.ShapeDtypeStruct((cells, channels), bf16),
            jax.ShapeDtypeStruct((cells, channels), bf16),
        ],
        in_specs=[
            pl.BlockSpec((phases, cells, GROUP), lambda g: (0, 0, g)),
            pl.BlockSpec((GROUP, 9 * GROUP), lambda g: (g, 0)),
        ],
        out_specs=[
            pl.BlockSpec((cells, GROUP), lambda g: (0, g)),
            pl.BlockSpec((cells, GROUP), lambda g: (0, g)),
        ],
        scratch_shapes=[pltpu.VMEM((chunk * CELLS, 9 * GROUP), bf16)],
        compiler_params=pltpu.CompilerParams(vmem_limit_bytes=32 * MIB),
        cost_estimate=pl.CostEstimate(
            flops=2 * cells * channels * 9 * GROUP,
            bytes_accessed=cells * channels * (6 + 2 * phases),
            transcendentals=cells * channels,
        ),
        name="conv_forward",
    )(act, weight)


def conv_back_kernel(taps, chunk, up_ref, act_ref, pre_ref, w_ref, down_ref, grad_ref, w_cols, up_cols, act_cols):
    rows = chunk * CELLS
    phases = act_ref.shape[0]
    order = [t for q in range(phases) for t in range(9) if taps[t][0] == q]
    place = {t: i for i, t in enumerate(order)}
    for t in range(9):
        w_cols[place[t] * GROUP : (place[t] + 1) * GROUP, :] = w_ref[:, t * GROUP : (t + 1) * GROUP]

    def step(i, carry):
        base = pl.multiple_of(i * rows, rows)
        for n in range(chunk):

            def read_act(phase, n=n):
                return act_ref[phase, pl.ds(base + n * CELLS, CELLS), :]

            def write_act(tap, window, n=n):
                act_cols[pl.ds(base + n * CELLS, CELLS), tap * GROUP : (tap + 1) * GROUP] = window

            fill_taps(taps, 1, read_act, write_act)
            flat = tuple((0, t[1], t[2]) for t in taps)

            def read_up(phase, n=n):
                return up_ref[pl.ds(base + n * CELLS, CELLS), :]

            def write_up(tap, window, n=n):
                at = place[tap] * GROUP
                up_cols[n * CELLS : (n + 1) * CELLS, at : at + GROUP] = window

            fill_taps(flat, -1, read_up, write_up)
        at = 0
        for phase in range(phases):
            size = sum(t[0] == phase for t in taps) * GROUP
            back = jnp.dot(
                up_cols[:, at : at + size], w_cols[at : at + size, :], preferred_element_type=f32
            )
            at += size
            pre = pre_ref[phase, pl.ds(base, rows), :].astype(f32)
            down_ref[phase, pl.ds(base, rows), :] = (gelu_prime(pre) * GAMMA * back).astype(bf16)
        return carry

    lax.fori_loop(0, up_ref.shape[0] // rows, step, 0)
    grad_ref[...] = lax.dot_general(
        up_ref[...], act_cols[...], (((0,), (0,)), ((), ())), preferred_element_type=f32
    ).astype(grad_ref.dtype)


def conv_backward(up, act, pre, weight, taps):
    phases, cells, channels = act.shape
    chunk = min(CHUNK, cells // CELLS)
    return pl.pallas_call(
        functools.partial(conv_back_kernel, taps, chunk),
        grid=(channels // GROUP,),
        out_shape=[
            jax.ShapeDtypeStruct((phases, cells, channels), bf16),
            jax.ShapeDtypeStruct((channels, 9 * GROUP), bf16),
        ],
        in_specs=[
            pl.BlockSpec((cells, GROUP), lambda g: (0, g)),
            pl.BlockSpec((phases, cells, GROUP), lambda g: (0, 0, g)),
            pl.BlockSpec((phases, cells, GROUP), lambda g: (0, 0, g)),
            pl.BlockSpec((GROUP, 9 * GROUP), lambda g: (g, 0)),
        ],
        out_specs=[
            pl.BlockSpec((phases, cells, GROUP), lambda g: (0, 0, g)),
            pl.BlockSpec((GROUP, 9 * GROUP), lambda g: (g, 0)),
        ],
        scratch_shapes=[
            pltpu.VMEM((9 * GROUP, GROUP), bf16),
            pltpu.VMEM((chunk * CELLS, 9 * GROUP), bf16),
            pltpu.VMEM((cells, 9 * GROUP), bf16),
        ],
        compiler_params=pltpu.CompilerParams(vmem_limit_bytes=48 * MIB),
        cost_estimate=pl.CostEstimate(
            flops=4 * cells * channels * 9 * GROUP,
            bytes_accessed=cells * channels * (2 + 8 * phases),
            transcendentals=cells * channels * phases,
        ),
        name="conv_backward",
    )(up, act, pre, weight)


def new_values(w, g, m, v, standard, clip):
    fan_in = w.shape[1]
    if standard:
        centre = w - jnp.mean(w, axis=-1, keepdims=True)
        spread = jnp.mean(centre * centre, axis=-1, keepdims=True)
        scale = lax.rsqrt(spread * fan_in + STD_EPS)
        along = jnp.sum(g * centre, axis=-1, keepdims=True)
        mean_g = jnp.mean(g, axis=-1, keepdims=True)
        g = scale * (g - mean_g) - (scale * scale * scale * along) * centre
    if clip:
        ceiling = CLIP * jnp.sqrt(jnp.sum(w * w, axis=-1, keepdims=True))
        norm = jnp.sqrt(jnp.sum(g * g, axis=-1, keepdims=True))
        g = g * (ceiling / jnp.maximum(norm, ceiling))
    m = DECAY_ONE * m + (1.0 - DECAY_ONE) * g
    v = DECAY_TWO * v + (1.0 - DECAY_TWO) * g * g
    root = v * lax.rsqrt(v) * (1.0 - DECAY_TWO**STEP_COUNT) ** -0.5 + ADAM_EPS
    step = (RATE / (1.0 - DECAY_ONE**STEP_COUNT)) * m * pl.reciprocal(root)
    return m, v, (1.0 - RATE * WEIGHT_DECAY) * w - step


def update_packed_kernel(shapes, share_ref, packed_ref, *refs):
    count = len(shapes)
    valid = pl.program_id(0) < share_ref[0]
    at = 0
    for k, shape in enumerate(shapes):
        part, width = shape[-2] // 6, shape[-1]
        for lead in leads(shape):
            g, at = read_packed(packed_ref, at, part, width)
            g = jnp.where(valid, g.astype(f32), 0.0)
            w, m, v = (refs[3 * k + i][lead] for i in range(3))
            for i, value in enumerate(new_values(w, g, m, v, True, True)):
                refs[3 * (count + k) + i][lead] = value


def update_packed(packed, members, share):
    specs, operands, shapes = [], [], []
    for weight, first, second in members:
        shape = weight.shape
        block = shape[:-2] + (shape[-2] // 6, shape[-1])
        zeros = (0,) * (len(shape) - 2)
        specs += [pl.BlockSpec(block, lambda j, zeros=zeros: zeros + (j, 0))] * 3
        operands += [weight, first, second]
        shapes.append(shape)
    total = sum(o.size for o in operands)
    outs = pl.pallas_call(
        functools.partial(update_packed_kernel, tuple(shapes)),
        grid=(6,),
        out_shape=[jax.ShapeDtypeStruct(o.shape, f32) for o in operands],
        in_specs=[
            pl.BlockSpec(memory_space=pltpu.SMEM),
            pl.BlockSpec((None,) + packed.shape[1:], lambda j: (j, 0, 0)),
        ]
        + specs,
        out_specs=specs,
        compiler_params=pltpu.CompilerParams(vmem_limit_bytes=58 * MIB),
        cost_estimate=pl.CostEstimate(
            flops=10 * total, bytes_accessed=9 * total, transcendentals=total // 3
        ),
        name="update_packed",
    )(share, packed, *operands)
    return [tuple(outs[3 * k : 3 * k + 3]) for k in range(len(members))]


def update_factors_kernel(unit, turned, block, share_ref, units_ref, inputs_ref, w_ref, m_ref, v_ref, m_out, v_out, w_out, g_all):
    step = pl.program_id(1)

    @pl.when(step == 0)
    def _():
        left, right = (inputs_ref, units_ref) if turned else (units_ref, inputs_ref)
        g_all[...] = lax.dot_general(
            left[...], right[...], (((0,), (0,)), ((), ())), preferred_element_type=f32
        )

    rows = pl.ds(pl.multiple_of(step * block, 8), block)
    shape = w_ref.shape
    index = lax.broadcasted_iota(jnp.int32, shape if turned else (block, 1), 1 if turned else 0)
    index += 0 if turned else step * block
    g = jnp.where(index < share_ref[0] * unit, g_all[rows, :], 0.0)
    m_out[...], v_out[...], w_out[...] = new_values(
        w_ref[...], g, m_ref[...], v_ref[...], False, not turned
    )


def update_factors(weight, units, gathered, columns, first, second, share, turned=False):
    count, rows, width = weight.shape
    images = units.shape[1]
    start, across, stride = columns
    block = 504 if turned else rows
    steps = -(-rows // block)
    spec = pl.BlockSpec((None, block, width), lambda k, i: (k, i, 0))
    owned = (width if turned else rows) // 6
    made = (across, width) if turned else (rows, across)
    return pl.pallas_call(
        functools.partial(update_factors_kernel, owned, turned, block),
        grid=(count, steps),
        out_shape=[jax.ShapeDtypeStruct(weight.shape, f32)] * 3,
        in_specs=[
            pl.BlockSpec(memory_space=pltpu.SMEM),
            pl.BlockSpec((None, images, units.shape[2]), lambda k, i: (k, 0, 0)),
            pl.BlockSpec((images, across), lambda k, i: (0, start + stride * k)),
        ]
        + [spec] * 3,
        out_specs=[spec] * 3,
        scratch_shapes=[pltpu.VMEM(made, f32)],
        compiler_params=pltpu.CompilerParams(vmem_limit_bytes=56 * MIB),
        cost_estimate=pl.CostEstimate(
            flops=count * rows * width * (2 * images + 15),
            bytes_accessed=24 * count * rows * width,
            transcendentals=count * rows * width,
        ),
        name="update_factors",
    )(share, units, gathered, weight, first, second)


def update_kernel(unit, standard, clip, block, share_ref, w_ref, g_ref, m_ref, v_ref, m_out, v_out, w_out):
    row = pl.program_id(0) * block + lax.broadcasted_iota(jnp.int32, (block, 1), 0)
    g = jnp.where(row % (6 * unit) < share_ref[0] * unit, g_ref[...].astype(f32), 0.0)
    m_out[...], v_out[...], w_out[...] = new_values(
        w_ref[...], g, m_ref[...], v_ref[...], standard, clip
    )


def update(weight, gradient, first, second, share, standard, clip):
    shape = weight.shape
    width = shape[-1]
    flat = [a.reshape(-1, width) for a in (weight, gradient, first, second)]
    rows = flat[0].shape[0]
    block = rows
    for size in range(192, 0, -16):
        if rows % size == 0:
            block = size
            break
    spec = pl.BlockSpec((block, width), lambda i: (i, 0))
    outs = pl.pallas_call(
        functools.partial(update_kernel, shape[-2] // 6, standard, clip, block),
        grid=(rows // block,),
        out_shape=[jax.ShapeDtypeStruct((rows, width), f32)] * 3,
        in_specs=[pl.BlockSpec(memory_space=pltpu.SMEM)] + [spec] * 4,
        out_specs=[spec] * 3,
        compiler_params=pltpu.CompilerParams(vmem_limit_bytes=48 * MIB),
        cost_estimate=pl.CostEstimate(
            flops=30 * rows * width, bytes_accessed=28 * rows * width, transcendentals=rows * width
        ),
        name="update",
    )(share, *flat)
    return tuple(o.reshape(shape) for o in outs)


def split_small(values, rows):
    values = jnp.pad(values, (0, -values.shape[0] % (128 * rows))).reshape(rows, -1)
    terms = []
    for _ in range(3):
        term = lax.reduce_precision(values, 8, 7)
        terms.append(term.astype(bf16))
        values = values - term
    return terms


def join_small(terms, rows):
    width = terms.shape[1] // 3
    total = jnp.sum(terms.astype(f32).reshape(-1, rows, 3 * width), axis=0)
    return (total[:, :width] + total[:, width : 2 * width] + total[:, 2 * width :]).reshape(-1)


def dot_t(left, right):
    return lax.dot_general(
        left, right, (((left.ndim - 1,), (1,)), ((), ())), preferred_element_type=f32
    )


def dot_n(left, right):
    return lax.dot_general(
        left, right, (((left.ndim - 1,), (0,)), ((), ())), preferred_element_type=f32
    )


def dot_sum(upstream, inputs):
    up = upstream.reshape(-1, upstream.shape[-1])
    low = inputs.reshape(-1, inputs.shape[-1])
    return lax.dot_general(up, low, (((0,), (0,)), ((), ())), preferred_element_type=f32)


def tail_forward(act_three, out_w, down_w, up_w):
    images = act_three.shape[0] // CELLS
    pre_four = dot_t(act_three, out_w).reshape(images, CELLS, -1)
    kept_four = pre_four.astype(bf16)
    squeezed = (jnp.sum(pre_four, axis=1) / CELLS).astype(bf16)
    pre_down = dot_t(squeezed, down_w)
    act_down = gelu_act(pre_down).astype(bf16)
    gate_sig = jax.nn.sigmoid(dot_t(act_down, up_w))
    return kept_four, squeezed, pre_down, act_down, gate_sig


def tail_backward(grad_hidden, stored, down_w, up_w, gain):
    pre_four, squeezed, pre_down, act_down, gate_sig = stored
    gate = 2.0 * gate_sig
    raw_gate = jnp.sum(grad_hidden * pre_four, axis=1)
    gain_part = ALPHA * jnp.sum(raw_gate * gate)
    grad_gate = raw_gate * (ALPHA * gain)
    grad_up = (grad_gate * 2.0 * gate_sig * (1.0 - gate_sig)).astype(bf16)
    grad_down = (gelu_prime(pre_down) * dot_n(grad_up, up_w)).astype(bf16)
    grad_squeezed = dot_n(grad_down, down_w)
    grad_four = (
        grad_hidden * (ALPHA * gain * gate)[:, None, :] + (grad_squeezed / CELLS)[:, None, :]
    ).astype(bf16)
    factors = [grad_up, act_down, grad_down, squeezed]
    return grad_four.reshape(-1, grad_four.shape[-1]), factors, gain_part


def body(
    images,
    labels,
    class_counts,
    owner_share,
    w_entry,
    first_entry,
    second_entry,
    w_in,
    first_in,
    second_in,
    w_mid,
    first_mid,
    second_mid,
    w_out,
    first_out,
    second_out,
    se_down,
    first_down,
    second_down,
    se_up,
    first_up,
    second_up,
    w_final,
    first_final,
    second_final,
    head,
    first_head,
    second_head,
    small_params,
    first_small,
    second_small,
):
    owner, local, starts, slot_part = owner_tables(owner_share)
    me = lax.axis_index("dp")
    devices = lax.axis_size("dp")
    my_share = lax.dynamic_slice_in_dim(owner_share, me, 1, 0)
    my_start = lax.dynamic_index_in_dim(starts, me, 0, keepdims=False)

    rows_n, cols_n = lax.axis_size("ha"), lax.axis_size("wa")
    spread = rows_n * cols_n
    micro, per_dp, tile_h, tile_w, in_width = images.shape
    count = micro * per_dp // spread
    tiles = images.reshape(spread, count, tile_h, tile_w, in_width)
    tiles = lax.all_to_all(tiles, ("ha", "wa"), 0, 0, tiled=True)
    spot = lax.axis_index("ha") * cols_n + lax.axis_index("wa")
    my_labels = lax.dynamic_slice_in_dim(labels.reshape(-1), spot * count, count, 0)

    def middle(layer):
        return [(w_mid, (layer, 0), True), (w_mid, (layer, 1), True)]

    def rest(layer):
        return [(w_out, (layer,), True), (se_down, (layer,), False), (se_up, (layer,), False)]

    groups = [
        [(w_entry, (), True)],
        middle(0) + rest(0),
        [(w_in, (0,), True)] + middle(1) + rest(1),
        [(w_final, (), True)],
        [(head, (), False)],
    ]
    staged = known_mesh()
    if staged:
        tables = source_tables(owner, local)
        moves = [Gather(groups[0]), Gather(groups[1])]
        moves[0].along_x()
        moves[1].along_x(moves[0].near)
        moves[0].along_y()
        for entries in groups[2:]:
            entries[0] = (after(entries[0][0], moves[0].near),) + entries[0][1:]
            moves.append(Gather(entries))
        moves[1].near = after(moves[1].near, moves[0].far, *[m.own for m in moves[2:]])
        moves[0].cores()
        moves[1].along_y()
        moves[2].along_x(moves[1].near)
    cells = count * CELLS
    if staged:
        act_zero, pooled = prepare(tiles, rows_n, cols_n)
    else:
        pixels = tiles.reshape(
            rows_n, cols_n, count, tile_h // 2, 2, tile_w // 2, 2, in_width
        ).transpose(4, 6, 2, 0, 3, 1, 5, 7).reshape(4, cells, in_width)
        act_zero = (gelu_act(pixels.astype(f32)) * GAMMA).astype(bf16)
        pooled = (jnp.sum(act_zero.astype(f32), axis=0) * 0.25).astype(bf16)

    def hold(value, arrivals, *then):
        if not staged:
            return value
        came = [getattr(moves[k], name) for k, name in arrivals]
        value, *came = lax.optimization_barrier((value, *came))
        for (k, name), buffer in zip(arrivals, came):
            setattr(moves[k], name, buffer)
        for step, k in then:
            if step == "x":
                moves[k].along_x(moves[k - 1].near)
            elif step == "y":
                moves[k].along_y()
            else:
                moves[k].cores()
        return value

    def weights_of(group):
        if staged:
            return moves[group].unpacked(tables)
        return gather_plain(groups[group], owner, local)

    gains = small_params[:LAYERS]
    head_bias = small_params[LAYERS:]
    images_all = micro * per_dp * lax.axis_size("dp")
    class_weight = 1.0 / class_counts.astype(f32)

    kept = []
    weights = []
    hidden = None
    for layer in range(LAYERS):
        if layer:
            scale = GAMMA * (1.0 + layer * ALPHA * ALPHA) ** (-0.5)
            act_zero = (gelu_act(hidden) * scale).astype(bf16).reshape(1, cells, -1)
        taps = TAPS_TWO if layer == 0 else TAPS_ONE
        if layer == 0:
            (entry_low,) = weights_of(0)
            in_low, skip_low = entry_low[:NECK], entry_low[NECK:]
        else:
            in_low, *others = weights_of(2)
        pre_one = dot_t(act_zero, in_low)
        act_one = (gelu_act(pre_one) * GAMMA).astype(bf16)
        if layer == 0:
            act_one = hold(
                act_one, [(1, "far"), (2, "near")], ("cores", 1), ("y", 2), ("x", 3)
            )
            others = weights_of(1)
        mid_a, mid_b, out_low, down_low, up_low = others
        weights.append((in_low, mid_a, mid_b, out_low, down_low, up_low))
        pre_two, act_two = conv_forward(act_one, mid_a, taps)
        pre_three, act_three = conv_forward(act_two[None], mid_b, TAPS_ONE)
        if layer:
            act_three = hold(act_three, [(4, "near")], ("y", 4))
        tail = tail_forward(act_three, out_low, down_low, up_low)
        branch = (ALPHA * gains[layer]) * tail[0] * (2.0 * tail[4])[:, None, :]
        if layer == 0:
            shortcut = dot_t(pooled, skip_low).reshape(branch.shape)
        else:
            shortcut = hidden.reshape(branch.shape)
        before = None if hidden is None else hidden.astype(bf16)
        hidden = (shortcut + branch).reshape(cells, -1)
        if layer == 0:
            hidden = hold(hidden, [(2, "far"), (3, "near")], ("cores", 2), ("y", 3), ("x", 4))
        else:
            hidden = hold(hidden, [(3, "far")], ("cores", 3))
        kept.append((before, act_zero, pre_one.astype(bf16), act_one, pre_two, act_two, pre_three, act_three, tail, pooled))
    (final_low,) = weights_of(3)
    hidden_low = hidden.astype(bf16)
    pre_final = dot_t(hidden_low, final_low).reshape(count, CELLS, -1)
    pooled_final = (jnp.sum(gelu_act(pre_final) * GAMMA, axis=1) / CELLS).astype(bf16)
    pooled_final = hold(pooled_final, [(4, "far")], ("cores", 4))
    (head_low,) = weights_of(4)
    logits = dot_n(pooled_final, head_low) + head_bias
    largest = jnp.max(logits, axis=1, keepdims=True)
    log_total = largest[:, 0] + jnp.log(jnp.sum(jnp.exp(logits - largest), axis=1))
    one_hot = (my_labels[:, None] == jnp.arange(logits.shape[1])[None, :]).astype(f32)
    picked = jnp.sum(one_hot * logits, axis=1)
    image_weight = jnp.sum(one_hot * class_weight[None, :], axis=1)
    loss_part = jnp.sum(image_weight * (log_total - picked))
    softmax_p = jnp.exp(logits - log_total[:, None])
    grad_logits = image_weight[:, None] * (softmax_p - one_hot) / images_all
    bias_part = jnp.sum(grad_logits, axis=0)
    grad_low = grad_logits.astype(bf16)
    grad_pooled = dot_t(grad_low, head_low) * (GAMMA / CELLS)
    grad_final = (gelu_prime(pre_final.astype(bf16).astype(f32)) * grad_pooled[:, None, :]).astype(bf16).reshape(cells, -1)
    final_grad = dot_sum(grad_final, hidden_low).astype(bf16)
    if staged:
        packed = pack_gradients([final_grad], slot_part, devices, 16)
        packed, grad_final = lax.optimization_barrier((packed, grad_final))
        final_part = lax.psum_scatter(
            packed.reshape(devices, -1, 128), "dp", scatter_dimension=0, tiled=False
        )
        final_sum = lax.psum(final_part, ("ha", "wa")).reshape(6, -1, 128)
    grad_hidden = dot_n(grad_final, final_low)

    in_grads = [None] * LAYERS
    mid_grads = [None] * LAYERS
    out_grads = [None] * LAYERS
    all_factors = [pooled_final, grad_low]
    gain_parts = [None] * LAYERS
    for layer in reversed(range(LAYERS)):
        before, act_zero, pre_one, act_one, pre_two, act_two, pre_three, act_three, tail, pooled = kept[layer]
        in_low, mid_a, mid_b, out_low, down_low, up_low = weights[layer]
        taps = TAPS_TWO if layer == 0 else TAPS_ONE
        grad_four, factors, gain_parts[layer] = tail_backward(
            grad_hidden.reshape(count, CELLS, -1), tail, down_low, up_low, gains[layer]
        )
        all_factors = factors + all_factors
        if layer == 0:
            small = jnp.concatenate([loss_part[None], jnp.stack(gain_parts), bias_part])
            all_factors = jnp.concatenate(all_factors + split_small(small, count), axis=1)
            all_factors, grad_four = lax.optimization_barrier((all_factors, grad_four))
            gathered = lax.all_gather(all_factors, EVERY, axis=0, tiled=True)
        out_grads[layer] = dot_sum(grad_four, act_three).astype(bf16)
        grad_three = (gelu_prime(pre_three.astype(f32)) * GAMMA * dot_n(grad_four, out_low)).astype(bf16)
        grad_two, mid_grad_b = conv_backward(grad_three, act_two[None], pre_two[None], mid_b, TAPS_ONE)
        grad_one, mid_grad_a = conv_backward(grad_two[0], act_one, pre_one, mid_a, taps)
        mid_grads[layer] = (mid_grad_a, mid_grad_b)
        in_grad = dot_sum(grad_one, act_zero).astype(bf16)
        if layer == 0:
            skip_grad = dot_sum(grad_hidden.astype(bf16), pooled).astype(bf16)
            in_grads[layer] = jnp.concatenate([in_grad, skip_grad], axis=0)
        else:
            in_grads[layer] = in_grad
            scale = GAMMA * (1.0 + layer * ALPHA * ALPHA) ** (-0.5)
            grad_zero = dot_n(grad_one[0], in_low)
            grad_hidden = grad_hidden + gelu_prime(before.astype(f32)) * scale * grad_zero

    def own_units(span):
        part = span[1] // starts.shape[0] // 4
        return lax.dynamic_slice_in_dim(gathered, span[0] + my_start * part, 6 * part, 1)

    wide, narrow, final_width = tail[0].shape[-1], tail[3].shape[-1], pooled_final.shape[1]
    spans = []
    at = 0
    for width in [wide, narrow, narrow, wide] * LAYERS + [final_width, logits.shape[1]]:
        spans.append((at, width))
        at += width

    small = join_small(gathered[:, at:], count)
    loss_sum = small[0]
    small_grad = small[1 : 1 + small_params.shape[0]]

    flat_mids = [g for pair in mid_grads for g in pair]
    local_grads = in_grads + out_grads + flat_mids
    members = (
        (w_entry, first_entry, second_entry),
        (w_in, first_in, second_in),
        (w_out, first_out, second_out),
        (w_mid, first_mid, second_mid),
        (w_final, first_final, second_final),
    )
    if staged:
        packed = pack_gradients(local_grads, slot_part, devices, SPAN)
        packed = after(packed, final_part)
        new = update_packed(sum_at_owners(packed), members[:-1], my_share)
        new += update_packed(final_sum, members[-1:], my_share)
    else:
        sums = [sum_plain(g, slot_part[0]) for g in local_grads + [final_grad]]
        new = []
        for weight, first, second in members:
            count = len(leads(weight.shape))
            total, sums = jnp.stack(sums[:count]), sums[count:]
            new.append(update(weight, total, first, second, my_share, True, True))
    entry_new, in_new, out_new, mid_new, final_new = new
    def owned(first_span):
        return jnp.stack([own_units(spans[4 * k + first_span]) for k in range(LAYERS)])

    def blocks(first_span):
        (at, across), (then, _) = spans[first_span], spans[4 + first_span]
        return at // across, across, (then - at) // across

    up_new = update_factors(
        se_up, owned(0), gathered, blocks(1), first_up, second_up, my_share
    )
    down_new = update_factors(
        se_down, owned(2), gathered, blocks(3), first_down, second_down, my_share
    )
    head_new = update_factors(
        head.T[None],
        own_units(spans[-2])[None],
        gathered,
        (spans[-1][0] // 1024, 1024, 0),
        first_head.T[None],
        second_head.T[None],
        my_share,
        turned=True,
    )
    head_new = [a[0].T for a in head_new]
    results = [loss_sum]
    for new in (entry_new, in_new, mid_new, out_new, down_new, up_new, final_new, head_new):
        results.extend(new)
    m = DECAY_ONE * first_small + (1.0 - DECAY_ONE) * small_grad
    v = DECAY_TWO * second_small + (1.0 - DECAY_TWO) * small_grad * small_grad
    m_hat = m / (1.0 - DECAY_ONE**STEP_COUNT)
    v_hat = v / (1.0 - DECAY_TWO**STEP_COUNT)
    results.extend(
        [
            m,
            v,
            small_params
            - SMALL_RATE * (m_hat / (jnp.sqrt(v_hat) + ADAM_EPS) + WEIGHT_DECAY * small_params),
        ]
    )
    return tuple(results)


def solution(mesh):
    owned = (
        [P("dp", None)] * 3
        + [P(None, "dp", None)] * 3
        + [P(None, None, "dp", None)] * 3
        + [P(None, "dp", None)] * 9
        + [P("dp", None)] * 6
        + [P()] * 3
    )
    return jax.shard_map(
        body,
        mesh=mesh,
        in_specs=tuple([P(None, "dp", "ha", "wa", None), P(None, "dp"), P(), P()] + owned),
        out_specs=tuple([P()] + owned),
        check_vma=False,
    )
```
